32 devices in a mesh: fsdp: 8 (over y, x, core), seq: 4 (over z).
Axes of the slice: x: 2, y: 2, z: 4, core: 2. Of those that a mesh axis runs over, the one named last changes fastest.
Arguments:
- hidden_in: bfloat16 [8, 1024, 2048], P('fsdp', 'seq'), may hold values from -6 to 6
- norm_attn: bfloat16 [2048], P('fsdp'), may hold values from 0.5 to 1.5
- qkv_weight: bfloat16 [2048, 2560], P('fsdp'), may hold values from -0.1875 to 0.1875
- out_weight: bfloat16 [2048, 2048], P('fsdp'), may hold values from -1 to 1
- norm_ffn: bfloat16 [2048], P('fsdp'), may hold values from 0.29882812 to 3
- gate_up_weight: bfloat16 [2048, 11264], P('fsdp'), may hold values from -0.125 to 0.125
- down_weight: bfloat16 [5632, 2048], P('fsdp'), may hold values from -0.078125 to 0.078125
- cotangent: bfloat16 [8, 1024, 2048], P('fsdp', 'seq'), may hold values from -6 to 6
Outputs:
- out: bfloat16 [8, 1024, 2048], P('fsdp', 'seq')
- grad_input: bfloat16 [8, 1024, 2048], P('fsdp', 'seq')
- grad_norm_attn: float32 [2048], P('fsdp')
- grad_qkv_weight: float32 [2048, 2560], P('fsdp')
- grad_out_weight: float32 [2048, 2048], P('fsdp')
- grad_norm_ffn: float32 [2048], P('fsdp')
- grad_gate_up_weight: float32 [2048, 11264], P('fsdp')
- grad_down_weight: float32 [5632, 2048], P('fsdp')
The draws below stay inside these ranges and needn't reach their ends.
All inputs are finite; a program needn't handle non-finite values.
Results may differ from the reference program's by a relative error of at most 0.017.
The reference program's roundings to bfloat16 on the way count: a program that leaves them out, or rounds other values in their place, can miss the bound.
Values may be sent and summed in bfloat16 or wider, within the bound.
No kernel may reach another device: no remote copies, remote signals or barrier semaphores. Data moves between devices by JAX's collectives and lax.ppermute only.
A program may use at most 512 MiB of HBM per device.

```python
import math
import jax
import jax.numpy as jnp
from jax import lax

D = 2048
HEADS = 32
KVH = 4
HD = 64
FF = 5632
QKV = 2560
SEQS = 8
LEN = 1024
N_SEQ = 4


def block_scale(own_key, extent, shards, least, high):
    factor_of = 1.0
    for axis_at, blocks in shards:
        heights = jax.random.uniform(jax.random.fold_in(jax.random.fold_in(own_key, 6), axis_at), (blocks,), jnp.float32, least / len(shards), high / len(shards))
        factor_of = factor_of * jnp.repeat(jnp.exp(heights), extent[axis_at] // blocks).reshape((-1,) + (1,) * (len(extent) - 1 - axis_at))
    return factor_of


def gaussian(own_key, dims, scale, reach, shards=(), kind=jnp.bfloat16):
    array = jax.random.normal(own_key, dims, jnp.float32) * scale
    if len(shards) > 0:
        array = block_scale(own_key, dims, shards, -0.22, 0.18) * array
    return jnp.clip(array, min=-reach, max=reach).astype(kind)


def setup_inputs(seed: int = 0) -> dict:
    key_list = jax.random.split(jax.random.key(seed), 9)
    hidden_in = gaussian(key_list[0], (SEQS, LEN, D), 1.0, 6.0, ((0, 8), (1, 4)))
    norm_attn = jnp.clip(1.0 + 0.1 * jax.random.normal(key_list[1], (D,), jnp.float32), 0.5, 1.5).astype(jnp.bfloat16)
    qkv_weight = gaussian(key_list[2], (D, QKV), (D // 2) ** -0.5, 0.1875, ((0, 8),))
    out_weight = gaussian(key_list[3], (HEADS * HD, D), (D // 64) ** -0.5, 1.0, ((0, 8),))
    norm_ffn = jnp.clip(jnp.exp(math.log(3.0) - 2.306499 * jax.random.uniform(key_list[4], (D,), jnp.float32) ** block_scale(key_list[4], (D,), ((0, 8),), -0.2, 0.2)), 0.29882812, 3.0).astype(jnp.bfloat16)
    gate_up_weight = gaussian(key_list[5], (D, 2 * FF), D ** -0.5, 0.125, ((0, 8),))
    down_weight = gaussian(key_list[6], (FF, D), FF ** -0.5, 0.078125, ((0, 8),))
    cotangent = gaussian(key_list[7], (SEQS, LEN, D), 1.0, 6.0, ((0, 8), (1, 4)))
    return {"hidden_in": hidden_in, "norm_attn": norm_attn, "qkv_weight": qkv_weight, "out_weight": out_weight, "norm_ffn": norm_ffn, "gate_up_weight": gate_up_weight, "down_weight": down_weight, "cotangent": cotangent}


epsilon = 1e-05
masked_value = -1e+30
highest = lax.Precision.HIGHEST

@jax.custom_vjp
def low(v):
    return lax.optimization_barrier(v.astype(jnp.bfloat16)).astype(jnp.float32)

@jax.custom_vjp
def low_back(v):
    return v

def low_keep(v):
    return (low(v), None)

def low_pass(kept, grad):
    return (grad,)

def back_keep(v):
    return (v, None)

def back_low(kept, grad):
    return (low(grad),)
low.defvjp(low_keep, low_pass)
low_back.defvjp(back_keep, back_low)

def angle_tables(length):
    half_dim = HD // 2
    inverse = 10000.0 ** (-jnp.arange(half_dim, dtype=jnp.float32) * 2.0 / HD)
    angles = jnp.arange(length, dtype=jnp.float32)[:, None] * inverse[None, :]
    return (jnp.cos(angles), jnp.sin(angles))

def rotate(values, cosine, sine):
    half_dim = values.shape[-1] // 2
    first, second = (values[..., :half_dim], values[..., half_dim:])
    cos_wide, sin_wide = (cosine[:, None, :], sine[:, None, :])
    return jnp.concatenate([first * cos_wide - second * sin_wide, second * cos_wide + first * sin_wide], -1)

def rms_norm(values, gain):
    factor = lax.rsqrt(lax.optimization_barrier(jnp.mean(values * values, axis=-1, keepdims=True)) + epsilon)
    return values * factor * gain

def attend(queries, key_slots, value_slots):
    length = queries.shape[0]
    block_rows = min(512, length)
    block_count = length // block_rows
    per_dev = HEADS // N_SEQ
    grouped = queries.reshape(block_count, block_rows, N_SEQ, per_dev, HD)
    starts = jnp.arange(block_count, dtype=jnp.int32) * block_rows
    key_place = jnp.arange(length, dtype=jnp.int32)

    def one_block(block_item):
        query_block, start_row = block_item
        scores = jnp.einsum('qnhd,knd->nhqk', query_block, key_slots, precision=highest) * HD ** (-0.5)
        query_place = start_row + jnp.arange(block_rows, dtype=jnp.int32)
        allowed = key_place[None, :] <= query_place[:, None]
        scores = low_back(jnp.where(allowed, scores, masked_value))
        log_total = jax.nn.logsumexp(scores, axis=-1, keepdims=True)
        attn_probs = low(jnp.exp(scores - log_total))
        return jnp.einsum('nhqk,knd->qnhd', attn_probs, value_slots, precision=highest)
    outputs = lax.map(jax.checkpoint(one_block), (grouped, starts))
    return outputs.reshape(length, HEADS * HD)

def layer(hidden, norm_attn, qkv_weight, out_weight, norm_ffn, gate_up_weight, down_weight, cosine, sine):
    length = hidden.shape[0]
    q_width = HEADS * HD
    kv_width = KVH * HD
    copies = N_SEQ // KVH
    normed = low(rms_norm(hidden, norm_attn))
    joined = low_back(jnp.dot(normed, qkv_weight, precision=highest))
    queries = low_back(low(rotate(joined[:, :q_width].reshape(length, HEADS, HD), cosine, sine)))
    keys = low(rotate(joined[:, q_width:q_width + kv_width].reshape(length, KVH, HD), cosine, sine))
    values = low(joined[:, q_width + kv_width:].reshape(length, KVH, HD))
    key_slots = low_back(jnp.repeat(keys, copies, axis=1))
    value_slots = low_back(jnp.repeat(values, copies, axis=1))
    attended = low_back(low(attend(queries, key_slots, value_slots)))
    middle = hidden + low_back(jnp.dot(attended, out_weight, precision=highest))
    normed_ffn = low(rms_norm(middle, norm_ffn))
    gate_up = low_back(jnp.dot(normed_ffn, gate_up_weight, precision=highest))
    mixed = low(jax.nn.silu(gate_up[:, :FF]) * gate_up[:, FF:])
    return middle + low_back(jnp.dot(mixed, down_weight, precision=highest))

def reference(hidden_in, norm_attn, qkv_weight, out_weight, norm_ffn, gate_up_weight, down_weight, cotangent):
    cosine, sine = angle_tables(LEN)
    params = tuple((matrix.astype(jnp.float32) for matrix in (norm_attn, qkv_weight, out_weight, norm_ffn, gate_up_weight, down_weight)))

    def forward(hidden, *weights):
        return layer(hidden, *weights, cosine, sine)

    def one_sequence(running, seq_item):
        seq_hidden, seq_grad = seq_item
        result, pull_back = jax.vjp(forward, seq_hidden.astype(jnp.float32), *params)
        gradients = pull_back(seq_grad.astype(jnp.float32))
        running = tuple((before + update for before, update in zip(running, gradients[1:])))
        return (running, (result.astype(jnp.bfloat16), gradients[0].astype(jnp.bfloat16)))
    zeros = tuple((jnp.zeros(matrix.shape, jnp.float32) for matrix in params))
    running, (outputs, input_grads) = lax.scan(one_sequence, zeros, (hidden_in, cotangent))
    return (outputs, input_grads, running[0], running[1], running[2], running[3], running[4], running[5])
```

```python
import functools

import jax
import jax.numpy as jnp
from jax import lax
from jax.experimental import pallas as pl
from jax.experimental.pallas import tpu as pltpu
from jax.sharding import PartitionSpec as P

HEADS = 32
KVH = 4
HD = 64
FF = 5632

epsilon = 1e-05
masked_value = -1e30
log2e = 1.4426950408889634
contract_last = (((1,), (1,)), ((), ()))
contract_first = (((0,), (0,)), ((), ()))
bf16 = jnp.bfloat16
f32 = jnp.float32


def send(x, k):
    n = lax.axis_size("fsdp")
    return lax.ppermute(x, "fsdp", [(i, i ^ k) for i in range(n)])


def chip_bits():
    n = lax.axis_size("fsdp")
    return [1 << i for i in range(1, n.bit_length() - 1)]


def piece_order():
    n = lax.axis_size("fsdp")
    return list(range(0, n, 2)) + list(range(1, n, 2))


def gather_pieces(x):
    bits = chip_bits()
    pieces = {0: x}
    rest = bits
    if len(bits) >= 2:
        a, b = bits[:2]
        rest = bits[2:]
        half = x.shape[0] // 2
        pieces[a], pieces[b] = send(x, a), send(x, b)
        lower = send(pieces[b][:half], a)
        upper = send(pieces[a][half:], b)
        pieces[a | b] = jnp.concatenate([lower, upper], 0)
    for b in rest:
        for k in list(pieces):
            pieces[k | b] = send(pieces[k], b)
    for k in list(pieces):
        pieces[k | 1] = send(pieces[k], 1)
    return pieces


def gather_rows(x):
    pieces = gather_pieces(x)
    return jnp.concatenate([pieces[k] for k in piece_order()], 0)


def scatter_sum(whole):
    n = lax.axis_size("fsdp")
    rows = whole.shape[0] // n
    bits = chip_bits()
    even, odd = whole[: n // 2 * rows], whole[n // 2 * rows :]
    got = send(odd, 1)
    total = {
        k: even[i * rows : (i + 1) * rows].astype(f32) + got[i * rows : (i + 1) * rows].astype(f32)
        for i, k in enumerate(piece_order()[: n // 2])
    }
    for b in reversed(bits[2:] if len(bits) >= 2 else bits):
        for k in [k for k in total if not k & b]:
            total[k] = total[k] + send(total.pop(k | b).astype(bf16), b).astype(f32)
    if len(bits) < 2:
        return total[0]
    a, b = bits[:2]
    half = rows // 2
    far = total[a | b].astype(bf16)
    lower, upper = send(far[:half], a), send(far[half:], b)
    to_b = jnp.concatenate([total[b][:half] + lower.astype(f32), total[b][half:]], 0).astype(bf16)
    to_a = jnp.concatenate([total[a][:half], total[a][half:] + upper.astype(f32)], 0).astype(bf16)
    return total[0] + send(to_a, a).astype(f32) + send(to_b, b).astype(f32)


def line_sum(x):
    n = lax.axis_size("seq")
    if n == 1:
        return x
    if n % 2:
        return lax.psum(x.astype(f32), "seq").astype(bf16)
    me = lax.axis_index("seq")
    mid = n // 2
    total = x

    def add(one, two):
        return (one.astype(f32) + two.astype(f32)).astype(bf16)

    for i in range(mid - 1):
        total = add(total, lax.ppermute(total, "seq", [(i, i + 1), (n - 1 - i, n - 2 - i)]))
    total = add(total, lax.ppermute(total, "seq", [(mid - 1, mid), (mid, mid - 1)]))
    for i in range(mid - 1):
        got = lax.ppermute(total, "seq", [(mid - 1 - i, mid - 2 - i), (mid + i, mid + 1 + i)])
        taken = (me == mid - 2 - i) | (me == mid + 1 + i)
        total = jnp.where(taken, got, total)
    return total


def turn_kernel(sign, x_ref, cos_ref, sin_ref, o_ref):
    x = x_ref[...].astype(f32)
    width = x.shape[1]
    lane = lax.broadcasted_iota(jnp.int32, x.shape, 1)
    first = (lane % HD) < HD // 2
    other = jnp.where(
        first, -pltpu.roll(x, width - HD // 2, 1), pltpu.roll(x, HD // 2, 1)
    )
    o_ref[...] = (x * cos_ref[...] + sign * other * sin_ref[...]).astype(o_ref.dtype)


def turn(x, cos_wide, sin_wide, sign):
    rows, width = x.shape
    block = cos_wide.shape[1]
    return pl.pallas_call(
        functools.partial(turn_kernel, float(sign)),
        out_shape=jax.ShapeDtypeStruct((rows, width), bf16),
        grid=(width // block,),
        in_specs=[
            pl.BlockSpec((rows, block), lambda i: (0, i)),
            pl.BlockSpec((rows, block), lambda i: (0, 0)),
            pl.BlockSpec((rows, block), lambda i: (0, 0)),
        ],
        out_specs=pl.BlockSpec((rows, block), lambda i: (0, i)),
    )(x, cos_wide, sin_wide)


def mask_bias(start, length, rows):
    key_place = lax.broadcasted_iota(jnp.int32, (length, rows), 0)
    query_place = start + lax.broadcasted_iota(jnp.int32, (length, rows), 1)
    return jnp.where(key_place <= query_place, 0.0, masked_value).astype(f32)


def attend_kernel(per_kv, start_ref, q_ref, k_ref, v_ref, o_ref, lse_ref):
    length, rows = k_ref.shape[1], q_ref.shape[0]
    scale2 = HD**-0.5 * log2e
    bias = mask_bias(start_ref[0], length, rows)
    keys = k_ref[0]
    values_t = v_ref[0].astype(f32).T.astype(bf16)
    q_t = q_ref[...].astype(f32).T.astype(bf16)
    outs = []
    for h in range(per_kv):
        scores = (
            jnp.dot(keys, q_t[h * HD : (h + 1) * HD], preferred_element_type=f32) + bias
        )
        top = jnp.max(scores, axis=0, keepdims=True)
        weights = jnp.exp2((scores - top) * scale2)
        total = jnp.sum(weights, axis=0, keepdims=True)
        probs = (weights * (1.0 / total)).astype(bf16)
        outs.append(jnp.dot(values_t, probs, preferred_element_type=f32))
        lse_ref[0, h : h + 1, :] = top * scale2 + jnp.log2(total)
    o_ref[...] = jnp.concatenate(outs, 0).T.astype(bf16)


def attend(start, queries, keys, values):
    rows, width = queries.shape
    length = keys.shape[1]
    per_kv = HEADS // KVH
    block = per_kv * HD
    return pl.pallas_call(
        functools.partial(attend_kernel, per_kv),
        out_shape=(
            jax.ShapeDtypeStruct((rows, width), bf16),
            jax.ShapeDtypeStruct((KVH, per_kv, rows), f32),
        ),
        grid=(KVH,),
        in_specs=[
            pl.BlockSpec(memory_space=pltpu.SMEM),
            pl.BlockSpec((rows, block), lambda i: (0, i)),
            pl.BlockSpec((1, length, HD), lambda i: (i, 0, 0)),
            pl.BlockSpec((1, length, HD), lambda i: (i, 0, 0)),
        ],
        out_specs=(
            pl.BlockSpec((rows, block), lambda i: (0, i)),
            pl.BlockSpec((1, per_kv, rows), lambda i: (i, 0, 0)),
        ),
        compiler_params=pltpu.CompilerParams(vmem_limit_bytes=40 << 20),
        cost_estimate=pl.CostEstimate(
            flops=4 * HEADS * rows * length * HD * 4,
            bytes_accessed=4 * rows * width,
            transcendentals=HEADS * rows * length,
        ),
    )(start, queries, keys, values)


def attend_back_kernel(
    per_kv, start_ref, q_ref, k_ref, v_ref, g_ref, lse_ref, dq_ref, dk_ref, dv_ref
):
    length, rows = k_ref.shape[1], q_ref.shape[0]
    scale = HD**-0.5
    scale2 = scale * log2e
    bias = mask_bias(start_ref[0], length, rows)
    keys, values = k_ref[0], v_ref[0]
    keys_t = keys.astype(f32).T.astype(bf16)
    q_t = q_ref[...].astype(f32).T.astype(bf16)
    g_t = g_ref[...].astype(f32).T.astype(bf16)
    dk = jnp.zeros((length, HD), f32)
    dv = jnp.zeros((length, HD), f32)
    outs = []
    for h in range(per_kv):
        q_h, g_h = q_t[h * HD : (h + 1) * HD], g_t[h * HD : (h + 1) * HD]
        scores = jnp.dot(keys, q_h, preferred_element_type=f32) + bias
        weights = jnp.exp2(scores * scale2 - lse_ref[0, h : h + 1, :])
        grad_p = jnp.dot(values, g_h, preferred_element_type=f32)
        delta = jnp.sum(grad_p * weights, axis=0, keepdims=True)
        grad_s = (weights * (grad_p - delta)).astype(bf16)
        outs.append(jnp.dot(keys_t, grad_s, preferred_element_type=f32))
        dk += lax.dot_general(grad_s, q_h, contract_last, preferred_element_type=f32)
        dv += lax.dot_general(
            weights.astype(bf16), g_h, contract_last, preferred_element_type=f32
        )
    dq_ref[...] = (jnp.concatenate(outs, 0) * scale).T.astype(bf16)
    dk_ref[0] = (dk * scale).astype(bf16)
    dv_ref[0] = dv.astype(bf16)


def attend_back(start, queries, keys, values, grads, lse):
    rows, width = queries.shape
    length = keys.shape[1]
    per_kv = HEADS // KVH
    block = per_kv * HD
    wide = pl.BlockSpec((rows, block), lambda i: (0, i))
    narrow = pl.BlockSpec((1, length, HD), lambda i: (i, 0, 0))
    return pl.pallas_call(
        functools.partial(attend_back_kernel, per_kv),
        out_shape=(
            jax.ShapeDtypeStruct((rows, width), bf16),
            jax.ShapeDtypeStruct((KVH, length, HD), bf16),
            jax.ShapeDtypeStruct((KVH, length, HD), bf16),
        ),
        grid=(KVH,),
        in_specs=[
            pl.BlockSpec(memory_space=pltpu.SMEM),
            wide,
            narrow,
            narrow,
            wide,
            pl.BlockSpec((1, per_kv, rows), lambda i: (i, 0, 0)),
        ],
        out_specs=(wide, narrow, narrow),
        compiler_params=pltpu.CompilerParams(vmem_limit_bytes=48 << 20),
        cost_estimate=pl.CostEstimate(
            flops=10 * HEADS * rows * length * HD * 4,
            bytes_accessed=6 * rows * width,
            transcendentals=HEADS * rows * length,
        ),
    )(start, queries, keys, values, grads, lse)


def angle_tables(positions, heads):
    half_dim = HD // 2
    inverse = 10000.0 ** (-jnp.arange(half_dim, dtype=f32) * 2.0 / HD)
    angles = positions.astype(f32)[:, None] * inverse[None, :]
    return tuple(jnp.tile(t, (1, 2 * heads)) for t in (jnp.cos(angles), jnp.sin(angles)))


def norm_factor(values):
    return lax.rsqrt(jnp.mean(values * values, axis=-1, keepdims=True) + epsilon)


def norm_back(incoming, inputs, factor, gain):
    weighted = incoming * gain
    gain_grad = jnp.sum(incoming * (inputs * factor), axis=0)
    input_grad = weighted * factor - inputs * (factor * factor * factor) * jnp.mean(
        weighted * inputs, axis=-1, keepdims=True
    )
    return (gain_grad, input_grad)


def dot(one, two):
    return jnp.dot(one, two, preferred_element_type=f32)


def dot_last(one, two):
    return lax.dot_general(one, two, contract_last, preferred_element_type=f32)


def dot_first(one, two):
    return lax.dot_general(one, two, contract_first, preferred_element_type=f32)


def on_device(
    hidden_in, norm_attn, qkv_weight, out_weight, norm_ffn, gate_up_weight, down_weight, cotangent
):
    n = lax.axis_size("fsdp")
    me = lax.axis_index("fsdp")
    order = piece_order()
    width = hidden_in.shape[2]
    rows = hidden_in.shape[0] * hidden_in.shape[1]
    q_width = HEADS * HD
    kv_width = KVH * HD
    share = FF // n
    block = width // n
    seq_at = lax.axis_index("seq")

    def to_order(x):
        size = x.shape[1] // n
        return jnp.concatenate(
            [lax.dynamic_slice_in_dim(x, (me ^ k) * size, size, 1) for k in order], 1
        )

    def from_order(x):
        size = x.shape[1] // n
        where = {k: i for i, k in enumerate(order)}
        place = jnp.zeros((n,), jnp.int32)
        place = jnp.array([where[k] for k in range(n)], jnp.int32)[me ^ jnp.arange(n)]
        return jnp.concatenate(
            [lax.dynamic_slice_in_dim(x, place[j] * size, size, 1) for j in range(n)], 1
        )

    gains = lax.all_gather(jnp.stack([norm_attn, norm_ffn]), "fsdp", axis=1, tiled=True)
    gain_one, gain_two = gains[0].astype(f32), gains[1].astype(f32)
    full_qkv = gather_rows(qkv_weight)

    inputs = hidden_in.reshape(rows, width).astype(f32)
    factor_one = norm_factor(inputs)
    normed_one = to_order((inputs * factor_one * gain_one).astype(bf16))
    joined = dot(normed_one, full_qkv)
    positions = seq_at * rows + jnp.arange(rows, dtype=jnp.int32)
    cos_wide, sin_wide = angle_tables(positions, KVH)
    turned = turn(joined[:, : q_width + kv_width], cos_wide, sin_wide, 1)
    queries = turned[:, :q_width]
    keys_values = jnp.concatenate(
        [turned[:, q_width:], joined[:, q_width + kv_width :].astype(bf16)], 1
    )
    all_kv = lax.all_gather(keys_values, "seq", axis=0, tiled=True)
    length = all_kv.shape[0]
    all_kv = all_kv.reshape(length, 2, KVH, HD).transpose(1, 2, 0, 3)
    all_keys, all_values = all_kv[0], all_kv[1]
    start = (seq_at * rows).astype(jnp.int32).reshape(1)
    attended, lse = attend(start, queries, all_keys, all_values)

    full_out = gather_rows(out_weight)
    attended_x = to_order(attended)
    middle = inputs + dot(attended_x, full_out)

    by_owner = gate_up_weight.reshape(block, 2, n, share).transpose(2, 0, 1, 3)
    by_owner = by_owner.reshape(n, block, 2 * share)
    mine = jnp.zeros((width, 2 * share), bf16)
    for k in range(n):
        part = lax.dynamic_index_in_dim(by_owner, me ^ k, 0, keepdims=False)
        part = send(part, k) if k else part
        mine = lax.dynamic_update_slice_in_dim(mine, part, (me ^ k) * block, 0)

    factor_two = norm_factor(middle)
    normed_two = (middle * factor_two * gain_two).astype(bf16)
    tokens = gather_rows(normed_two)
    grad_result = cotangent.reshape(rows, width)
    grads = gather_rows(grad_result)

    gate_pre = dot(tokens, mine[:, :share])
    up_proj = dot(tokens, mine[:, share:])
    sigmoid_gate = jax.nn.sigmoid(gate_pre)
    gate_act = gate_pre * sigmoid_gate
    mixed = (gate_act * up_proj).astype(bf16)
    grad_mixed = dot_last(grads, down_weight)
    grad_gate = grad_mixed * up_proj * (sigmoid_gate * (1.0 + gate_pre * (1.0 - sigmoid_gate)))
    grad_gate_up = jnp.concatenate([grad_gate, grad_mixed * gate_act], -1).astype(bf16)

    grad_normed_two = scatter_sum(dot_last(grad_gate_up, mine).astype(bf16))
    result = middle + scatter_sum(dot(mixed, down_weight).astype(bf16))
    out = result.astype(bf16).reshape(hidden_in.shape)

    pieces = 4 if share % 64 == 0 else 2
    grad_down = dot_first(mixed, grads).astype(bf16)
    size = share // pieces
    down_sums = jnp.concatenate(
        [line_sum(grad_down[i * size : (i + 1) * size]) for i in range(pieces)], 0
    ).astype(f32)

    grad_gate_up_w = dot_first(tokens, grad_gate_up).astype(bf16)
    landed = jnp.zeros((n, block, 2 * share), bf16)
    for k in range(n):
        part = lax.dynamic_slice_in_dim(grad_gate_up_w, (me ^ k) * block, block, 0)
        part = line_sum(send(part, k) if k else part)
        landed = lax.dynamic_update_index_in_dim(landed, part, me ^ k, 0)
    gate_up_sums = (
        landed.reshape(n, block, 2, share).transpose(1, 2, 0, 3).reshape(block, 2 * FF).astype(f32)
    )

    grad_gain_two, grad_norm_two = norm_back(grad_normed_two, middle, factor_two, gain_two)
    grad_middle = grad_result.astype(f32) + grad_norm_two
    grad_branch = grad_middle.astype(bf16)
    grad_attended = from_order(dot_last(grad_branch, full_out).astype(bf16))
    out_sums = line_sum(
        scatter_sum(dot_first(attended_x, grad_branch).astype(bf16)).astype(bf16)
    ).astype(f32)

    grad_queries, grad_keys, grad_values = attend_back(
        start, queries, all_keys, all_values, grad_attended, lse
    )
    kv_parts = jnp.stack([grad_keys, grad_values]).transpose(2, 0, 1, 3).reshape(length, 2 * kv_width)
    kv_sums = lax.psum_scatter(kv_parts, "seq", scatter_dimension=0, tiled=True)
    unturned = turn(
        jnp.concatenate([grad_queries, kv_sums[:, :kv_width]], 1), cos_wide, sin_wide, -1
    )
    grad_joined = jnp.concatenate([unturned, kv_sums[:, kv_width:]], 1)
    qkv_sums = line_sum(
        scatter_sum(dot_first(normed_one, grad_joined).astype(bf16)).astype(bf16)
    ).astype(f32)
    grad_normed_one = from_order(dot_last(grad_joined, full_qkv))
    grad_gain_one, grad_norm_one = norm_back(grad_normed_one, inputs, factor_one, gain_one)
    grad_input = (grad_middle + grad_norm_one).astype(bf16).reshape(hidden_in.shape)

    gain_stack = jnp.stack([grad_gain_one, grad_gain_two])
    gain_sums = lax.psum(
        lax.psum_scatter(gain_stack, "fsdp", scatter_dimension=1, tiled=True), "seq"
    )
    return (
        out,
        grad_input,
        gain_sums[0],
        qkv_sums,
        out_sums,
        gain_sums[1],
        gate_up_sums,
        down_sums,
    )


def solution(mesh):
    placed = (
        P("fsdp", "seq", None),
        P("fsdp"),
        P("fsdp", None),
        P("fsdp", None),
        P("fsdp"),
        P("fsdp", None),
        P("fsdp", None),
        P("fsdp", "seq", None),
    )
    return jax.shard_map(
        on_device,
        mesh=mesh,
        in_specs=placed,
        out_specs=(
            P("fsdp", "seq", None),
            P("fsdp", "seq", None),
            P("fsdp"),
            P("fsdp", None),
            P("fsdp", None),
            P("fsdp"),
            P("fsdp", None),
            P("fsdp", None),
        ),
        check_vma=False,
    )
```

```python
import functools

import jax
import jax.numpy as jnp
from jax import lax
from jax.experimental import pallas as pl
from jax.experimental.pallas import tpu as pltpu
from jax.sharding import PartitionSpec as P

HEADS = 32
KVH = 4
HD = 64
FF = 5632

epsilon = 1e-05
masked_value = -1e30
log2e = 1.4426950408889634
contract_last = (((1,), (1,)), ((), ()))
contract_first = (((0,), (0,)), ((), ()))
bf16 = jnp.bfloat16
f32 = jnp.float32


def send(x, k):
    n = lax.axis_size("fsdp")
    return lax.ppermute(x, "fsdp", [(i, i ^ k) for i in range(n)])


def chip_bits():
    n = lax.axis_size("fsdp")
    return [1 << i for i in range(1, n.bit_length() - 1)]


def piece_order():
    n = lax.axis_size("fsdp")
    return list(range(0, n, 2)) + list(range(1, n, 2))


def gather_small(x):
    n, me = lax.axis_size("fsdp"), lax.axis_index("fsdp")
    for k in (1 << i for i in range(n.bit_length() - 1)):
        got = send(x, k)
        x = jnp.where(
            me & k == 0, jnp.concatenate([x, got], 1), jnp.concatenate([got, x], 1)
        )
    return x


def neighbour(x):
    n = lax.axis_size("seq")
    return lax.ppermute(x, "seq", [(i, i ^ 1) for i in range(n)])


def after(x, *others):
    return lax.optimization_barrier((x, *others))[0]


def added(one, two):
    return (one.astype(f32) + two.astype(f32)).astype(bf16)


def line_sum(x):
    n = lax.axis_size("seq")
    if n == 1:
        return x
    if n % 2:
        return lax.psum(x.astype(f32), "seq").astype(bf16)
    me = lax.axis_index("seq")
    mid = n // 2
    total = x
    for i in range(mid - 1):
        total = added(total, lax.ppermute(total, "seq", [(i, i + 1), (n - 1 - i, n - 2 - i)]))
    total = added(total, lax.ppermute(total, "seq", [(mid - 1, mid), (mid, mid - 1)]))
    for i in range(mid - 1):
        got = lax.ppermute(total, "seq", [(mid - 1 - i, mid - 2 - i), (mid + i, mid + 1 + i)])
        taken = (me == mid - 2 - i) | (me == mid + 1 + i)
        total = jnp.where(taken, got, total)
    return total


def line_step(live, new=None, cross=None, out=None):
    if lax.axis_size("seq") != 4:
        if new is not None:
            live["o" + new] = live["t" + new] = line_sum(live["z" + new])
        return
    inward, outward, across = [(0, 1), (3, 2)], [(1, 0), (2, 3)], [(1, 2), (2, 1)]
    x = total = None
    if out is not None:
        total = live["t" + out] = added(live["p" + out], live["x" + out])
    if new is not None:
        x = live["z" + new]
    if x is not None and total is not None and x.shape == total.shape:
        got = lax.ppermute(jnp.where(is_outer(), x, total), "seq", inward + outward)
        live["i" + new] = live["o" + out] = got
    else:
        if x is not None:
            live["i" + new] = lax.ppermute(x, "seq", inward)
        if total is not None:
            live["o" + out] = lax.ppermute(total, "seq", outward)
    if cross is not None:
        part = live["p" + cross] = added(live["z" + cross], live["i" + cross])
        live["x" + cross] = lax.ppermute(part, "seq", across)


def is_outer():
    me, n = lax.axis_index("seq"), lax.axis_size("seq")
    return (me == 0) | (me == n - 1)


def small_sum(x):
    for axis in ("fsdp", "seq"):
        n = lax.axis_size(axis)
        if n & (n - 1):
            x = lax.psum(x, axis)
            continue
        for k in (1 << i for i in range(n.bit_length() - 1)):
            x = x + lax.ppermute(x, axis, [(i, i ^ k) for i in range(n)])
    return x


def copy_kernel(table_ref, x_ref, o_ref):
    o_ref[...] = x_ref[...].astype(o_ref.dtype)


def pick(x, table, size, dtype=None, rows_at=None):
    rows, count = x.shape[0], table.shape[0]
    if size % 128:
        return jnp.concatenate(
            [lax.dynamic_slice_in_dim(x, table[i] * size, size, 1) for i in range(count)], 1
        ).astype(dtype or x.dtype)
    if rows_at is not None:
        rows = rows_at[1]
    row = jnp.zeros((), jnp.int32) if rows_at is None else rows_at[0]
    table = jnp.concatenate([table, row.reshape(1)]).astype(jnp.int32)
    return pl.pallas_call(
        copy_kernel,
        out_shape=jax.ShapeDtypeStruct((rows, count * size), dtype or x.dtype),
        grid_spec=pltpu.PrefetchScalarGridSpec(
            num_scalar_prefetch=1,
            grid=(count,),
            in_specs=[pl.BlockSpec((rows, size), lambda i, table: (table[count], table[i]))],
            out_specs=pl.BlockSpec((rows, size), lambda i, table: (0, i)),
        ),
        cost_estimate=pl.CostEstimate(
            flops=0, transcendentals=0, bytes_accessed=rows * count * size * 4
        ),
    )(table, x)


def blank_kernel(o_ref):
    pass


def blank(shape, dtype):
    return pl.pallas_call(
        blank_kernel,
        out_shape=jax.ShapeDtypeStruct(shape, dtype),
        out_specs=pl.BlockSpec(memory_space=pl.ANY),
    )()


def turn_kernel(sign, x_ref, cos_ref, sin_ref, o_ref):
    x = x_ref[...].astype(f32)
    width = x.shape[1]
    lane = lax.broadcasted_iota(jnp.int32, x.shape, 1)
    first = (lane % HD) < HD // 2
    other = jnp.where(
        first, -pltpu.roll(x, width - HD // 2, 1), pltpu.roll(x, HD // 2, 1)
    )
    o_ref[...] = (x * cos_ref[...] + sign * other * sin_ref[...]).astype(o_ref.dtype)


def turn(x, cos_wide, sin_wide, sign):
    return pl.pallas_call(
        functools.partial(turn_kernel, float(sign)),
        out_shape=jax.ShapeDtypeStruct(x.shape, bf16),
    )(x, cos_wide, sin_wide)


def place_kernel(info_ref, buffer_ref, got_ref, total_ref, o_ref):
    o_ref[...] = jnp.where(info_ref[0] == 1, got_ref[...], total_ref[...]).astype(f32)


def place(buffer, pair, outer, where, size):
    got, total = pair
    rows = got.shape[0]
    if size % 128:
        picked = jnp.where(outer, got, total).astype(f32)
        for i in range(2):
            buffer = lax.dynamic_update_slice_in_dim(
                buffer, picked[:, i * size : (i + 1) * size], where[i] * size, 1
            )
        return buffer
    info = jnp.concatenate([outer.astype(jnp.int32).reshape(1), where.astype(jnp.int32)])
    own = pl.BlockSpec((rows, size), lambda i, info: (0, i))
    return pl.pallas_call(
        place_kernel,
        out_shape=jax.ShapeDtypeStruct(buffer.shape, f32),
        grid_spec=pltpu.PrefetchScalarGridSpec(
            num_scalar_prefetch=1,
            grid=(2,),
            in_specs=[pl.BlockSpec(memory_space=pl.ANY), own, own],
            out_specs=pl.BlockSpec((rows, size), lambda i, info: (0, info[1 + i])),
        ),
        input_output_aliases={1: 0},
    )(info, buffer, got, total)


def mask_bias(start, length, rows):
    key_place = lax.broadcasted_iota(jnp.int32, (length, rows), 0)
    query_place = start + lax.broadcasted_iota(jnp.int32, (length, rows), 1)
    return jnp.where(key_place <= query_place, 0.0, masked_value).astype(f32)


def turned_t(x, cos, sin):
    one, two = x[: HD // 2], x[HD // 2 :]
    return jnp.concatenate([one * cos - two * sin, two * cos + one * sin], 0)


def kv_head(ref, index):
    both = ref[...]
    return jnp.where(index % 2 == 0, both[:, :HD], both[:, HD:])


def attend_kernel(
    heads, per_kv, info_ref, q_ref, k_ref, v_ref, cos_ref, sin_ref, o_ref, lse_ref, bias_ref
):
    length, rows = k_ref.shape[0], q_ref.shape[0]
    scale2 = HD**-0.5 * log2e
    step = pl.program_id(0)

    @pl.when(step == 0)
    def _():
        bias_ref[...] = mask_bias(info_ref[0], length, rows)

    kv = step * heads // per_kv
    keys = kv_head(k_ref, kv)
    values_t = kv_head(v_ref, kv).astype(f32).T.astype(bf16)
    q_t = q_ref[...].T
    cos, sin = cos_ref[...], sin_ref[...]
    outs = []
    for h in range(heads):
        q_h = turned_t(q_t[h * HD : (h + 1) * HD], cos, sin).astype(bf16)
        scores = jnp.dot(keys, q_h, preferred_element_type=f32) + bias_ref[...]
        top = jnp.max(scores, axis=0, keepdims=True)
        weights = jnp.exp2((scores - top) * scale2)
        total = jnp.sum(weights, axis=0, keepdims=True)
        probs = (weights * (1.0 / total)).astype(bf16)
        outs.append(jnp.dot(values_t, probs, preferred_element_type=f32))
        lse_ref[0, h : h + 1, :] = top * scale2 + jnp.log2(total)
    o_ref[...] = jnp.concatenate(outs, 0).T.astype(bf16)


def attend_specs(n, rows, length):
    heads = HEADS // n
    per_kv = HEADS // KVH
    kv_at = lambda i: (i * heads // per_kv) // 2
    return dict(
        plain=pl.BlockSpec((rows, heads * HD), lambda i, info: (0, i)),
        ordered=pl.BlockSpec((rows, heads * HD), lambda i, info: (0, info[1 + i])),
        keys=pl.BlockSpec((length, 2 * HD), lambda i, info: (0, kv_at(i))),
        values=pl.BlockSpec((length, 2 * HD), lambda i, info: (0, KVH // 2 + kv_at(i))),
        table=pl.BlockSpec((HD // 2, rows), lambda i, info: (0, 0)),
        lse=pl.BlockSpec((1, heads, rows), lambda i, info: (i, 0, 0)),
    )


def attend(info, joined, all_kv, cos_t, sin_t):
    n = lax.axis_size("fsdp")
    rows, length = joined.shape[0], all_kv.shape[0]
    heads = HEADS // n
    spec = attend_specs(n, rows, length)
    return pl.pallas_call(
        functools.partial(attend_kernel, heads, HEADS // KVH),
        out_shape=(
            jax.ShapeDtypeStruct((rows, HEADS * HD), bf16),
            jax.ShapeDtypeStruct((n, heads, rows), f32),
        ),
        grid_spec=pltpu.PrefetchScalarGridSpec(
            num_scalar_prefetch=1,
            grid=(n,),
            in_specs=[spec[k] for k in ("plain", "keys", "values", "table", "table")],
            out_specs=(spec["ordered"], spec["lse"]),
            scratch_shapes=[pltpu.VMEM((length, rows), f32)],
        ),
        compiler_params=pltpu.CompilerParams(vmem_limit_bytes=40 << 20),
        cost_estimate=pl.CostEstimate(
            flops=4 * HEADS * rows * length * HD * 4,
            bytes_accessed=6 * rows * HEADS * HD,
            transcendentals=HEADS * rows * length,
        ),
    )(info, joined, all_kv, all_kv, cos_t, sin_t)


def attend_back_kernel(
    heads, per_kv, info_ref, q_ref, k_ref, v_ref, g_ref, cos_ref, sin_ref, lse_ref,
    dq_ref, dkv_ref, bias_ref, dk_ref, dv_ref,
):
    length, rows = k_ref.shape[0], q_ref.shape[0]
    scale = HD**-0.5
    scale2 = scale * log2e
    step = pl.program_id(0)
    steps = per_kv // heads

    @pl.when(step == 0)
    def _():
        bias_ref[...] = mask_bias(info_ref[0], length, rows)

    @pl.when(step % steps == 0)
    def _():
        dk_ref[...] = jnp.zeros_like(dk_ref)
        dv_ref[...] = jnp.zeros_like(dv_ref)

    kv = step * heads // per_kv
    keys, values = kv_head(k_ref, kv), kv_head(v_ref, kv)
    keys_t = keys.astype(f32).T.astype(bf16)
    q_t = q_ref[...].T
    g_t = g_ref[...].astype(f32).T.astype(bf16)
    cos, sin = cos_ref[...], sin_ref[...]
    outs = []
    dk, dv = dk_ref[...], dv_ref[...]
    for h in range(heads):
        q_h = turned_t(q_t[h * HD : (h + 1) * HD], cos, sin).astype(bf16)
        g_h = g_t[h * HD : (h + 1) * HD]
        scores = jnp.dot(keys, q_h, preferred_element_type=f32) + bias_ref[...]
        weights = jnp.exp2(scores * scale2 - lse_ref[0, h : h + 1, :])
        grad_p = jnp.dot(values, g_h, preferred_element_type=f32)
        delta = jnp.sum(grad_p * weights, axis=0, keepdims=True)
        grad_s = (weights * (grad_p - delta)).astype(bf16)
        grad_q = jnp.dot(keys_t, grad_s, preferred_element_type=f32) * scale
        outs.append(turned_t(grad_q.astype(bf16).astype(f32), cos, -sin))
        dk += lax.dot_general(grad_s, q_h, contract_last, preferred_element_type=f32)
        dv += lax.dot_general(
            weights.astype(bf16), g_h, contract_last, preferred_element_type=f32
        )
    dk_ref[...], dv_ref[...] = dk, dv
    dq_ref[...] = jnp.concatenate(outs, 0).T.astype(bf16)

    @pl.when(step % steps == steps - 1)
    def _():
        dkv_ref[0] = jnp.concatenate([dk * scale, dv], 1).astype(bf16)


def attend_back(info, joined, all_kv, cos_t, sin_t, grads, lse):
    n = lax.axis_size("fsdp")
    rows, length = joined.shape[0], all_kv.shape[0]
    heads, per_kv = HEADS // n, HEADS // KVH
    spec = attend_specs(n, rows, length)
    names = ("plain", "keys", "values", "ordered", "table", "table", "lse")
    return pl.pallas_call(
        functools.partial(attend_back_kernel, heads, per_kv),
        out_shape=(
            jax.ShapeDtypeStruct((rows, HEADS * HD), bf16),
            jax.ShapeDtypeStruct((KVH, length, 2 * HD), bf16),
        ),
        grid_spec=pltpu.PrefetchScalarGridSpec(
            num_scalar_prefetch=1,
            grid=(n,),
            in_specs=[spec[k] for k in names],
            out_specs=(
                spec["plain"],
                pl.BlockSpec((1, length, 2 * HD), lambda i, info: (i * heads // per_kv, 0, 0)),
            ),
            scratch_shapes=[
                pltpu.VMEM((length, rows), f32),
                pltpu.VMEM((length, HD), f32),
                pltpu.VMEM((length, HD), f32),
            ],
        ),
        compiler_params=pltpu.CompilerParams(vmem_limit_bytes=48 << 20),
        cost_estimate=pl.CostEstimate(
            flops=10 * HEADS * rows * length * HD * 4,
            bytes_accessed=8 * rows * HEADS * HD,
            transcendentals=HEADS * rows * length,
        ),
    )(info, joined, all_kv, all_kv, grads, cos_t, sin_t, lse)


def column_chunks(total, size=256):
    return [(c, min(size, total - c)) for c in range(0, total, size)]


def ffn_kernel(n, count, info_ref, *refs):
    x_refs, g_refs, refs = refs[:count], refs[count : 2 * count], refs[2 * count :]
    w_own, w_other, d_own, d_other = refs[:4]
    outs, (x, g, w, d, both, mid, sems) = refs[4 : 4 + 4 * count], refs[4 + 4 * count :]
    mixed_refs, both_refs = outs[:count], outs[count : 2 * count]
    back_refs, out_refs = outs[2 * count : 3 * count], outs[3 * count :]
    me, part = info_ref[0], info_ref[1]
    rows, width = x_refs[0].shape
    cols = d.shape[0]
    share = cols // 2
    block = width // n
    half = block // 2
    evens = range(0, n, 2)

    copies = []
    for source, flip in ((w_own, 0), (w_other, 1)):
        for i, k in enumerate(evens):
            owner = (me ^ (k | flip)) * block
            for j in range(2):
                at = owner if k == 0 else owner + (part if j == 0 else 1 - part) * half
                if k == 0:
                    at = at + j * half
                copies.append(
                    pltpu.make_async_copy(
                        source.at[pl.ds(i * block + j * half, half)],
                        w.at[pl.ds(pl.multiple_of(at, half), half)],
                        sems.at[len(copies)],
                    )
                )
    core = me % 2
    for source, at in ((d_own, core), (d_other, 1 - core)):
        copies.append(
            pltpu.make_async_copy(
                source, d.at[pl.ds(pl.multiple_of(at * share, share), share)], sems.at[len(copies)]
            )
        )
    for copy in copies:
        copy.start()
    for i in range(count):
        x[i * rows : (i + 1) * rows] = x_refs[i][...]
        g[i * rows : (i + 1) * rows] = g_refs[i][...]
    for copy in copies:
        copy.wait()

    def columns(at, size):
        gate_w, up_w = w[:, pl.ds(at, size)], w[:, pl.ds(cols + at, size)]
        gate = jnp.dot(x[...], gate_w, preferred_element_type=f32)
        up = jnp.dot(x[...], up_w, preferred_element_type=f32)
        grad = lax.dot_general(
            g[...], d[pl.ds(at, size)], contract_last, preferred_element_type=f32
        )
        sig = 1.0 / (1.0 + jnp.exp(-gate))
        act = gate * sig
        mid[:, pl.ds(at, size)] = (act * up).astype(bf16)
        both[:, pl.ds(at, size)] = (grad * up * (sig * (1.0 + gate * (1.0 - sig)))).astype(bf16)
        both[:, pl.ds(cols + at, size)] = (grad * act).astype(bf16)

    full = cols // 256
    pl.loop(0, full)(lambda c: columns(pl.multiple_of(c * 256, 256), 256))
    if cols % 256:
        columns(full * 256, cols % 256)
    for i in range(count):
        at = slice(i * rows, (i + 1) * rows)
        mixed_refs[i][...] = mid[at].astype(f32).T.astype(bf16)
        both_refs[i][...] = both[at]

    @pl.loop(0, width // 256)
    def _(t):
        at = pl.multiple_of(t * 256, 256)
        back = lax.dot_general(
            both[...], w[pl.ds(at, 256)], contract_last, preferred_element_type=f32
        ).astype(bf16)
        out = jnp.dot(mid[...], d[:, pl.ds(at, 256)], preferred_element_type=f32).astype(bf16)
        for i in range(count):
            back_refs[i][:, pl.ds(at, 256)] = back[i * rows : (i + 1) * rows]
            out_refs[i][:, pl.ds(at, 256)] = out[i * rows : (i + 1) * rows]


def ffn(info, xs, gs, w_own, w_other, d_own, d_other):
    n = lax.axis_size("fsdp")
    count = len(xs)
    rows, width = xs[0].shape
    cols = 2 * d_own.shape[0]
    if cols % 128:
        return ffn_plain(info, xs, gs, w_own, w_other, d_own, d_other)
    shapes = (
        [jax.ShapeDtypeStruct((cols, rows), bf16)] * count
        + [jax.ShapeDtypeStruct((rows, 2 * cols), bf16)] * count
        + [jax.ShapeDtypeStruct((rows, width), bf16)] * (2 * count)
    )
    vmem, hbm = pl.BlockSpec(memory_space=pltpu.VMEM), pl.BlockSpec(memory_space=pl.ANY)
    outs = pl.pallas_call(
        functools.partial(ffn_kernel, n, count),
        out_shape=shapes,
        in_specs=[pl.BlockSpec(memory_space=pltpu.SMEM)] + [vmem] * (2 * count) + [hbm] * 4,
        out_specs=[vmem] * (4 * count),
        scratch_shapes=[
            pltpu.VMEM((count * rows, width), bf16),
            pltpu.VMEM((count * rows, width), bf16),
            pltpu.VMEM((width, 2 * cols), bf16),
            pltpu.VMEM((cols, width), bf16),
            pltpu.VMEM((count * rows, 2 * cols), bf16),
            pltpu.VMEM((count * rows, cols), bf16),
            pltpu.SemaphoreType.DMA((2 * n + 2,)),
        ],
        compiler_params=pltpu.CompilerParams(vmem_limit_bytes=56 << 20),
        cost_estimate=pl.CostEstimate(
            flops=2 * count * rows * width * cols * 6,
            bytes_accessed=6 * width * cols,
            transcendentals=count * rows * cols,
        ),
    )(info, *xs, *gs, w_own, w_other, d_own, d_other)
    return [outs[i * count : (i + 1) * count] for i in range(4)]


def ffn_plain(info, xs, gs, w_own, w_other, d_own, d_other):
    n = lax.axis_size("fsdp")
    me, part = info[0], info[1]
    width, share = xs[0].shape[1], d_own.shape[0]
    block, cols = width // n, 2 * share
    half = block // 2
    w = jnp.zeros((width, 2 * cols), bf16)
    for source, flip in ((w_own, 0), (w_other, 1)):
        for i, k in enumerate(range(0, n, 2)):
            for j in range(2):
                at = j if k == 0 else (part if j == 0 else 1 - part)
                rows = source[i * block + j * half : i * block + (j + 1) * half]
                w = lax.dynamic_update_slice_in_dim(w, rows, (me ^ (k | flip)) * block + at * half, 0)
    d = jnp.where(
        me % 2 == 0, jnp.concatenate([d_own, d_other], 0), jnp.concatenate([d_other, d_own], 0)
    )
    mixed, both, back, out = [], [], [], []
    for x, g in zip(xs, gs, strict=True):
        gate, up = dot(x, w[:, :cols]), dot(x, w[:, cols:])
        sig = jax.nn.sigmoid(gate)
        act = gate * sig
        grad = dot_last(g, d)
        mid = (act * up).astype(bf16)
        two = jnp.concatenate(
            [grad * up * (sig * (1.0 + gate * (1.0 - sig))), grad * act], 1
        ).astype(bf16)
        mixed.append(mid.T)
        both.append(two)
        back.append(dot_last(two, w).astype(bf16))
        out.append(dot(mid, d).astype(bf16))
    return mixed, both, back, out


def down_grad_kernel(count, info_ref, *refs):
    lefts, rights, rest = refs[:count], refs[count : 2 * count], refs[2 * count :]
    total = sum(
        jnp.dot(one[...], two[...], preferred_element_type=f32)
        for one, two in zip(lefts, rights, strict=True)
    )
    if len(rest) == 2:
        total = total.astype(bf16).astype(f32) + rest[0][...].astype(f32)
    rest[-1][...] = total.astype(bf16)


def down_grad(info, at, mixed, gs, got=None):
    count = len(mixed)
    cols, rows = mixed[0].shape
    width = gs[0].shape[1]
    size = min(512, width)
    out = pl.BlockSpec((cols // 2, size), lambda i, info: (0, i))
    return pl.pallas_call(
        functools.partial(down_grad_kernel, count),
        out_shape=jax.ShapeDtypeStruct((cols // 2, width), bf16),
        grid_spec=pltpu.PrefetchScalarGridSpec(
            num_scalar_prefetch=1,
            grid=(width // size,),
            in_specs=[pl.BlockSpec((cols // 2, rows), lambda i, info: (info[at], 0))] * count
            + [pl.BlockSpec((rows, size), lambda i, info: (0, i))] * count
            + ([] if got is None else [out]),
            out_specs=out,
        ),
        compiler_params=pltpu.CompilerParams(vmem_limit_bytes=40 << 20),
        cost_estimate=pl.CostEstimate(
            flops=count * rows * width * cols,
            bytes_accessed=4 * width * cols,
            transcendentals=0,
        ),
    )(info, *mixed, *gs, *([] if got is None else [got]))


def up_grad_kernel(count, chips, info_ref, *refs):
    lefts, rights, rest = refs[:count], refs[count : 2 * count], refs[2 * count :]
    gots, outs = rest[:-chips], rest[-chips:]
    total = sum(
        lax.dot_general(one[...], two[...], contract_first, preferred_element_type=f32)
        for one, two in zip(lefts, rights, strict=True)
    )
    for i in range(chips):

        @pl.when(pl.program_id(1) == i)
        def _(i=i):
            if gots:
                outs[i][...] = (
                    total.astype(bf16).astype(f32) + gots[i][...].astype(f32)
                ).astype(bf16)
            else:
                outs[i][...] = total.astype(bf16)


def up_grad(table, xs, both, gots=()):
    count, chips = len(xs), table.shape[0]
    rows, width = xs[0].shape
    cols = both[0].shape[1] // 2
    block = width // lax.axis_size("fsdp")
    if cols % 128 or block % 128:
        whole = sum(dot_first(one, two) for one, two in zip(xs, both, strict=True))
        outs = [
            lax.dynamic_slice_in_dim(whole, table[i] * block, block, 0).astype(bf16)
            for i in range(chips)
        ]
        return [added(one, two) for one, two in zip(outs, gots)] if gots else outs
    outs = [
        pl.BlockSpec(
            (block, cols), lambda h, b, table, i=i: (0, jnp.where(b >= i, h, jnp.maximum(h - 1, 0)))
        )
        for i in range(chips)
    ]
    return pl.pallas_call(
        functools.partial(up_grad_kernel, count, chips),
        out_shape=[jax.ShapeDtypeStruct((block, 2 * cols), bf16)] * chips,
        grid_spec=pltpu.PrefetchScalarGridSpec(
            num_scalar_prefetch=1,
            grid=(2, chips),
            in_specs=[pl.BlockSpec((rows, block), lambda h, b, table: (0, table[b]))] * count
            + [pl.BlockSpec((rows, cols), lambda h, b, table: (0, h))] * count
            + (outs if gots else []),
            out_specs=outs,
        ),
        compiler_params=pltpu.CompilerParams(vmem_limit_bytes=48 << 20),
        cost_estimate=pl.CostEstimate(
            flops=4 * count * rows * chips * block * cols,
            bytes_accessed=4 * chips * block * cols * 2,
            transcendentals=0,
        ),
    )(table, *xs, *both, *gots)


def angle_tables(positions):
    half_dim = HD // 2
    inverse = 10000.0 ** (-jnp.arange(half_dim, dtype=f32) * 2.0 / HD)
    angles = positions.astype(f32)[:, None] * inverse[None, :]
    return jnp.cos(angles), jnp.sin(angles)


def norm_factor(values):
    return lax.rsqrt(jnp.mean(values * values, axis=-1, keepdims=True) + epsilon)


def norm_back(incoming, inputs, factor, gain):
    weighted = incoming * gain
    gain_grad = jnp.sum(incoming * (inputs * factor), axis=0)
    input_grad = weighted * factor - inputs * (factor * factor * factor) * jnp.mean(
        weighted * inputs, axis=-1, keepdims=True
    )
    return (gain_grad, input_grad)


def dot(one, two):
    return jnp.dot(one, two, preferred_element_type=f32)


def dot_last(one, two):
    return lax.dot_general(one, two, contract_last, preferred_element_type=f32)


def dot_first(one, two):
    return lax.dot_general(one, two, contract_first, preferred_element_type=f32)


def on_device(
    hidden_in, norm_attn, qkv_weight, out_weight, norm_ffn, gate_up_weight, down_weight, cotangent
):
    n = lax.axis_size("fsdp")
    me = lax.axis_index("fsdp")
    chips, chip, core = n // 2, me // 2, me % 2
    order = piece_order()
    evens = order[:chips]
    near, rest = evens[1:3], evens[3:]
    width = hidden_in.shape[2]
    rows = hidden_in.shape[0] * hidden_in.shape[1]
    q_width = HEADS * HD
    kv_width = KVH * HD
    share = FF // n
    chip_share = 2 * share
    block = width // n
    half = block // 2
    seq_at = lax.axis_index("seq")
    rank = {k: i for i, k in enumerate(order)}
    to_table = (me ^ jnp.array(order, jnp.int32)).astype(jnp.int32)
    at_table = jnp.array([rank[k] for k in range(n)], jnp.int32)[
        me ^ jnp.arange(n, dtype=jnp.int32)
    ]
    odd_table, even_table = to_table[chips:], to_table[:chips]
    assisted = lax.axis_size("seq") % 2 == 0
    part_at = seq_at % 2 if assisted else jnp.zeros_like(seq_at)

    live = {}

    def fence(**more):
        live.update(more)
        new = lax.optimization_barrier(live)
        live.clear()
        live.update(new)

    def two_hops(pieces):
        if len(rest) != 1:
            return {k: send(pieces[0], k) for k in rest}
        a, b = near
        size = pieces[0].shape[0] // 2
        lower, upper = send(pieces[b][:size], a), send(pieces[a][size:], b)
        return {rest[0]: (lower, upper)}

    def whole_piece(x):
        return jnp.concatenate(x, 0) if isinstance(x, tuple) else x

    full_qkv = lax.all_gather(qkv_weight, "fsdp", axis=0, tiled=True)
    fence(
        gains=gather_small(jnp.stack([norm_attn, norm_ffn])),
        hidden=hidden_in.reshape(rows, width),
        grad=cotangent.reshape(rows, width),
        gate_up=gate_up_weight,
        down=down_weight,
        out=out_weight,
    )

    def my_columns(k, at):
        cols = chip ^ (k // 2)
        spots = jnp.stack([cols, cols + chips]).astype(jnp.int32)
        if at is None:
            return pick(live["gate_up"], spots, chip_share)
        if chip_share % 128:
            part = pick(live["gate_up"], spots, chip_share)
            return lax.dynamic_slice_in_dim(part, at * half, half, 0)
        return pick(live["gate_up"], spots, chip_share, rows_at=(at, half))

    def fetched(k):
        return send(my_columns(k, part_at), k)

    def other_half(k, first):
        return neighbour(first) if assisted else send(my_columns(k, 1 - part_at), k)

    firsts = {k: fetched(k) for k in near}
    fence(firsts=firsts, own=my_columns(0, None), d_other=send(live["down"], 1))
    firsts = live.pop("firsts")
    seconds = {k: other_half(k, x) for k, x in firsts.items()}
    inputs = live["hidden"].astype(f32)
    factor_one = norm_factor(inputs)
    gains = live["gains"].astype(f32)
    normed_one = (inputs * factor_one * gains[:1]).astype(bf16)
    firsts |= {k: fetched(k) for k in rest}
    fence(
        firsts=firsts,
        seconds=seconds,
        qkv=full_qkv,
        normed_one=normed_one,
        normed_one_x=pick(normed_one, to_table, block),
    )
    del live["gate_up"]

    joined = dot(live["normed_one"], live["qkv"])
    positions = seq_at * rows + jnp.arange(rows, dtype=jnp.int32)
    cosine, sine = angle_tables(positions)
    cos_wide, sin_wide = jnp.tile(cosine, (1, 2 * KVH)), jnp.tile(sine, (1, 2 * KVH))
    cos_t, sin_t = cosine.T, sine.T
    keys_values = jnp.concatenate(
        [
            turn(joined[:, q_width : q_width + kv_width], cos_wide, sin_wide, 1),
            joined[:, q_width + kv_width :].astype(bf16),
        ],
        1,
    )
    all_kv = lax.all_gather(keys_values, "seq", axis=0, tiled=True)
    outs = {0: live.pop("out")}
    outs |= {k: send(outs[0], k) for k in near}
    fence(joined=joined, kv=all_kv, outs=outs)

    firsts, seconds, outs = live.pop("firsts"), live.pop("seconds"), live.pop("outs")
    seconds |= {k: other_half(k, firsts[k]) for k in rest}
    outs |= two_hops(outs)
    grads = {0: live["grad"]}
    grads |= {k: send(grads[0], k) for k in near}
    info = jnp.concatenate([(seq_at * rows).reshape(1), at_table]).astype(jnp.int32)
    attended, lse = attend(info, live["joined"], live["kv"], cos_t, sin_t)
    fence(firsts=firsts, seconds=seconds, outs=outs, grads=grads, attended=attended, lse=lse)

    outs, grads = live.pop("outs"), live.pop("grads")
    out_even = jnp.concatenate([whole_piece(outs[k]) for k in evens], 0)
    out_odd = send(out_even, 1)
    grads |= two_hops(grads)
    middle = dot(live["attended"][:, : q_width // 2], out_even)
    middle = live["hidden"].astype(f32) + (
        middle + dot(live["attended"][:, q_width // 2 :], out_odd)
    )
    factor_two = norm_factor(middle)
    gain_two = live["gains"][1:].astype(f32)
    normed_two = (middle * factor_two * gain_two).astype(bf16)
    w_own = [live.pop("own")]
    firsts, seconds = live.pop("firsts"), live.pop("seconds")
    for k in evens[1:]:
        w_own += [firsts[k], seconds[k]]
    w_own = jnp.concatenate(w_own, 0)
    w_other = send(w_own, 1)
    fence(
        w_own=w_own,
        w_other=w_other,
        out_even=out_even,
        out_odd=out_odd,
        grads=grads,
        middle=middle,
        tokens={0: normed_two},
    )

    ffn_info = jnp.stack([me, part_at, core, 1 - core]).astype(jnp.int32)

    def ffn_of(group):
        names = ("mixed", "both", "back", "parts")
        weights = [live[k] for k in ("w_own", "w_other", "down", "d_other")]
        results = ffn(
            ffn_info,
            [live["tokens"][k] for k in group],
            [whole_piece(live["grads"][k]) for k in group],
            *weights,
        )
        for name, new in zip(names, results, strict=True):
            live[name] = live.get(name, {}) | dict(zip(group, new, strict=True))

    new = {k: send(live["tokens"][0], k) for k in near}
    ffn_of([0])
    live["tokens"] |= new
    fence()
    new = {k: send(live["tokens"][0], k) for k in rest}
    ffn_of(near)
    live["tokens"] |= new
    fence()
    new = {k: send(live["back"][k], k) for k in near}
    if rest:
        ffn_of(rest)
    fence(returned=new)

    live["returned"] |= {k: send(live["back"][k], k) for k in rest}

    def each(name):
        return [whole_piece(live[name][k]) for k in evens]

    theirs = down_grad(ffn_info, 3, each("mixed"), each("grads"))
    gots = up_grad(after(odd_table, theirs), each("tokens"), each("both"))
    got = send(theirs, 1)
    grad_down = down_grad(after(ffn_info, gots[0]), 2, each("mixed"), each("grads"), got)
    fence(gots=list(gots), zd=grad_down[: share // 2], ze=grad_down[share // 2 :])

    line_step(live, new="d")
    gots = [send(x, 1) for x in live.pop("gots")]
    grad_normed_two = live["back"][0].astype(f32)
    for k in evens[1:]:
        grad_normed_two = grad_normed_two + live["returned"][k].astype(f32)
    middle = live["middle"]
    factor_two = norm_factor(middle)
    gain_two = live["gains"][1:].astype(f32)
    grad_gain_two, grad_norm_two = norm_back(grad_normed_two, middle, factor_two, gain_two)
    grad_middle = live["grad"].astype(f32) + grad_norm_two
    grad_branch = grad_middle.astype(bf16)
    grad_attended = jnp.concatenate(
        [dot_last(grad_branch, live[k]).astype(bf16) for k in ("out_even", "out_odd")], 1
    )
    parts = up_grad(even_table, each("tokens"), each("both"), gots)
    for k in ("tokens", "grads", "both", "mixed", "back", "returned", "w_own", "w_other", "d_other"):
        del live[k]
    del live["out_even"], live["out_odd"], live["down"], live["grad"]
    fence(
        ups=dict(zip(evens, parts, strict=True)),
        grad_gain_two=grad_gain_two,
        grad_middle=grad_middle,
        grad_branch=grad_branch,
        grad_attended=grad_attended,
    )

    names = [str(k) for k in evens]

    def crossed(whole):
        return send(whole[whole.shape[0] // 2 :], 1)

    def blocks(whole, got):
        return {
            k: added(whole[i * block : (i + 1) * block], got[i * block : (i + 1) * block])
            for i, k in enumerate(evens)
        }

    def far_sends(parts):
        if len(rest) != 1:
            return [send(parts[k], k) for k in rest]
        far = parts[rest[0]]
        size = far.shape[0] // 2
        return [send(far[:size], near[0]), send(far[size:], near[1])]

    def near_sends(parts, got):
        if len(rest) != 1:
            return [send(parts[k], k) for k in near]
        size = parts[0].shape[0] // 2
        lower, upper = got
        one, two = parts[near[0]], parts[near[1]]
        one = jnp.concatenate([one[:size], added(one[size:], upper)], 0)
        two = jnp.concatenate([added(two[:size], lower), two[size:]], 0)
        return [send(one, near[0]), send(two, near[1])]

    def total_of(parts, *got):
        total = parts[0].astype(f32)
        for x in sum([g for g in got if g[0].shape == parts[0].shape], []):
            total = total + x.astype(f32)
        return total

    line_step(live, new="e", cross="d")
    sent = {k: send(live["ups"][k], k) for k in near}
    grad_queries, kv_parts = attend_back(
        info, live["joined"], live["kv"], cos_t, sin_t, live["grad_attended"], live["lse"]
    )
    fence(sent=sent, grad_queries=grad_queries, kv_parts=kv_parts)
    for k in ("grad_attended", "joined", "kv", "lse"):
        del live[k]

    ups = live.pop("ups")
    live["z0"] = ups[0]
    for k, x in live.pop("sent").items():
        live[f"z{k}"] = x
    line_step(live, new=names[0], cross="e", out="d")
    sent = {k: send(ups[k], k) for k in rest}
    length = live["kv_parts"].shape[1]
    kv_parts = live.pop("kv_parts").reshape(KVH, length, 2, HD).transpose(1, 2, 0, 3)
    kv_sums = lax.psum_scatter(
        kv_parts.reshape(length, 2 * kv_width), "seq", scatter_dimension=0, tiled=True
    )
    grad_out = dot_first(live.pop("attended"), live.pop("grad_branch")).astype(bf16)
    fence(sent=sent, kv_sums=kv_sums, grad_out=grad_out, got_out=crossed(grad_out))

    for k, x in live.pop("sent").items():
        live[f"z{k}"] = x
    line_step(live, new=names[1], cross=names[0], out="e")
    parts_out = blocks(live.pop("grad_out"), live.pop("got_out"))
    kv_sums = live.pop("kv_sums")
    grad_joined = jnp.concatenate(
        [
            live.pop("grad_queries"),
            turn(kv_sums[:, :kv_width], cos_wide, sin_wide, -1),
            kv_sums[:, kv_width:],
        ],
        1,
    )
    grad_qkv = dot_first(live.pop("normed_one_x"), grad_joined).astype(bf16)
    fence(
        parts_out=parts_out,
        far_out=far_sends(parts_out),
        grad_joined=grad_joined,
        grad_qkv=grad_qkv,
        got_qkv=crossed(grad_qkv),
    )

    gate_up_sums = blank((block, 2 * FF), f32)
    outer = is_outer()

    def summed(k):
        return jnp.where(outer, live.pop("o" + k), live.pop("t" + k)).astype(f32)

    def placed_in(buffer, k):
        cols = chip ^ (k // 2)
        spots = jnp.stack([cols, cols + chips])
        return place(buffer, (live.pop(f"o{k}"), live.pop(f"t{k}")), outer, spots, chip_share)

    line_step(live, new=names[2] if chips > 2 else None, cross=names[1], out=names[0])
    parts_qkv = blocks(live.pop("grad_qkv"), live.pop("got_qkv"))
    fence(
        near_out=near_sends(live["parts_out"], live["far_out"]),
        parts_qkv=parts_qkv,
        down_sums=jnp.concatenate([summed("d"), summed("e")], 0),
    )

    line_step(live, new=names[3] if chips > 3 else None, cross=names[2], out=names[1])
    for k in evens[4:]:
        line_step(live, new=str(k))
    gate_up_sums = placed_in(gate_up_sums, 0)
    zout = total_of(live.pop("parts_out"), live.pop("far_out"), live.pop("near_out"))
    inputs = live["hidden"].astype(f32)
    factor_one = norm_factor(inputs)
    grad_normed_one = dot_last(live.pop("grad_joined"), live.pop("qkv"))
    grad_gain_one, grad_norm_one = norm_back(
        grad_normed_one, inputs, factor_one, live["gains"][:1].astype(f32)
    )
    grad_input = (live["grad_middle"] + grad_norm_one).astype(bf16)
    fence(
        far_qkv=far_sends(live["parts_qkv"]),
        zout=zout.astype(bf16),
        grad_input=grad_input,
        grad_gains=jnp.stack([grad_gain_one, live.pop("grad_gain_two")]),
        sums=gate_up_sums,
    )

    line_step(live, new="out", cross=names[3], out=names[2])
    gate_up_sums = placed_in(live.pop("sums"), evens[1])
    fence(near_qkv=near_sends(live["parts_qkv"], live["far_qkv"]), sums=gate_up_sums)

    total = total_of(live.pop("parts_qkv"), live.pop("far_qkv"), live.pop("near_qkv")).astype(bf16)
    live["zq"], live["zr"] = total[:half], total[half:]
    line_step(live, new="q", cross="out", out=names[3])
    gate_up_sums = placed_in(live.pop("sums"), evens[2])
    fence(far=far_sends(live["parts"]), sums=gate_up_sums)

    line_step(live, new="r", cross="q", out="out")
    gate_up_sums = live.pop("sums")
    for k in evens[3:]:
        gate_up_sums = placed_in(gate_up_sums, k)
    fence(near=near_sends(live["parts"], live["far"]), sums=gate_up_sums)

    line_step(live, cross="r", out="q")
    out_sums = summed("out")
    grad_gains = small_sum(live.pop("grad_gains"))
    out = total_of(live.pop("parts"), live.pop("far"), live.pop("near"))
    out = (live["middle"] + out).astype(bf16)
    fence(grad_gains=grad_gains, out_final=out, out_sums=out_sums)

    line_step(live, out="r")
    qkv_sums = jnp.concatenate([summed("q"), summed("r")], 0)
    grad_gains = lax.dynamic_slice_in_dim(live["grad_gains"], me * block, block, 1)
    return (
        live["out_final"].reshape(hidden_in.shape),
        live["grad_input"].reshape(hidden_in.shape),
        grad_gains[0],
        qkv_sums,
        live["out_sums"],
        grad_gains[1],
        live["sums"],
        live["down_sums"],
    )


def solution(mesh):
    placed = (
        P("fsdp", "seq", None),
        P("fsdp"),
        P("fsdp", None),
        P("fsdp", None),
        P("fsdp"),
        P("fsdp", None),
        P("fsdp", None),
        P("fsdp", "seq", None),
    )
    return jax.shard_map(
        on_device,
        mesh=mesh,
        in_specs=placed,
        out_specs=(
            P("fsdp", "seq", None),
            P("fsdp", "seq", None),
            P("fsdp"),
            P("fsdp", None),
            P("fsdp", None),
            P("fsdp"),
            P("fsdp", None),
            P("fsdp", None),
        ),
        check_vma=False,
    )
```

```python
import functools

import jax
import jax.numpy as jnp
from jax import lax
from jax.experimental import pallas as pl
from jax.experimental.pallas import tpu as pltpu
from jax.sharding import PartitionSpec as P

HEADS = 32
KVH = 4
HD = 64
FF = 5632

epsilon = 1e-05
masked_value = -1e30
log2e = 1.4426950408889634
contract_last = (((1,), (1,)), ((), ()))
contract_first = (((0,), (0,)), ((), ()))
bf16 = jnp.bfloat16
f32 = jnp.float32


def send(x, k):
    n = lax.axis_size("fsdp")
    return lax.ppermute(x, "fsdp", [(i, i ^ k) for i in range(n)])


def chip_bits():
    n = lax.axis_size("fsdp")
    return [1 << i for i in range(1, n.bit_length() - 1)]


def piece_order():
    n = lax.axis_size("fsdp")
    return list(range(0, n, 2)) + list(range(1, n, 2))


def gather_small(x):
    n, me = lax.axis_size("fsdp"), lax.axis_index("fsdp")
    for k in (1 << i for i in range(n.bit_length() - 1)):
        got = send(x, k)
        x = jnp.where(
            me & k == 0, jnp.concatenate([x, got], 1), jnp.concatenate([got, x], 1)
        )
    return x


def neighbour(x):
    n = lax.axis_size("seq")
    return lax.ppermute(x, "seq", [(i, i ^ 1) for i in range(n)])


def after(x, *others):
    return lax.optimization_barrier((x, *others))[0]


def added(one, two):
    return (one.astype(f32) + two.astype(f32)).astype(bf16)


def line_sum(x):
    n = lax.axis_size("seq")
    if n == 1:
        return x
    if n % 2:
        return lax.psum(x.astype(f32), "seq").astype(bf16)
    me = lax.axis_index("seq")
    mid = n // 2
    total = x
    for i in range(mid - 1):
        total = added(total, lax.ppermute(total, "seq", [(i, i + 1), (n - 1 - i, n - 2 - i)]))
    total = added(total, lax.ppermute(total, "seq", [(mid - 1, mid), (mid, mid - 1)]))
    for i in range(mid - 1):
        got = lax.ppermute(total, "seq", [(mid - 1 - i, mid - 2 - i), (mid + i, mid + 1 + i)])
        taken = (me == mid - 2 - i) | (me == mid + 1 + i)
        total = jnp.where(taken, got, total)
    return total


def line_step(live, new=None, cross=None, out=None):
    if lax.axis_size("seq") != 4:
        if new is not None:
            live["o" + new] = live["t" + new] = line_sum(live["z" + new])
        return
    inward, outward, across = [(0, 1), (3, 2)], [(1, 0), (2, 3)], [(1, 2), (2, 1)]
    x = None if new is None else live["z" + new]
    part = None
    if cross is not None:
        part = live["p" + cross] = added(live["z" + cross], live["i" + cross])
        live["x" + cross] = lax.ppermute(part, "seq", across)
        if x is not None:
            x = after(x, part)
    if x is not None:
        live["i" + new] = lax.ppermute(x, "seq", inward)
    if out is not None:
        old = live["p" + out]
        if part is not None:
            old = after(old, part)
        total = live["t" + out] = added(old, live["x" + out])
        live["o" + out] = lax.ppermute(total, "seq", outward)


def is_outer():
    me, n = lax.axis_index("seq"), lax.axis_size("seq")
    return (me == 0) | (me == n - 1)


def small_sum(x, axis):
    n = lax.axis_size(axis)
    if n & (n - 1):
        return lax.psum(x, axis)
    for k in (1 << i for i in range(n.bit_length() - 1)):
        x = x + lax.ppermute(x, axis, [(i, i ^ k) for i in range(n)])
    return x


def copy_kernel(table_ref, x_ref, o_ref):
    o_ref[...] = x_ref[...].astype(o_ref.dtype)


def pick(x, table, size, dtype=None, rows_at=None):
    rows, count = x.shape[0], table.shape[0]
    if size % 128:
        return jnp.concatenate(
            [lax.dynamic_slice_in_dim(x, table[i] * size, size, 1) for i in range(count)], 1
        ).astype(dtype or x.dtype)
    if rows_at is not None:
        rows = rows_at[1]
    row = jnp.zeros((), jnp.int32) if rows_at is None else rows_at[0]
    table = jnp.concatenate([table, row.reshape(1)]).astype(jnp.int32)
    return pl.pallas_call(
        copy_kernel,
        out_shape=jax.ShapeDtypeStruct((rows, count * size), dtype or x.dtype),
        grid_spec=pltpu.PrefetchScalarGridSpec(
            num_scalar_prefetch=1,
            grid=(count,),
            in_specs=[pl.BlockSpec((rows, size), lambda i, table: (table[count], table[i]))],
            out_specs=pl.BlockSpec((rows, size), lambda i, table: (0, i)),
        ),
        cost_estimate=pl.CostEstimate(
            flops=0, transcendentals=0, bytes_accessed=rows * count * size * 4
        ),
    )(table, x)


def blank_kernel(o_ref):
    pass


def blank(shape, dtype):
    return pl.pallas_call(
        blank_kernel,
        out_shape=jax.ShapeDtypeStruct(shape, dtype),
        out_specs=pl.BlockSpec(memory_space=pl.ANY),
    )()


def turn_kernel(sign, x_ref, cos_ref, sin_ref, o_ref):
    x = x_ref[...].astype(f32)
    width = x.shape[1]
    lane = lax.broadcasted_iota(jnp.int32, x.shape, 1)
    first = (lane % HD) < HD // 2
    other = jnp.where(
        first, -pltpu.roll(x, width - HD // 2, 1), pltpu.roll(x, HD // 2, 1)
    )
    o_ref[...] = (x * cos_ref[...] + sign * other * sin_ref[...]).astype(o_ref.dtype)


def turn(x, cos_wide, sin_wide, sign):
    return pl.pallas_call(
        functools.partial(turn_kernel, float(sign)),
        out_shape=jax.ShapeDtypeStruct(x.shape, bf16),
    )(x, cos_wide, sin_wide)


def place_kernel(info_ref, buffer_ref, got_ref, total_ref, o_ref):
    o_ref[...] = jnp.where(info_ref[0] == 1, got_ref[...], total_ref[...]).astype(f32)


def place(buffer, pair, outer, where, size):
    got, total = pair
    rows = got.shape[0]
    if size % 128:
        picked = jnp.where(outer, got, total).astype(f32)
        for i in range(2):
            buffer = lax.dynamic_update_slice_in_dim(
                buffer, picked[:, i * size : (i + 1) * size], where[i] * size, 1
            )
        return buffer
    info = jnp.concatenate([outer.astype(jnp.int32).reshape(1), where.astype(jnp.int32)])
    own = pl.BlockSpec((rows, size), lambda i, info: (0, i))
    return pl.pallas_call(
        place_kernel,
        out_shape=jax.ShapeDtypeStruct(buffer.shape, f32),
        grid_spec=pltpu.PrefetchScalarGridSpec(
            num_scalar_prefetch=1,
            grid=(2,),
            in_specs=[pl.BlockSpec(memory_space=pl.ANY), own, own],
            out_specs=pl.BlockSpec((rows, size), lambda i, info: (0, info[1 + i])),
        ),
        input_output_aliases={1: 0},
    )(info, buffer, got, total)


def mask_bias(start, length, rows):
    key_place = lax.broadcasted_iota(jnp.int32, (length, rows), 0)
    query_place = start + lax.broadcasted_iota(jnp.int32, (length, rows), 1)
    return jnp.where(key_place <= query_place, 0.0, masked_value).astype(f32)


def turned_t(x, cos, sin):
    one, two = x[: HD // 2], x[HD // 2 :]
    return jnp.concatenate([one * cos - two * sin, two * cos + one * sin], 0)


def kv_head(ref, index):
    both = ref[...]
    return jnp.where(index % 2 == 0, both[:, :HD], both[:, HD:])


def attend_kernel(
    heads, per_kv, info_ref, q_ref, k_ref, v_ref, cos_ref, sin_ref, o_ref, lse_ref, bias_ref
):
    length, rows = k_ref.shape[0], q_ref.shape[0]
    scale2 = HD**-0.5 * log2e
    step = pl.program_id(0)

    @pl.when(step == 0)
    def _():
        bias_ref[...] = mask_bias(info_ref[0], length, rows)

    kv = step * heads // per_kv
    keys = kv_head(k_ref, kv)
    values_t = kv_head(v_ref, kv).astype(f32).T.astype(bf16)
    q_t = q_ref[...].T
    cos, sin = cos_ref[...], sin_ref[...]
    outs = []
    for h in range(heads):
        q_h = turned_t(q_t[h * HD : (h + 1) * HD], cos, sin).astype(bf16)
        scores = jnp.dot(keys, q_h, preferred_element_type=f32) + bias_ref[...]
        top = jnp.max(scores, axis=0, keepdims=True)
        weights = jnp.exp2((scores - top) * scale2)
        total = jnp.sum(weights, axis=0, keepdims=True)
        probs = (weights * (1.0 / total)).astype(bf16)
        outs.append(jnp.dot(values_t, probs, preferred_element_type=f32))
        lse_ref[0, h : h + 1, :] = top * scale2 + jnp.log2(total)
    o_ref[...] = jnp.concatenate(outs, 0).T.astype(bf16)


def attend_specs(n, rows, length):
    heads = HEADS // n
    per_kv = HEADS // KVH
    kv_at = lambda i: (i * heads // per_kv) // 2
    return dict(
        plain=pl.BlockSpec((rows, heads * HD), lambda i, info: (0, i)),
        ordered=pl.BlockSpec((rows, heads * HD), lambda i, info: (0, info[1 + i])),
        keys=pl.BlockSpec((length, 2 * HD), lambda i, info: (0, kv_at(i))),
        values=pl.BlockSpec((length, 2 * HD), lambda i, info: (0, KVH // 2 + kv_at(i))),
        table=pl.BlockSpec((HD // 2, rows), lambda i, info: (0, 0)),
        lse=pl.BlockSpec((1, heads, rows), lambda i, info: (i, 0, 0)),
    )


def attend(info, joined, all_kv, cos_t, sin_t):
    n = lax.axis_size("fsdp")
    rows, length = joined.shape[0], all_kv.shape[0]
    heads = HEADS // n
    spec = attend_specs(n, rows, length)
    return pl.pallas_call(
        functools.partial(attend_kernel, heads, HEADS // KVH),
        out_shape=(
            jax.ShapeDtypeStruct((rows, HEADS * HD), bf16),
            jax.ShapeDtypeStruct((n, heads, rows), f32),
        ),
        grid_spec=pltpu.PrefetchScalarGridSpec(
            num_scalar_prefetch=1,
            grid=(n,),
            in_specs=[spec[k] for k in ("plain", "keys", "values", "table", "table")],
            out_specs=(spec["ordered"], spec["lse"]),
            scratch_shapes=[pltpu.VMEM((length, rows), f32)],
        ),
        compiler_params=pltpu.CompilerParams(vmem_limit_bytes=40 << 20),
        cost_estimate=pl.CostEstimate(
            flops=4 * HEADS * rows * length * HD * 4,
            bytes_accessed=6 * rows * HEADS * HD,
            transcendentals=HEADS * rows * length,
        ),
    )(info, joined, all_kv, all_kv, cos_t, sin_t)


def attend_back_kernel(
    heads, per_kv, info_ref, q_ref, k_ref, v_ref, g_ref, cos_ref, sin_ref, lse_ref,
    dq_ref, dkv_ref, bias_ref, dk_ref, dv_ref,
):
    length, rows = k_ref.shape[0], q_ref.shape[0]
    scale = HD**-0.5
    scale2 = scale * log2e
    step = pl.program_id(0)
    steps = per_kv // heads

    @pl.when(step == 0)
    def _():
        bias_ref[...] = mask_bias(info_ref[0], length, rows)

    @pl.when(step % steps == 0)
    def _():
        dk_ref[...] = jnp.zeros_like(dk_ref)
        dv_ref[...] = jnp.zeros_like(dv_ref)

    kv = step * heads // per_kv
    keys, values = kv_head(k_ref, kv), kv_head(v_ref, kv)
    keys_t = keys.astype(f32).T.astype(bf16)
    q_t = q_ref[...].T
    g_t = g_ref[...].astype(f32).T.astype(bf16)
    cos, sin = cos_ref[...], sin_ref[...]
    outs = []
    dk, dv = dk_ref[...], dv_ref[...]
    for h in range(heads):
        q_h = turned_t(q_t[h * HD : (h + 1) * HD], cos, sin).astype(bf16)
        g_h = g_t[h * HD : (h + 1) * HD]
        scores = jnp.dot(keys, q_h, preferred_element_type=f32) + bias_ref[...]
        weights = jnp.exp2(scores * scale2 - lse_ref[0, h : h + 1, :])
        grad_p = jnp.dot(values, g_h, preferred_element_type=f32)
        delta = jnp.sum(grad_p * weights, axis=0, keepdims=True)
        grad_s = (weights * (grad_p - delta)).astype(bf16)
        grad_q = jnp.dot(keys_t, grad_s, preferred_element_type=f32) * scale
        outs.append(turned_t(grad_q.astype(bf16).astype(f32), cos, -sin))
        dk += lax.dot_general(grad_s, q_h, contract_last, preferred_element_type=f32)
        dv += lax.dot_general(
            weights.astype(bf16), g_h, contract_last, preferred_element_type=f32
        )
    dk_ref[...], dv_ref[...] = dk, dv
    dq_ref[...] = jnp.concatenate(outs, 0).T.astype(bf16)

    @pl.when(step % steps == steps - 1)
    def _():
        dkv_ref[...] = jnp.concatenate([dk * scale, dv], 1).astype(bf16)


def attend_back(info, joined, all_kv, cos_t, sin_t, grads, lse):
    n = lax.axis_size("fsdp")
    rows, length = joined.shape[0], all_kv.shape[0]
    heads, per_kv = HEADS // n, HEADS // KVH
    spec = attend_specs(n, rows, length)
    names = ("plain", "keys", "values", "ordered", "table", "table", "lse")
    return pl.pallas_call(
        functools.partial(attend_back_kernel, heads, per_kv),
        out_shape=(
            jax.ShapeDtypeStruct((rows, HEADS * HD), bf16),
            jax.ShapeDtypeStruct((length, 2 * KVH * HD), bf16),
        ),
        grid_spec=pltpu.PrefetchScalarGridSpec(
            num_scalar_prefetch=1,
            grid=(n,),
            in_specs=[spec[k] for k in names],
            out_specs=(
                spec["plain"],
                pl.BlockSpec((length, 2 * HD), lambda i, info: (0, i * heads // per_kv)),
            ),
            scratch_shapes=[
                pltpu.VMEM((length, rows), f32),
                pltpu.VMEM((length, HD), f32),
                pltpu.VMEM((length, HD), f32),
            ],
        ),
        compiler_params=pltpu.CompilerParams(vmem_limit_bytes=48 << 20),
        cost_estimate=pl.CostEstimate(
            flops=10 * HEADS * rows * length * HD * 4,
            bytes_accessed=8 * rows * HEADS * HD,
            transcendentals=HEADS * rows * length,
        ),
    )(info, joined, all_kv, all_kv, grads, cos_t, sin_t, lse)


def column_chunks(total, size=256):
    return [(c, min(size, total - c)) for c in range(0, total, size)]


def part_pieces(n):
    evens = list(range(0, n, 2))
    return evens[:3], evens[3:], [k | 1 for k in evens[:3]], [k | 1 for k in evens[3:]]


def ffn_kernel(n, count, info_ref, *refs):
    x_refs, g_refs, refs = refs[:count], refs[count : 2 * count], refs[2 * count :]
    parts, (d_own, d_other), refs = refs[:4], refs[4:6], refs[6:]
    outs, (x, g, w, d, both, mid, sems) = refs[: 4 * count], refs[4 * count :]
    mixed_refs, both_refs = outs[:count], outs[count : 2 * count]
    back_refs, out_refs = outs[2 * count : 3 * count], outs[3 * count :]
    me, part = info_ref[0], info_ref[1]
    rows, width = x_refs[0].shape
    cols = d.shape[0]
    share = cols // 2
    block = width // n
    half = block // 2

    copies = []
    for source, ks in zip(parts, part_pieces(n), strict=True):
        for i, k in enumerate(ks):
            owner = (me ^ k) * block
            for j in range(2):
                at = owner if k < 2 else owner + (part if j == 0 else 1 - part) * half
                if k < 2:
                    at = at + j * half
                copies.append(
                    pltpu.make_async_copy(
                        source.at[pl.ds(i * block + j * half, half)],
                        w.at[pl.ds(pl.multiple_of(at, half), half)],
                        sems.at[len(copies)],
                    )
                )
    core = me % 2
    for source, at in ((d_own, core), (d_other, 1 - core)):
        copies.append(
            pltpu.make_async_copy(
                source, d.at[pl.ds(pl.multiple_of(at * share, share), share)], sems.at[len(copies)]
            )
        )
    for copy in copies:
        copy.start()
    for i in range(count):
        x[i * rows : (i + 1) * rows] = x_refs[i][...]
        g[i * rows : (i + 1) * rows] = g_refs[i][...]
    for copy in copies:
        copy.wait()

    def columns(at, size):
        gate_w, up_w = w[:, pl.ds(at, size)], w[:, pl.ds(cols + at, size)]
        gate = jnp.dot(x[...], gate_w, preferred_element_type=f32)
        up = jnp.dot(x[...], up_w, preferred_element_type=f32)
        grad = lax.dot_general(
            g[...], d[pl.ds(at, size)], contract_last, preferred_element_type=f32
        )
        sig = 1.0 / (1.0 + jnp.exp(-gate))
        act = gate * sig
        mid[:, pl.ds(at, size)] = (act * up).astype(bf16)
        both[:, pl.ds(at, size)] = (grad * up * (sig * (1.0 + gate * (1.0 - sig)))).astype(bf16)
        both[:, pl.ds(cols + at, size)] = (grad * act).astype(bf16)

    full = cols // 256
    pl.loop(0, full)(lambda c: columns(pl.multiple_of(c * 256, 256), 256))
    if cols % 256:
        columns(full * 256, cols % 256)
    for i in range(count):
        at = slice(i * rows, (i + 1) * rows)
        mixed_refs[i][...] = mid[at].astype(f32).T.astype(bf16)
        both_refs[i][...] = both[at]

    @pl.loop(0, width // 256)
    def _(t):
        at = pl.multiple_of(t * 256, 256)
        back = lax.dot_general(
            both[...], w[pl.ds(at, 256)], contract_last, preferred_element_type=f32
        ).astype(bf16)
        out = jnp.dot(mid[...], d[:, pl.ds(at, 256)], preferred_element_type=f32).astype(bf16)
        for i in range(count):
            back_refs[i][:, pl.ds(at, 256)] = back[i * rows : (i + 1) * rows]
            out_refs[i][:, pl.ds(at, 256)] = out[i * rows : (i + 1) * rows]


def ffn(info, xs, gs, parts, d_own, d_other):
    n = lax.axis_size("fsdp")
    count = len(xs)
    rows, width = xs[0].shape
    cols = 2 * d_own.shape[0]
    if cols % 128:
        return ffn_plain(info, xs, gs, parts, d_own, d_other)
    shapes = (
        [jax.ShapeDtypeStruct((cols, rows), bf16)] * count
        + [jax.ShapeDtypeStruct((rows, 2 * cols), bf16)] * count
        + [jax.ShapeDtypeStruct((rows, width), bf16)] * (2 * count)
    )
    vmem, hbm = pl.BlockSpec(memory_space=pltpu.VMEM), pl.BlockSpec(memory_space=pl.ANY)
    outs = pl.pallas_call(
        functools.partial(ffn_kernel, n, count),
        out_shape=shapes,
        in_specs=[pl.BlockSpec(memory_space=pltpu.SMEM)] + [vmem] * (2 * count) + [hbm] * 6,
        out_specs=[vmem] * (4 * count),
        scratch_shapes=[
            pltpu.VMEM((count * rows, width), bf16),
            pltpu.VMEM((count * rows, width), bf16),
            pltpu.VMEM((width, 2 * cols), bf16),
            pltpu.VMEM((cols, width), bf16),
            pltpu.VMEM((count * rows, 2 * cols), bf16),
            pltpu.VMEM((count * rows, cols), bf16),
            pltpu.SemaphoreType.DMA((2 * n + 2,)),
        ],
        compiler_params=pltpu.CompilerParams(vmem_limit_bytes=56 << 20),
        cost_estimate=pl.CostEstimate(
            flops=2 * count * rows * width * cols * 6,
            bytes_accessed=6 * width * cols,
            transcendentals=count * rows * cols,
        ),
    )(info, *xs, *gs, *parts, d_own, d_other)
    return [outs[i * count : (i + 1) * count] for i in range(4)]


def ffn_plain(info, xs, gs, parts, d_own, d_other):
    n = lax.axis_size("fsdp")
    me, part = info[0], info[1]
    width, share = xs[0].shape[1], d_own.shape[0]
    block, cols = width // n, 2 * share
    half = block // 2
    w = jnp.zeros((width, 2 * cols), bf16)
    for source, ks in zip(parts, part_pieces(n), strict=True):
        for i, k in enumerate(ks):
            for j in range(2):
                at = j if k < 2 else (part if j == 0 else 1 - part)
                rows = source[i * block + j * half : i * block + (j + 1) * half]
                w = lax.dynamic_update_slice_in_dim(w, rows, (me ^ k) * block + at * half, 0)
    d = jnp.where(
        me % 2 == 0, jnp.concatenate([d_own, d_other], 0), jnp.concatenate([d_other, d_own], 0)
    )
    mixed, both, back, out = [], [], [], []
    for x, g in zip(xs, gs, strict=True):
        gate, up = dot(x, w[:, :cols]), dot(x, w[:, cols:])
        sig = jax.nn.sigmoid(gate)
        act = gate * sig
        grad = dot_last(g, d)
        mid = (act * up).astype(bf16)
        two = jnp.concatenate(
            [grad * up * (sig * (1.0 + gate * (1.0 - sig))), grad * act], 1
        ).astype(bf16)
        mixed.append(mid.T)
        both.append(two)
        back.append(dot_last(two, w).astype(bf16))
        out.append(dot(mid, d).astype(bf16))
    return mixed, both, back, out


def down_grad_kernel(count, info_ref, *refs):
    lefts, rights, rest = refs[:count], refs[count : 2 * count], refs[2 * count :]
    total = sum(
        jnp.dot(one[...], two[...], preferred_element_type=f32)
        for one, two in zip(lefts, rights, strict=True)
    )
    if len(rest) == 2:
        total = total.astype(bf16).astype(f32) + rest[0][...].astype(f32)
    rest[-1][...] = total.astype(bf16)


def down_grad(info, at, mixed, gs, got=None):
    count = len(mixed)
    cols, rows = mixed[0].shape
    width = gs[0].shape[1]
    size = min(512, width)
    out = pl.BlockSpec((cols // 2, size), lambda i, info: (0, i))
    return pl.pallas_call(
        functools.partial(down_grad_kernel, count),
        out_shape=jax.ShapeDtypeStruct((cols // 2, width), bf16),
        grid_spec=pltpu.PrefetchScalarGridSpec(
            num_scalar_prefetch=1,
            grid=(width // size,),
            in_specs=[pl.BlockSpec((cols // 2, rows), lambda i, info: (info[at], 0))] * count
            + [pl.BlockSpec((rows, size), lambda i, info: (0, i))] * count
            + ([] if got is None else [out]),
            out_specs=out,
        ),
        compiler_params=pltpu.CompilerParams(vmem_limit_bytes=40 << 20),
        cost_estimate=pl.CostEstimate(
            flops=count * rows * width * cols,
            bytes_accessed=4 * width * cols,
            transcendentals=0,
        ),
    )(info, *mixed, *gs, *([] if got is None else [got]))


def up_grad_kernel(count, split, info_ref, *refs):
    lefts, rights, rest = refs[:count], refs[count : 2 * count], refs[2 * count :]
    total = sum(
        lax.dot_general(one[...], two[...], contract_first, preferred_element_type=f32)
        for one, two in zip(lefts, rights, strict=True)
    ).astype(bf16)
    if not split:
        rest[0][...] = total
        return
    total = (total.astype(f32) + rest[0][...].astype(f32)).astype(bf16)
    for i, out in enumerate(rest[1:]):

        @pl.when(pl.program_id(1) == i)
        def _(out=out):
            out[...] = total


def up_grad(table, xs, both, got=None):
    count, chips = len(xs), table.shape[0]
    rows, width = xs[0].shape
    cols = both[0].shape[1] // 2
    block = width // lax.axis_size("fsdp")
    if cols % 128 or block % 128:
        whole = sum(dot_first(one, two) for one, two in zip(xs, both, strict=True))
        outs = [
            lax.dynamic_slice_in_dim(whole, table[i] * block, block, 0).astype(bf16)
            for i in range(chips)
        ]
        if got is None:
            return jnp.concatenate(outs, 0)
        return [added(x, got[i * block : (i + 1) * block]) for i, x in enumerate(outs)]
    one = pl.BlockSpec((block, cols), lambda h, b, table: (b, h))
    outs = [
        pl.BlockSpec(
            (block, cols), lambda h, b, table, i=i: (0, jnp.where(b >= i, h, jnp.maximum(h - 1, 0)))
        )
        for i in range(chips)
    ]
    split = got is not None
    shape = jax.ShapeDtypeStruct((block, 2 * cols), bf16)
    return pl.pallas_call(
        functools.partial(up_grad_kernel, count, split),
        out_shape=[shape] * chips
        if split
        else jax.ShapeDtypeStruct((chips * block, 2 * cols), bf16),
        grid_spec=pltpu.PrefetchScalarGridSpec(
            num_scalar_prefetch=1,
            grid=(2, chips),
            in_specs=[pl.BlockSpec((rows, block), lambda h, b, table: (0, table[b]))] * count
            + [pl.BlockSpec((rows, cols), lambda h, b, table: (0, h))] * count
            + ([one] if split else []),
            out_specs=outs if split else one,
        ),
        compiler_params=pltpu.CompilerParams(vmem_limit_bytes=48 << 20),
        cost_estimate=pl.CostEstimate(
            flops=4 * count * rows * chips * block * cols,
            bytes_accessed=4 * chips * block * cols * 2,
            transcendentals=0,
        ),
    )(table, *xs, *both, *([got] if split else []))


def angle_tables(positions):
    half_dim = HD // 2
    inverse = 10000.0 ** (-jnp.arange(half_dim, dtype=f32) * 2.0 / HD)
    angles = positions.astype(f32)[:, None] * inverse[None, :]
    return jnp.cos(angles), jnp.sin(angles)


def norm_factor(values):
    return lax.rsqrt(jnp.mean(values * values, axis=-1, keepdims=True) + epsilon)


def norm_back(incoming, inputs, factor, gain):
    weighted = incoming * gain
    gain_grad = jnp.sum(incoming * (inputs * factor), axis=0)
    input_grad = weighted * factor - inputs * (factor * factor * factor) * jnp.mean(
        weighted * inputs, axis=-1, keepdims=True
    )
    return (gain_grad, input_grad)


def dot(one, two):
    return jnp.dot(one, two, preferred_element_type=f32)


def dot_last(one, two):
    return lax.dot_general(one, two, contract_last, preferred_element_type=f32)


def dot_first(one, two):
    return lax.dot_general(one, two, contract_first, preferred_element_type=f32)


def on_device(
    hidden_in, norm_attn, qkv_weight, out_weight, norm_ffn, gate_up_weight, down_weight, cotangent
):
    n = lax.axis_size("fsdp")
    me = lax.axis_index("fsdp")
    chips, chip, core = n // 2, me // 2, me % 2
    order = piece_order()
    evens = order[:chips]
    near, rest = evens[1:3], evens[3:]
    width = hidden_in.shape[2]
    rows = hidden_in.shape[0] * hidden_in.shape[1]
    q_width = HEADS * HD
    kv_width = KVH * HD
    share = FF // n
    chip_share = 2 * share
    block = width // n
    half = block // 2
    seq_at = lax.axis_index("seq")
    rank = {k: i for i, k in enumerate(order)}
    to_table = (me ^ jnp.array(order, jnp.int32)).astype(jnp.int32)
    at_table = jnp.array([rank[k] for k in range(n)], jnp.int32)[
        me ^ jnp.arange(n, dtype=jnp.int32)
    ]
    odd_table, even_table = to_table[chips:], to_table[:chips]
    assisted = lax.axis_size("seq") % 2 == 0
    part_at = seq_at % 2 if assisted else jnp.zeros_like(seq_at)

    live = {}

    def fence(**more):
        live.update(more)
        new = lax.optimization_barrier(live)
        live.clear()
        live.update(new)

    def two_hops(pieces):
        if len(rest) != 1:
            return {k: send(pieces[0], k) for k in rest}
        a, b = near
        size = pieces[0].shape[0] // 2
        lower, upper = send(pieces[b][:size], a), send(pieces[a][size:], b)
        return {rest[0]: (lower, upper)}

    def whole_piece(x):
        return jnp.concatenate(x, 0) if isinstance(x, tuple) else x

    def my_columns(k, at):
        cols = chip ^ (k // 2)
        spots = jnp.stack([cols, cols + chips]).astype(jnp.int32)
        if at is None:
            return pick(live["gate_up"], spots, chip_share)
        if chip_share % 128:
            part = pick(live["gate_up"], spots, chip_share)
            return lax.dynamic_slice_in_dim(part, at * half, half, 0)
        return pick(live["gate_up"], spots, chip_share, rows_at=(at, half))

    def other_half(k, first):
        return neighbour(first) if assisted else send(live["others"][k], k)

    full_qkv = lax.all_gather(qkv_weight, "fsdp", axis=0, tiled=True)
    fence(
        gains=gather_small(jnp.stack([norm_attn, norm_ffn])),
        hidden=hidden_in.reshape(rows, width),
        grad=cotangent.reshape(rows, width),
        gate_up=gate_up_weight,
        down=down_weight,
        out=out_weight,
    )

    firsts = {k: send(my_columns(k, part_at), k) for k in near}
    fence(
        firsts=firsts,
        others={} if assisted else {k: my_columns(k, 1 - part_at) for k in evens[1:]},
        own=my_columns(0, None),
        d_other=send(live["down"], 1),
    )
    inputs = live["hidden"].astype(f32)
    factor_one = norm_factor(inputs)
    gains = live["gains"].astype(f32)
    normed_one = (inputs * factor_one * gains[:1]).astype(bf16)
    fence(
        seconds={k: other_half(k, live["firsts"][k]) for k in near},
        mine={k: my_columns(k, part_at) for k in rest},
        qkv=full_qkv,
        normed_one=normed_one,
        normed_one_x=pick(normed_one, to_table, block),
    )
    del live["gate_up"]

    normed_one = live.pop("normed_one")
    joined = dot(normed_one, live["qkv"][:, q_width:])
    positions = seq_at * rows + jnp.arange(rows, dtype=jnp.int32)
    cosine, sine = angle_tables(positions)
    cos_wide, sin_wide = jnp.tile(cosine, (1, 2 * KVH)), jnp.tile(sine, (1, 2 * KVH))
    cos_t, sin_t = cosine.T, sine.T
    keys_values = jnp.concatenate(
        [turn(joined[:, :kv_width], cos_wide, sin_wide, 1), joined[:, kv_width:].astype(bf16)], 1
    )
    all_kv = lax.all_gather(keys_values, "seq", axis=0, tiled=True)
    joined = dot(normed_one, live["qkv"][:, :q_width])
    outs = {0: live.pop("out")}
    outs |= {k: send(outs[0], k) for k in near}
    firsts, seconds = live.pop("firsts"), live.pop("seconds")
    w_own = jnp.concatenate(sum([[firsts[k], seconds[k]] for k in near], [live.pop("own")]), 0)
    fence(w_own=w_own, joined=joined, kv=all_kv, outs=outs)

    outs = live.pop("outs")
    outs |= two_hops(outs)
    firsts = {k: send(x, k) for k, x in live.pop("mine").items()}
    info = jnp.concatenate([(seq_at * rows).reshape(1), at_table]).astype(jnp.int32)
    attended, lse = attend(info, live["joined"], live["kv"], cos_t, sin_t)
    fence(firsts=firsts, outs=outs, attended=attended, lse=lse, w_other=send(live["w_own"], 1))

    outs, firsts = live.pop("outs"), live.pop("firsts")
    out_even = jnp.concatenate([whole_piece(outs[k]) for k in evens], 0)
    out_odd = send(out_even, 1)
    grads = {0: live["grad"]}
    grads |= {k: send(grads[0], k) for k in near}
    seconds = {k: other_half(k, firsts[k]) for k in rest}
    middle = dot(live["attended"][:, : q_width // 2], out_even)
    middle = live["hidden"].astype(f32) + (
        middle + dot(live["attended"][:, q_width // 2 :], out_odd)
    )
    factor_two = norm_factor(middle)
    gain_two = live["gains"][1:].astype(f32)
    normed_two = (middle * factor_two * gain_two).astype(bf16)
    fence(
        firsts=firsts,
        seconds=seconds,
        out_even=out_even,
        out_odd=out_odd,
        grads=grads,
        middle=middle,
        tokens={0: normed_two},
    )

    ffn_info = jnp.stack([me, part_at, core, 1 - core]).astype(jnp.int32)

    def ffn_of(group):
        names = ("mixed", "both", "back", "parts")
        weights = [live[k] for k in ("w_own", "w_rest", "w_other", "w_rest_other")]
        results = ffn(
            ffn_info,
            [whole_piece(live["tokens"][k]) for k in group],
            [whole_piece(live["grads"][k]) for k in group],
            weights,
            live["down"],
            live["d_other"],
        )
        for name, new in zip(names, results, strict=True):
            live[name] = live.get(name, {}) | dict(zip(group, new, strict=True))

    new = {k: send(live["tokens"][0], k) for k in near}
    firsts, seconds = live.pop("firsts"), live.pop("seconds")
    w_rest = sum([[firsts[k], seconds[k]] for k in rest], [])
    live["w_rest"] = jnp.concatenate(w_rest or [live["w_own"]], 0)
    live["w_rest_other"] = send(live["w_rest"], 1)
    ffn_of([0])
    live["tokens"] |= new
    fence()
    far_tokens, far_grads = two_hops(live["tokens"]), two_hops(live["grads"])
    ffn_of(near)
    live["tokens"] |= far_tokens
    live["grads"] |= far_grads
    fence()
    new = {k: send(live["back"][k], k) for k in near}
    if rest:
        ffn_of(rest)
    fence(returned=new)

    live["returned"] |= {k: send(live["back"][k], k) for k in rest}

    def each(name):
        return [whole_piece(live[name][k]) for k in evens]

    theirs = down_grad(ffn_info, 3, each("mixed"), each("grads"))
    gots = up_grad(after(odd_table, theirs), each("tokens"), each("both"))
    got = send(theirs, 1)
    grad_down = down_grad(after(ffn_info, gots), 2, each("mixed"), each("grads"), got)
    fence(gots=gots, zd=grad_down[: share // 2], ze=grad_down[share // 2 :])

    line_step(live, new="d")
    gots = send(live.pop("gots"), 1)
    grad_normed_two = live["back"][0].astype(f32)
    for k in evens[1:]:
        grad_normed_two = grad_normed_two + live["returned"][k].astype(f32)
    middle = live["middle"]
    factor_two = norm_factor(middle)
    gain_two = live["gains"][1:].astype(f32)
    grad_gain_two, grad_norm_two = norm_back(grad_normed_two, middle, factor_two, gain_two)
    grad_middle = live["grad"].astype(f32) + grad_norm_two
    grad_branch = grad_middle.astype(bf16)
    grad_attended = jnp.concatenate(
        [dot_last(grad_branch, live[k]).astype(bf16) for k in ("out_even", "out_odd")], 1
    )
    parts = up_grad(even_table, each("tokens"), each("both"), gots)
    for k in ("tokens", "grads", "both", "mixed", "back", "returned", "d_other"):
        del live[k]
    for k in ("w_own", "w_rest", "w_other", "w_rest_other"):
        del live[k]
    del live["out_even"], live["out_odd"], live["down"], live["grad"]
    fence(
        ups=dict(zip(evens, parts, strict=True)),
        grad_gain_two=grad_gain_two,
        grad_middle=grad_middle,
        grad_branch=grad_branch,
        grad_attended=grad_attended,
    )

    names = [str(k) for k in evens]

    def blocks(whole, got):
        return {
            k: added(whole[i * block : (i + 1) * block], got[i * block : (i + 1) * block])
            for i, k in enumerate(evens)
        }

    def far_sends(parts):
        if len(rest) != 1:
            return [send(parts[k], k) for k in rest]
        far = parts[rest[0]]
        size = far.shape[0] // 2
        return [send(far[:size], near[0]), send(far[size:], near[1])]

    def near_sends(parts, got):
        if len(rest) != 1:
            return [send(parts[k], k) for k in near]
        size = parts[0].shape[0] // 2
        lower, upper = got
        one, two = parts[near[0]], parts[near[1]]
        one = jnp.concatenate([one[:size], added(one[size:], upper)], 0)
        two = jnp.concatenate([added(two[:size], lower), two[size:]], 0)
        return [send(one, near[0]), send(two, near[1])]

    def total_of(parts, *got):
        total = parts[0].astype(f32)
        for x in sum([g for g in got if g[0].shape == parts[0].shape], []):
            total = total + x.astype(f32)
        return total

    line_step(live, new="e", cross="d")
    sent = {k: send(live["ups"][k], k) for k in near}
    grad_queries, kv_parts = attend_back(
        info, live["joined"], live["kv"], cos_t, sin_t, live["grad_attended"], live["lse"]
    )
    fence(sent=sent, grad_queries=grad_queries, kv_parts=kv_parts)
    for k in ("grad_attended", "joined", "kv", "lse"):
        del live[k]

    ups = live.pop("ups")
    live["z0"] = ups[0]
    for k, x in live.pop("sent").items():
        live[f"z{k}"] = x
    line_step(live, new=names[0], cross="e", out="d")
    sent = {k: send(ups[k], k) for k in rest}
    kv_sums = lax.psum_scatter(live.pop("kv_parts"), "seq", scatter_dimension=0, tiled=True)
    kv_sums = kv_sums.reshape(rows, KVH, 2, HD).transpose(0, 2, 1, 3).reshape(rows, 2 * kv_width)
    grad_joined = jnp.concatenate(
        [
            live.pop("grad_queries"),
            turn(kv_sums[:, :kv_width], cos_wide, sin_wide, -1),
            kv_sums[:, kv_width:],
        ],
        1,
    )
    normed_one_x = live.pop("normed_one_x")
    theirs = dot_first(normed_one_x[:, width // 2 :], grad_joined).astype(bf16)
    attended = pick(live.pop("attended"), at_table, block)
    grad_out = dot_first(attended, live.pop("grad_branch")).astype(bf16)
    fence(
        sent=sent,
        grad_out=grad_out,
        grad_joined=grad_joined,
        normed_one_x=normed_one_x,
        theirs=theirs,
    )

    for k, x in live.pop("sent").items():
        live[f"z{k}"] = x
    line_step(live, new=names[1], cross=names[0], out="e")
    out_total = lax.psum_scatter(live.pop("grad_out"), "fsdp", scatter_dimension=0, tiled=True)
    mine = dot_first(live.pop("normed_one_x")[:, : width // 2], live["grad_joined"])
    fence(got_qkv=send(live.pop("theirs"), 1), mine=mine.astype(bf16))

    gate_up_sums = blank((block, 2 * FF), f32)
    outer = is_outer()

    def summed(k):
        return jnp.where(outer, live.pop("o" + k), live.pop("t" + k)).astype(f32)

    def placed_in(buffer, k):
        cols = chip ^ (k // 2)
        spots = jnp.stack([cols, cols + chips])
        return place(buffer, (live.pop(f"o{k}"), live.pop(f"t{k}")), outer, spots, chip_share)

    line_step(live, new=names[2] if chips > 2 else None, cross=names[1], out=names[0])
    parts_qkv = blocks(live.pop("mine"), live.pop("got_qkv"))
    down_sums = jnp.concatenate([summed("d"), summed("e")], 0)
    fence(parts_qkv=parts_qkv, far_qkv=far_sends(parts_qkv), down_sums=down_sums)

    line_step(live, new=names[3] if chips > 3 else None, cross=names[2], out=names[1])
    for k in evens[4:]:
        line_step(live, new=str(k))
    gate_up_sums = placed_in(gate_up_sums, 0)
    inputs = live["hidden"].astype(f32)
    factor_one = norm_factor(inputs)
    grad_normed_one = dot_last(live.pop("grad_joined"), live.pop("qkv"))
    grad_gain_one, grad_norm_one = norm_back(
        grad_normed_one, inputs, factor_one, live["gains"][:1].astype(f32)
    )
    grad_input = (live["grad_middle"] + grad_norm_one).astype(bf16)
    fence(
        near_qkv=near_sends(live["parts_qkv"], live["far_qkv"]),
        zout=out_total,
        sums=gate_up_sums,
        grad_input=grad_input,
        grad_gains=jnp.stack([grad_gain_one, live.pop("grad_gain_two")]),
    )

    line_step(live, new="out", cross=names[3], out=names[2])
    gate_up_sums = placed_in(live.pop("sums"), evens[1])
    total = total_of(live.pop("parts_qkv"), live.pop("far_qkv"), live.pop("near_qkv")).astype(bf16)
    fence(far=far_sends(live["parts"]), sums=gate_up_sums, zq=total[:half], zr=total[half:])

    line_step(live, new="q", cross="out", out=names[3])
    gate_up_sums = placed_in(live.pop("sums"), evens[2])
    fence(near=near_sends(live["parts"], live["far"]), sums=gate_up_sums)

    line_step(live, new="r", cross="q", out="out")
    gate_up_sums = live.pop("sums")
    for k in evens[3:]:
        gate_up_sums = placed_in(gate_up_sums, k)
    grad_gains = small_sum(live.pop("grad_gains"), "fsdp")
    out = total_of(live.pop("parts"), live.pop("far"), live.pop("near"))
    out = (live["middle"] + out).astype(bf16)
    fence(sums=gate_up_sums, grad_gains=grad_gains, out_final=out)

    line_step(live, cross="r", out="q")
    fence(out_sums=summed("out"))

    line_step(live, out="r")
    grad_gains = small_sum(live.pop("grad_gains"), "seq")
    qkv_sums = jnp.concatenate([summed("q"), summed("r")], 0)
    grad_gains = lax.dynamic_slice_in_dim(grad_gains, me * block, block, 1)
    return (
        live["out_final"].reshape(hidden_in.shape),
        live["grad_input"].reshape(hidden_in.shape),
        grad_gains[0],
        qkv_sums,
        live["out_sums"],
        grad_gains[1],
        live["sums"],
        live["down_sums"],
    )


def solution(mesh):
    placed = (
        P("fsdp", "seq", None),
        P("fsdp"),
        P("fsdp", None),
        P("fsdp", None),
        P("fsdp"),
        P("fsdp", None),
        P("fsdp", None),
        P("fsdp", "seq", None),
    )
    return jax.shard_map(
        on_device,
        mesh=mesh,
        in_specs=placed,
        out_specs=(
            P("fsdp", "seq", None),
            P("fsdp", "seq", None),
            P("fsdp"),
            P("fsdp", None),
            P("fsdp", None),
            P("fsdp"),
            P("fsdp", None),
            P("fsdp", None),
        ),
        check_vma=False,
    )
```

```python
import functools

import jax
import jax.numpy as jnp
from jax import lax
from jax.experimental import pallas as pl
from jax.experimental.pallas import tpu as pltpu
from jax.sharding import PartitionSpec as P

HEADS = 32
KVH = 4
HD = 64
FF = 5632

epsilon = 1e-05
masked_value = -1e30
log2e = 1.4426950408889634
contract_last = (((1,), (1,)), ((), ()))
contract_first = (((0,), (0,)), ((), ()))
bf16 = jnp.bfloat16
f32 = jnp.float32


def send(x, k):
    n = lax.axis_size("fsdp")
    return lax.ppermute(x, "fsdp", [(i, i ^ k) for i in range(n)])


def chip_bits():
    n = lax.axis_size("fsdp")
    return [1 << i for i in range(1, n.bit_length() - 1)]


def piece_order():
    n = lax.axis_size("fsdp")
    return list(range(0, n, 2)) + list(range(1, n, 2))


def gather_small(x):
    n, me = lax.axis_size("fsdp"), lax.axis_index("fsdp")
    for k in (1 << i for i in range(n.bit_length() - 1)):
        got = send(x, k)
        x = jnp.where(
            me & k == 0, jnp.concatenate([x, got], 1), jnp.concatenate([got, x], 1)
        )
    return x


def neighbour(x):
    n = lax.axis_size("seq")
    return lax.ppermute(x, "seq", [(i, i ^ 1) for i in range(n)])


def after(x, *others):
    return lax.optimization_barrier((x, *others))[0]


def added(one, two):
    return (one.astype(f32) + two.astype(f32)).astype(bf16)


def line_sum(x):
    n = lax.axis_size("seq")
    if n == 1:
        return x
    if n % 2:
        return lax.psum(x.astype(f32), "seq").astype(bf16)
    me = lax.axis_index("seq")
    mid = n // 2
    total = x
    for i in range(mid - 1):
        total = added(total, lax.ppermute(total, "seq", [(i, i + 1), (n - 1 - i, n - 2 - i)]))
    total = added(total, lax.ppermute(total, "seq", [(mid - 1, mid), (mid, mid - 1)]))
    for i in range(mid - 1):
        got = lax.ppermute(total, "seq", [(mid - 1 - i, mid - 2 - i), (mid + i, mid + 1 + i)])
        taken = (me == mid - 2 - i) | (me == mid + 1 + i)
        total = jnp.where(taken, got, total)
    return total


def line_step(live, new=None, cross=None, out=None):
    if lax.axis_size("seq") != 4:
        if new is not None:
            live["o" + new] = live["t" + new] = line_sum(live["z" + new])
        return
    inward, outward, across = [(0, 1), (3, 2)], [(1, 0), (2, 3)], [(1, 2), (2, 1)]
    x = None if new is None else live["z" + new]
    part = None
    if cross is not None:
        part = live["p" + cross] = added(live["z" + cross], live["i" + cross])
        live["x" + cross] = lax.ppermute(part, "seq", across)
        others = {k: v for k, v in live.items() if not k.endswith(cross)}
        live.update(lax.optimization_barrier((others, part))[0])
    if x is not None:
        live["i" + new] = lax.ppermute(x, "seq", inward)
    if out is not None:
        total = live["t" + out] = added(live["p" + out], live["x" + out])
        live["o" + out] = lax.ppermute(total, "seq", outward)


def is_outer():
    me, n = lax.axis_index("seq"), lax.axis_size("seq")
    return (me == 0) | (me == n - 1)


def small_sum(x, axis):
    n = lax.axis_size(axis)
    if n & (n - 1):
        return lax.psum(x, axis)
    for k in (1 << i for i in range(n.bit_length() - 1)):
        x = x + lax.ppermute(x, axis, [(i, i ^ k) for i in range(n)])
    return x


def copy_kernel(table_ref, x_ref, o_ref):
    o_ref[...] = x_ref[...].astype(o_ref.dtype)


def pick(x, table, size, dtype=None, rows_at=None):
    rows, count = x.shape[0], table.shape[0]
    if size % 128:
        return jnp.concatenate(
            [lax.dynamic_slice_in_dim(x, table[i] * size, size, 1) for i in range(count)], 1
        ).astype(dtype or x.dtype)
    if rows_at is not None:
        rows = rows_at[1]
    row = jnp.zeros((), jnp.int32) if rows_at is None else rows_at[0]
    table = jnp.concatenate([table, row.reshape(1)]).astype(jnp.int32)
    return pl.pallas_call(
        copy_kernel,
        out_shape=jax.ShapeDtypeStruct((rows, count * size), dtype or x.dtype),
        grid_spec=pltpu.PrefetchScalarGridSpec(
            num_scalar_prefetch=1,
            grid=(count,),
            in_specs=[pl.BlockSpec((rows, size), lambda i, table: (table[count], table[i]))],
            out_specs=pl.BlockSpec((rows, size), lambda i, table: (0, i)),
        ),
        cost_estimate=pl.CostEstimate(
            flops=0, transcendentals=0, bytes_accessed=rows * count * size * 4
        ),
    )(table, x)


def blank_kernel(o_ref):
    pass


def blank(shape, dtype):
    return pl.pallas_call(
        blank_kernel,
        out_shape=jax.ShapeDtypeStruct(shape, dtype),
        out_specs=pl.BlockSpec(memory_space=pl.ANY),
    )()


def turn_kernel(sign, x_ref, cos_ref, sin_ref, o_ref):
    x = x_ref[...].astype(f32)
    width = x.shape[1]
    lane = lax.broadcasted_iota(jnp.int32, x.shape, 1)
    first = (lane % HD) < HD // 2
    other = jnp.where(
        first, -pltpu.roll(x, width - HD // 2, 1), pltpu.roll(x, HD // 2, 1)
    )
    o_ref[...] = (x * cos_ref[...] + sign * other * sin_ref[...]).astype(o_ref.dtype)


def turn(x, cos_wide, sin_wide, sign):
    return pl.pallas_call(
        functools.partial(turn_kernel, float(sign)),
        out_shape=jax.ShapeDtypeStruct(x.shape, bf16),
    )(x, cos_wide, sin_wide)


def place_kernel(info_ref, buffer_ref, got_ref, total_ref, o_ref):
    o_ref[...] = jnp.where(info_ref[0] == 1, got_ref[...], total_ref[...]).astype(f32)


def place(buffer, pair, outer, where, size):
    got, total = pair
    rows = got.shape[0]
    if size % 128:
        picked = jnp.where(outer, got, total).astype(f32)
        for i in range(2):
            buffer = lax.dynamic_update_slice_in_dim(
                buffer, picked[:, i * size : (i + 1) * size], where[i] * size, 1
            )
        return buffer
    info = jnp.concatenate([outer.astype(jnp.int32).reshape(1), where.astype(jnp.int32)])
    own = pl.BlockSpec((rows, size), lambda i, info: (0, i))
    return pl.pallas_call(
        place_kernel,
        out_shape=jax.ShapeDtypeStruct(buffer.shape, f32),
        grid_spec=pltpu.PrefetchScalarGridSpec(
            num_scalar_prefetch=1,
            grid=(2,),
            in_specs=[pl.BlockSpec(memory_space=pl.ANY), own, own],
            out_specs=pl.BlockSpec((rows, size), lambda i, info: (0, info[1 + i])),
        ),
        input_output_aliases={1: 0},
    )(info, buffer, got, total)


def mask_bias(start, length, rows):
    key_place = lax.broadcasted_iota(jnp.int32, (length, rows), 0)
    query_place = start + lax.broadcasted_iota(jnp.int32, (length, rows), 1)
    return jnp.where(key_place <= query_place, 0.0, masked_value).astype(f32)


def turned_t(x, cos, sin):
    one, two = x[: HD // 2], x[HD // 2 :]
    return jnp.concatenate([one * cos - two * sin, two * cos + one * sin], 0)


def kv_head(ref, index):
    both = ref[...]
    return jnp.where(index % 2 == 0, both[:, :HD], both[:, HD:])


def attend_kernel(
    heads, per_kv, info_ref, q_ref, k_ref, v_ref, cos_ref, sin_ref, o_ref, lse_ref, bias_ref
):
    length, rows = k_ref.shape[0], q_ref.shape[0]
    scale2 = HD**-0.5 * log2e
    step = pl.program_id(0)

    @pl.when(step == 0)
    def _():
        bias_ref[...] = mask_bias(info_ref[0], length, rows)

    kv = step * heads // per_kv
    keys = kv_head(k_ref, kv)
    values_t = kv_head(v_ref, kv).astype(f32).T.astype(bf16)
    q_t = q_ref[...].T
    cos, sin = cos_ref[...], sin_ref[...]
    q_all = [
        turned_t(q_t[h * HD : (h + 1) * HD], cos, sin).astype(bf16) for h in range(heads)
    ]

    key_size = jnp.max(jnp.sum(jnp.square(keys.astype(f32)), axis=1))
    query_size = jnp.max(
        sum(
            jnp.sum(jnp.square(q.astype(f32)), axis=0, keepdims=True) for q in q_all
        )
    )
    small = key_size * query_size * scale2**2 < 50.0**2

    def run(shift):
        outs = []
        for h in range(heads):
            scores = jnp.dot(keys, q_all[h], preferred_element_type=f32) + bias_ref[...]
            if shift:
                top = jnp.max(scores, axis=0, keepdims=True)
                weights = jnp.exp2((scores - top) * scale2)
            else:
                weights = jnp.exp2(scores * scale2)
            total = jnp.sum(weights, axis=0, keepdims=True)
            out = jnp.dot(values_t, weights.astype(bf16), preferred_element_type=f32)
            outs.append(out * (1.0 / total))
            lse = jnp.log2(total)
            lse_ref[0, h : h + 1, :] = lse + top * scale2 if shift else lse
        o_ref[...] = jnp.concatenate(outs, 0).T.astype(bf16)

    pl.when(small)(lambda: run(False))
    pl.when(jnp.logical_not(small))(lambda: run(True))


def attend_specs(n, rows, length):
    heads = HEADS // n
    per_kv = HEADS // KVH
    kv_at = lambda i: (i * heads // per_kv) // 2
    return dict(
        plain=pl.BlockSpec((rows, heads * HD), lambda i, info: (0, i)),
        ordered=pl.BlockSpec((rows, heads * HD), lambda i, info: (0, info[1 + i])),
        keys=pl.BlockSpec((length, 2 * HD), lambda i, info: (0, kv_at(i))),
        values=pl.BlockSpec((length, 2 * HD), lambda i, info: (0, KVH // 2 + kv_at(i))),
        table=pl.BlockSpec((HD // 2, rows), lambda i, info: (0, 0)),
        lse=pl.BlockSpec((1, heads, rows), lambda i, info: (i, 0, 0)),
    )


def attend(info, joined, all_kv, cos_t, sin_t):
    n = lax.axis_size("fsdp")
    rows, length = joined.shape[0], all_kv.shape[0]
    heads = HEADS // n
    spec = attend_specs(n, rows, length)
    return pl.pallas_call(
        functools.partial(attend_kernel, heads, HEADS // KVH),
        out_shape=(
            jax.ShapeDtypeStruct((rows, HEADS * HD), bf16),
            jax.ShapeDtypeStruct((n, heads, rows), f32),
        ),
        grid_spec=pltpu.PrefetchScalarGridSpec(
            num_scalar_prefetch=1,
            grid=(n,),
            in_specs=[spec[k] for k in ("plain", "keys", "values", "table", "table")],
            out_specs=(spec["ordered"], spec["lse"]),
            scratch_shapes=[pltpu.VMEM((length, rows), f32)],
        ),
        compiler_params=pltpu.CompilerParams(vmem_limit_bytes=40 << 20),
        cost_estimate=pl.CostEstimate(
            flops=4 * HEADS * rows * length * HD * 4,
            bytes_accessed=6 * rows * HEADS * HD,
            transcendentals=HEADS * rows * length,
        ),
    )(info, joined, all_kv, all_kv, cos_t, sin_t)


def attend_back_kernel(
    heads, per_kv, info_ref, q_ref, k_ref, v_ref, g_ref, o_ref, cos_ref, sin_ref, lse_ref,
    dq_ref, dkv_ref, bias_ref, dk_ref, dv_ref,
):
    length, rows = k_ref.shape[0], q_ref.shape[0]
    scale = HD**-0.5
    scale2 = scale * log2e
    step = pl.program_id(0)
    steps = per_kv // heads

    @pl.when(step == 0)
    def _():
        bias_ref[...] = mask_bias(info_ref[0], length, rows)

    @pl.when(step % steps == 0)
    def _():
        dk_ref[...] = jnp.zeros_like(dk_ref)
        dv_ref[...] = jnp.zeros_like(dv_ref)

    kv = step * heads // per_kv
    keys, values = kv_head(k_ref, kv), kv_head(v_ref, kv)
    keys_t = keys.astype(f32).T.astype(bf16)
    q_t = q_ref[...].T
    g_t = g_ref[...].astype(f32).T
    deltas = g_t * o_ref[...].astype(f32).T
    g_t = g_t.astype(bf16)
    cos, sin = cos_ref[...], sin_ref[...]
    outs = []
    dk, dv = dk_ref[...], dv_ref[...]
    for h in range(heads):
        q_h = turned_t(q_t[h * HD : (h + 1) * HD], cos, sin).astype(bf16)
        g_h = g_t[h * HD : (h + 1) * HD]
        scores = jnp.dot(keys, q_h, preferred_element_type=f32) + bias_ref[...]
        weights = jnp.exp2(scores * scale2 - lse_ref[0, h : h + 1, :])
        grad_p = jnp.dot(values, g_h, preferred_element_type=f32)
        delta = jnp.sum(deltas[h * HD : (h + 1) * HD], axis=0, keepdims=True)
        grad_s = (weights * (grad_p - delta)).astype(bf16)
        grad_q = jnp.dot(keys_t, grad_s, preferred_element_type=f32) * scale
        outs.append(turned_t(grad_q.astype(bf16).astype(f32), cos, -sin))
        dk += lax.dot_general(grad_s, q_h, contract_last, preferred_element_type=f32)
        dv += lax.dot_general(
            weights.astype(bf16), g_h, contract_last, preferred_element_type=f32
        )
    dk_ref[...], dv_ref[...] = dk, dv
    dq_ref[...] = jnp.concatenate(outs, 0).T.astype(bf16)

    @pl.when(step % steps == steps - 1)
    def _():
        dkv_ref[...] = jnp.concatenate([dk * scale, dv], 1).astype(bf16)


def attend_back(info, joined, all_kv, cos_t, sin_t, grads, outs, lse):
    n = lax.axis_size("fsdp")
    rows, length = joined.shape[0], all_kv.shape[0]
    heads, per_kv = HEADS // n, HEADS // KVH
    spec = attend_specs(n, rows, length)
    names = ("plain", "keys", "values", "ordered", "ordered", "table", "table", "lse")
    return pl.pallas_call(
        functools.partial(attend_back_kernel, heads, per_kv),
        out_shape=(
            jax.ShapeDtypeStruct((rows, HEADS * HD), bf16),
            jax.ShapeDtypeStruct((length, 2 * KVH * HD), bf16),
        ),
        grid_spec=pltpu.PrefetchScalarGridSpec(
            num_scalar_prefetch=1,
            grid=(n,),
            in_specs=[spec[k] for k in names],
            out_specs=(
                spec["plain"],
                pl.BlockSpec((length, 2 * HD), lambda i, info: (0, i * heads // per_kv)),
            ),
            scratch_shapes=[
                pltpu.VMEM((length, rows), f32),
                pltpu.VMEM((length, HD), f32),
                pltpu.VMEM((length, HD), f32),
            ],
        ),
        compiler_params=pltpu.CompilerParams(vmem_limit_bytes=48 << 20),
        cost_estimate=pl.CostEstimate(
            flops=10 * HEADS * rows * length * HD * 4,
            bytes_accessed=8 * rows * HEADS * HD,
            transcendentals=HEADS * rows * length,
        ),
    )(info, joined, all_kv, all_kv, grads, outs, cos_t, sin_t, lse)


def column_chunks(total, size=256):
    return [(c, min(size, total - c)) for c in range(0, total, size)]


def part_pieces(n):
    evens = list(range(0, n, 2))
    return evens[:3], evens[3:], [k | 1 for k in evens[:3]], [k | 1 for k in evens[3:]]


def ffn_kernel(n, count, info_ref, *refs):
    x_refs, g_refs, refs = refs[:count], refs[count : 2 * count], refs[2 * count :]
    parts, (d_own, d_other), refs = refs[:4], refs[4:6], refs[6:]
    outs, (x, g, w, d, both, mid, sems) = refs[: 4 * count], refs[4 * count :]
    mixed_refs, both_refs = outs[:count], outs[count : 2 * count]
    back_refs, out_refs = outs[2 * count : 3 * count], outs[3 * count :]
    me, part = info_ref[0], info_ref[1]
    rows, width = x_refs[0].shape
    cols = d.shape[0]
    share = cols // 2
    block = width // n
    half = block // 2

    copies = []
    for source, ks in zip(parts, part_pieces(n), strict=True):
        for i, k in enumerate(ks):
            owner = (me ^ k) * block
            for j in range(2):
                at = owner if k < 2 else owner + (part if j == 0 else 1 - part) * half
                if k < 2:
                    at = at + j * half
                copies.append(
                    pltpu.make_async_copy(
                        source.at[pl.ds(i * block + j * half, half)],
                        w.at[pl.ds(pl.multiple_of(at, half), half)],
                        sems.at[len(copies)],
                    )
                )
    core = me % 2
    for source, at in ((d_own, core), (d_other, 1 - core)):
        copies.append(
            pltpu.make_async_copy(
                source, d.at[pl.ds(pl.multiple_of(at * share, share), share)], sems.at[len(copies)]
            )
        )
    for copy in copies:
        copy.start()
    for i in range(count):
        x[i * rows : (i + 1) * rows] = x_refs[i][...]
        g[i * rows : (i + 1) * rows] = g_refs[i][...]
    for copy in copies:
        copy.wait()

    def columns(at, size):
        gate_w, up_w = w[:, pl.ds(at, size)], w[:, pl.ds(cols + at, size)]
        gate = jnp.dot(x[...], gate_w, preferred_element_type=f32)
        up = jnp.dot(x[...], up_w, preferred_element_type=f32)
        grad = lax.dot_general(
            g[...], d[pl.ds(at, size)], contract_last, preferred_element_type=f32
        )
        sig = 1.0 / (1.0 + jnp.exp(-gate))
        act = gate * sig
        mid[:, pl.ds(at, size)] = (act * up).astype(bf16)
        both[:, pl.ds(at, size)] = (grad * up * (sig * (1.0 + gate * (1.0 - sig)))).astype(bf16)
        both[:, pl.ds(cols + at, size)] = (grad * act).astype(bf16)

    full = cols // 256
    pl.loop(0, full)(lambda c: columns(pl.multiple_of(c * 256, 256), 256))
    if cols % 256:
        columns(full * 256, cols % 256)
    for i in range(count):
        at = slice(i * rows, (i + 1) * rows)
        mixed_refs[i][...] = mid[at].astype(f32).T.astype(bf16)
        both_refs[i][...] = both[at]

    @pl.loop(0, width // 256)
    def _(t):
        at = pl.multiple_of(t * 256, 256)
        back = lax.dot_general(
            both[...], w[pl.ds(at, 256)], contract_last, preferred_element_type=f32
        ).astype(bf16)
        out = jnp.dot(mid[...], d[:, pl.ds(at, 256)], preferred_element_type=f32).astype(bf16)
        for i in range(count):
            back_refs[i][:, pl.ds(at, 256)] = back[i * rows : (i + 1) * rows]
            out_refs[i][:, pl.ds(at, 256)] = out[i * rows : (i + 1) * rows]


def ffn(info, xs, gs, parts, d_own, d_other):
    n = lax.axis_size("fsdp")
    count = len(xs)
    rows, width = xs[0].shape
    cols = 2 * d_own.shape[0]
    if cols % 128:
        return ffn_plain(info, xs, gs, parts, d_own, d_other)
    shapes = (
        [jax.ShapeDtypeStruct((cols, rows), bf16)] * count
        + [jax.ShapeDtypeStruct((rows, 2 * cols), bf16)] * count
        + [jax.ShapeDtypeStruct((rows, width), bf16)] * (2 * count)
    )
    vmem, hbm = pl.BlockSpec(memory_space=pltpu.VMEM), pl.BlockSpec(memory_space=pl.ANY)
    outs = pl.pallas_call(
        functools.partial(ffn_kernel, n, count),
        out_shape=shapes,
        in_specs=[pl.BlockSpec(memory_space=pltpu.SMEM)] + [vmem] * (2 * count) + [hbm] * 6,
        out_specs=[vmem] * (4 * count),
        scratch_shapes=[
            pltpu.VMEM((count * rows, width), bf16),
            pltpu.VMEM((count * rows, width), bf16),
            pltpu.VMEM((width, 2 * cols), bf16),
            pltpu.VMEM((cols, width), bf16),
            pltpu.VMEM((count * rows, 2 * cols), bf16),
            pltpu.VMEM((count * rows, cols), bf16),
            pltpu.SemaphoreType.DMA((2 * n + 2,)),
        ],
        compiler_params=pltpu.CompilerParams(vmem_limit_bytes=56 << 20),
        cost_estimate=pl.CostEstimate(
            flops=2 * count * rows * width * cols * 6,
            bytes_accessed=6 * width * cols,
            transcendentals=count * rows * cols,
        ),
    )(info, *xs, *gs, *parts, d_own, d_other)
    return [outs[i * count : (i + 1) * count] for i in range(4)]


def ffn_plain(info, xs, gs, parts, d_own, d_other):
    n = lax.axis_size("fsdp")
    me, part = info[0], info[1]
    width, share = xs[0].shape[1], d_own.shape[0]
    block, cols = width // n, 2 * share
    half = block // 2
    w = jnp.zeros((width, 2 * cols), bf16)
    for source, ks in zip(parts, part_pieces(n), strict=True):
        for i, k in enumerate(ks):
            for j in range(2):
                at = j if k < 2 else (part if j == 0 else 1 - part)
                rows = source[i * block + j * half : i * block + (j + 1) * half]
                w = lax.dynamic_update_slice_in_dim(w, rows, (me ^ k) * block + at * half, 0)
    d = jnp.where(
        me % 2 == 0, jnp.concatenate([d_own, d_other], 0), jnp.concatenate([d_other, d_own], 0)
    )
    mixed, both, back, out = [], [], [], []
    for x, g in zip(xs, gs, strict=True):
        gate, up = dot(x, w[:, :cols]), dot(x, w[:, cols:])
        sig = jax.nn.sigmoid(gate)
        act = gate * sig
        grad = dot_last(g, d)
        mid = (act * up).astype(bf16)
        two = jnp.concatenate(
            [grad * up * (sig * (1.0 + gate * (1.0 - sig))), grad * act], 1
        ).astype(bf16)
        mixed.append(mid.T)
        both.append(two)
        back.append(dot_last(two, w).astype(bf16))
        out.append(dot(mid, d).astype(bf16))
    return mixed, both, back, out


def down_grad_kernel(count, info_ref, *refs):
    lefts, rights, rest = refs[:count], refs[count : 2 * count], refs[2 * count :]
    total = sum(
        jnp.dot(one[...], two[...], preferred_element_type=f32)
        for one, two in zip(lefts, rights, strict=True)
    )
    if len(rest) == 2:
        total = total.astype(bf16).astype(f32) + rest[0][...].astype(f32)
    rest[-1][...] = total.astype(bf16)


def down_grad(info, at, mixed, gs, got=None):
    count = len(mixed)
    cols, rows = mixed[0].shape
    width = gs[0].shape[1]
    size = min(512, width)
    out = pl.BlockSpec((cols // 2, size), lambda i, info: (0, i))
    return pl.pallas_call(
        functools.partial(down_grad_kernel, count),
        out_shape=jax.ShapeDtypeStruct((cols // 2, width), bf16),
        grid_spec=pltpu.PrefetchScalarGridSpec(
            num_scalar_prefetch=1,
            grid=(width // size,),
            in_specs=[pl.BlockSpec((cols // 2, rows), lambda i, info: (info[at], 0))] * count
            + [pl.BlockSpec((rows, size), lambda i, info: (0, i))] * count
            + ([] if got is None else [out]),
            out_specs=out,
        ),
        compiler_params=pltpu.CompilerParams(vmem_limit_bytes=40 << 20),
        cost_estimate=pl.CostEstimate(
            flops=count * rows * width * cols,
            bytes_accessed=4 * width * cols,
            transcendentals=0,
        ),
    )(info, *mixed, *gs, *([] if got is None else [got]))


def up_grad_kernel(count, split, info_ref, *refs):
    lefts, rights, rest = refs[:count], refs[count : 2 * count], refs[2 * count :]
    total = sum(
        lax.dot_general(one[...], two[...], contract_first, preferred_element_type=f32)
        for one, two in zip(lefts, rights, strict=True)
    ).astype(bf16)
    if not split:
        rest[0][...] = total
        return
    total = (total.astype(f32) + rest[0][...].astype(f32)).astype(bf16)
    for i, out in enumerate(rest[1:]):

        @pl.when(pl.program_id(1) == i)
        def _(out=out):
            out[...] = total


def up_grad(table, xs, both, got=None):
    count, chips = len(xs), table.shape[0]
    rows, width = xs[0].shape
    cols = both[0].shape[1] // 2
    block = width // lax.axis_size("fsdp")
    if cols % 128 or block % 128:
        whole = sum(dot_first(one, two) for one, two in zip(xs, both, strict=True))
        outs = [
            lax.dynamic_slice_in_dim(whole, table[i] * block, block, 0).astype(bf16)
            for i in range(chips)
        ]
        if got is None:
            return jnp.concatenate(outs, 0)
        return [added(x, got[i * block : (i + 1) * block]) for i, x in enumerate(outs)]
    one = pl.BlockSpec((block, cols), lambda h, b, table: (b, h))
    outs = [
        pl.BlockSpec(
            (block, cols), lambda h, b, table, i=i: (0, jnp.where(b >= i, h, jnp.maximum(h - 1, 0)))
        )
        for i in range(chips)
    ]
    split = got is not None
    shape = jax.ShapeDtypeStruct((block, 2 * cols), bf16)
    return pl.pallas_call(
        functools.partial(up_grad_kernel, count, split),
        out_shape=[shape] * chips
        if split
        else jax.ShapeDtypeStruct((chips * block, 2 * cols), bf16),
        grid_spec=pltpu.PrefetchScalarGridSpec(
            num_scalar_prefetch=1,
            grid=(2, chips),
            in_specs=[pl.BlockSpec((rows, block), lambda h, b, table: (0, table[b]))] * count
            + [pl.BlockSpec((rows, cols), lambda h, b, table: (0, h))] * count
            + ([one] if split else []),
            out_specs=outs if split else one,
        ),
        compiler_params=pltpu.CompilerParams(vmem_limit_bytes=48 << 20),
        cost_estimate=pl.CostEstimate(
            flops=4 * count * rows * chips * block * cols,
            bytes_accessed=4 * chips * block * cols * 2,
            transcendentals=0,
        ),
    )(table, *xs, *both, *([got] if split else []))


def angle_tables(positions):
    half_dim = HD // 2
    inverse = 10000.0 ** (-jnp.arange(half_dim, dtype=f32) * 2.0 / HD)
    angles = positions.astype(f32)[:, None] * inverse[None, :]
    return jnp.cos(angles), jnp.sin(angles)


def norm_factor(values):
    return lax.rsqrt(jnp.mean(values * values, axis=-1, keepdims=True) + epsilon)


def norm_back(incoming, inputs, factor, gain):
    weighted = incoming * gain
    gain_grad = jnp.sum(incoming * (inputs * factor), axis=0)
    input_grad = weighted * factor - inputs * (factor * factor * factor) * jnp.mean(
        weighted * inputs, axis=-1, keepdims=True
    )
    return (gain_grad, input_grad)


def dot(one, two):
    return jnp.dot(one, two, preferred_element_type=f32)


def dot_last(one, two):
    return lax.dot_general(one, two, contract_last, preferred_element_type=f32)


def dot_first(one, two):
    return lax.dot_general(one, two, contract_first, preferred_element_type=f32)


def on_device(
    hidden_in, norm_attn, qkv_weight, out_weight, norm_ffn, gate_up_weight, down_weight, cotangent
):
    n = lax.axis_size("fsdp")
    me = lax.axis_index("fsdp")
    chips, chip, core = n // 2, me // 2, me % 2
    order = piece_order()
    evens = order[:chips]
    near, rest = evens[1:3], evens[3:]
    width = hidden_in.shape[2]
    rows = hidden_in.shape[0] * hidden_in.shape[1]
    q_width = HEADS * HD
    kv_width = KVH * HD
    share = FF // n
    chip_share = 2 * share
    block = width // n
    half = block // 2
    seq_at = lax.axis_index("seq")
    rank = {k: i for i, k in enumerate(order)}
    to_table = (me ^ jnp.array(order, jnp.int32)).astype(jnp.int32)
    at_table = jnp.array([rank[k] for k in range(n)], jnp.int32)[
        me ^ jnp.arange(n, dtype=jnp.int32)
    ]
    odd_table, even_table = to_table[chips:], to_table[:chips]
    assisted = lax.axis_size("seq") % 2 == 0
    part_at = seq_at % 2 if assisted else jnp.zeros_like(seq_at)

    live = {}

    def fence(**more):
        live.update(more)
        new = lax.optimization_barrier(live)
        live.clear()
        live.update(new)

    def two_hops(pieces):
        if len(rest) != 1:
            return {k: send(pieces[0], k) for k in rest}
        a, b = near
        size = pieces[0].shape[0] // 2
        lower, upper = send(pieces[b][:size], a), send(pieces[a][size:], b)
        return {rest[0]: (lower, upper)}

    def whole_piece(x):
        return jnp.concatenate(x, 0) if isinstance(x, tuple) else x

    def my_columns(k, at):
        cols = chip ^ (k // 2)
        spots = jnp.stack([cols, cols + chips]).astype(jnp.int32)
        if at is None:
            return pick(live["gate_up"], spots, chip_share)
        if chip_share % 128:
            part = pick(live["gate_up"], spots, chip_share)
            return lax.dynamic_slice_in_dim(part, at * half, half, 0)
        return pick(live["gate_up"], spots, chip_share, rows_at=(at, half))

    def other_half(k, first):
        return neighbour(first) if assisted else send(live["others"][k], k)

    full_qkv = lax.all_gather(qkv_weight, "fsdp", axis=0, tiled=True)
    fence(
        gains=gather_small(jnp.stack([norm_attn, norm_ffn])),
        hidden=hidden_in.reshape(rows, width),
        grad=cotangent.reshape(rows, width),
        gate_up=gate_up_weight,
        down=down_weight,
        out=out_weight,
    )

    firsts = {k: send(my_columns(k, part_at), k) for k in near}
    fence(
        firsts=firsts,
        others={} if assisted else {k: my_columns(k, 1 - part_at) for k in evens[1:]},
        own=my_columns(0, None),
        d_other=send(live["down"], 1),
    )
    inputs = live["hidden"].astype(f32)
    factor_one = norm_factor(inputs)
    gains = live["gains"].astype(f32)
    normed_one = (inputs * factor_one * gains[:1]).astype(bf16)
    fence(
        seconds={k: other_half(k, live["firsts"][k]) for k in near},
        mine={k: my_columns(k, part_at) for k in rest},
        qkv=full_qkv,
        normed_one=normed_one,
        normed_one_x=pick(normed_one, to_table, block),
    )
    del live["gate_up"]

    normed_one = live.pop("normed_one")
    joined = dot(normed_one, live["qkv"][:, q_width:])
    positions = seq_at * rows + jnp.arange(rows, dtype=jnp.int32)
    cosine, sine = angle_tables(positions)
    cos_wide, sin_wide = jnp.tile(cosine, (1, 2 * KVH)), jnp.tile(sine, (1, 2 * KVH))
    cos_t, sin_t = cosine.T, sine.T
    keys_values = jnp.concatenate(
        [turn(joined[:, :kv_width], cos_wide, sin_wide, 1), joined[:, kv_width:].astype(bf16)], 1
    )
    all_kv = lax.all_gather(keys_values, "seq", axis=0, tiled=True)
    joined = dot(normed_one, live["qkv"][:, :q_width])
    outs = {0: live.pop("out")}
    outs |= {k: send(outs[0], k) for k in near}
    firsts, seconds = live.pop("firsts"), live.pop("seconds")
    w_own = jnp.concatenate(sum([[firsts[k], seconds[k]] for k in near], [live.pop("own")]), 0)
    firsts = {k: send(x, k) for k, x in live.pop("mine").items()}
    fence(w_own=w_own, joined=joined, kv=all_kv, outs=outs, firsts=firsts)

    outs = live.pop("outs")
    outs |= two_hops(outs)
    firsts = live.pop("firsts")
    seconds = {k: other_half(k, firsts[k]) for k in rest}
    info = jnp.concatenate([(seq_at * rows).reshape(1), at_table]).astype(jnp.int32)
    attended, lse = attend(info, live["joined"], live["kv"], cos_t, sin_t)
    fence(
        firsts=firsts,
        seconds=seconds,
        outs=outs,
        attended=attended,
        lse=lse,
        w_other=send(live["w_own"], 1),
    )

    outs, firsts, seconds = live.pop("outs"), live.pop("firsts"), live.pop("seconds")
    out_even = jnp.concatenate([whole_piece(outs[k]) for k in evens], 0)
    out_odd = send(out_even, 1)
    grads = {0: live["grad"]}
    grads |= {k: send(grads[0], k) for k in near}
    w_rest = sum([[firsts[k], seconds[k]] for k in rest], [])
    w_rest = jnp.concatenate(w_rest or [live["w_own"]], 0)
    middle = dot(live["attended"][:, : q_width // 2], out_even)
    middle = live["hidden"].astype(f32) + (
        middle + dot(live["attended"][:, q_width // 2 :], out_odd)
    )
    factor_two = norm_factor(middle)
    gain_two = live["gains"][1:].astype(f32)
    normed_two = (middle * factor_two * gain_two).astype(bf16)
    fence(
        w_rest=w_rest,
        w_rest_other=send(w_rest, 1),
        out_even=out_even,
        out_odd=out_odd,
        grads=grads,
        middle=middle,
        tokens={0: normed_two},
    )

    ffn_info = jnp.stack([me, part_at, core, 1 - core]).astype(jnp.int32)

    def ffn_of(group):
        names = ("mixed", "both", "back", "parts")
        weights = [live[k] for k in ("w_own", "w_rest", "w_other", "w_rest_other")]
        results = ffn(
            ffn_info,
            [whole_piece(live["tokens"][k]) for k in group],
            [whole_piece(live["grads"][k]) for k in group],
            weights,
            live["down"],
            live["d_other"],
        )
        for name, new in zip(names, results, strict=True):
            live[name] = live.get(name, {}) | dict(zip(group, new, strict=True))

    new = {k: send(live["tokens"][0], k) for k in near}
    ffn_of([0])
    live["tokens"] |= new
    fence()
    far_tokens, far_grads = two_hops(live["tokens"]), two_hops(live["grads"])
    ffn_of(near)
    live["tokens"] |= far_tokens
    live["grads"] |= far_grads
    fence()
    new = {k: send(live["back"][k], k) for k in near}
    if rest:
        ffn_of(rest)
    fence(returned=new)

    live["returned"] |= {k: send(live["back"][k], k) for k in rest}

    def each(name):
        return [whole_piece(live[name][k]) for k in evens]

    theirs = down_grad(ffn_info, 3, each("mixed"), each("grads"))
    gots = up_grad(after(odd_table, theirs), each("tokens"), each("both"))
    got = send(theirs, 1)
    grad_down = down_grad(after(ffn_info, gots), 2, each("mixed"), each("grads"), got)
    fence(gots=gots, zd=grad_down[: share // 2], ze=grad_down[share // 2 :])

    line_step(live, new="d")
    gots = send(live.pop("gots"), 1)
    grad_normed_two = live["back"][0].astype(f32)
    for k in evens[1:]:
        grad_normed_two = grad_normed_two + live["returned"][k].astype(f32)
    middle = live["middle"]
    factor_two = norm_factor(middle)
    gain_two = live["gains"][1:].astype(f32)
    grad_gain_two, grad_norm_two = norm_back(grad_normed_two, middle, factor_two, gain_two)
    grad_middle = live["grad"].astype(f32) + grad_norm_two
    grad_branch = grad_middle.astype(bf16)
    grad_attended = jnp.concatenate(
        [dot_last(grad_branch, live[k]).astype(bf16) for k in ("out_even", "out_odd")], 1
    )
    parts = up_grad(even_table, each("tokens"), each("both"), gots)
    for k in ("tokens", "grads", "both", "mixed", "back", "returned", "d_other"):
        del live[k]
    for k in ("w_own", "w_rest", "w_other", "w_rest_other"):
        del live[k]
    del live["out_even"], live["out_odd"], live["down"], live["grad"]
    fence(
        ups=dict(zip(evens, parts, strict=True)),
        grad_gain_two=grad_gain_two,
        grad_middle=grad_middle,
        grad_branch=grad_branch,
        grad_attended=grad_attended,
    )

    names = [str(k) for k in evens]

    def blocks(whole, got):
        return {
            k: added(whole[i * block : (i + 1) * block], got[i * block : (i + 1) * block])
            for i, k in enumerate(evens)
        }

    def far_sends(parts):
        if len(rest) != 1:
            return [send(parts[k], k) for k in rest]
        far = parts[rest[0]]
        size = far.shape[0] // 2
        return [send(far[:size], near[0]), send(far[size:], near[1])]

    def near_sends(parts, got):
        if len(rest) != 1:
            return [send(parts[k], k) for k in near]
        size = parts[0].shape[0] // 2
        lower, upper = got
        one, two = parts[near[0]], parts[near[1]]
        one = jnp.concatenate([one[:size], added(one[size:], upper)], 0)
        two = jnp.concatenate([added(two[:size], lower), two[size:]], 0)
        return [send(one, near[0]), send(two, near[1])]

    def total_of(parts, *got):
        total = parts[0].astype(f32)
        for x in sum([g for g in got if g[0].shape == parts[0].shape], []):
            total = total + x.astype(f32)
        return total

    line_step(live, new="e", cross="d")
    sent = {k: send(live["ups"][k], k) for k in near}
    grad_queries, kv_parts = attend_back(
        info,
        live["joined"],
        live["kv"],
        cos_t,
        sin_t,
        live["grad_attended"],
        live["attended"],
        live["lse"],
    )
    fence(sent=sent, grad_queries=grad_queries, kv_parts=kv_parts)
    for k in ("grad_attended", "joined", "kv", "lse"):
        del live[k]

    ups = live.pop("ups")
    live["z0"] = ups[0]
    for k, x in live.pop("sent").items():
        live[f"z{k}"] = x
    line_step(live, new=names[0], cross="e", out="d")
    sent = {k: send(ups[k], k) for k in rest}
    kv_sums = lax.psum_scatter(live.pop("kv_parts"), "seq", scatter_dimension=0, tiled=True)
    kv_sums = kv_sums.reshape(rows, KVH, 2, HD).transpose(0, 2, 1, 3).reshape(rows, 2 * kv_width)
    grad_joined = jnp.concatenate(
        [
            live.pop("grad_queries"),
            turn(kv_sums[:, :kv_width], cos_wide, sin_wide, -1),
            kv_sums[:, kv_width:],
        ],
        1,
    )
    normed_one_x = live.pop("normed_one_x")
    theirs = dot_first(normed_one_x[:, width // 2 :], grad_joined).astype(bf16)
    attended = pick(live.pop("attended"), at_table, block)
    grad_out = dot_first(attended, live.pop("grad_branch")).astype(bf16)
    fence(
        sent=sent,
        grad_out=grad_out,
        grad_joined=grad_joined,
        normed_one_x=normed_one_x,
        theirs=theirs,
    )

    for k, x in live.pop("sent").items():
        live[f"z{k}"] = x
    line_step(live, new=names[1], cross=names[0], out="e")
    out_total = lax.psum_scatter(live.pop("grad_out"), "fsdp", scatter_dimension=0, tiled=True)
    mine = dot_first(live.pop("normed_one_x")[:, : width // 2], live["grad_joined"])
    fence(got_qkv=send(live.pop("theirs"), 1), mine=mine.astype(bf16))

    gate_up_sums = blank((block, 2 * FF), f32)
    outer = is_outer()

    def summed(k):
        return jnp.where(outer, live.pop("o" + k), live.pop("t" + k)).astype(f32)

    def placed_in(buffer, k):
        cols = chip ^ (k // 2)
        spots = jnp.stack([cols, cols + chips])
        return place(buffer, (live.pop(f"o{k}"), live.pop(f"t{k}")), outer, spots, chip_share)

    line_step(live, new=names[2] if chips > 2 else None, cross=names[1], out=names[0])
    parts_qkv = blocks(live.pop("mine"), live.pop("got_qkv"))
    down_sums = jnp.concatenate([summed("d"), summed("e")], 0)
    fence(parts_qkv=parts_qkv, far_qkv=far_sends(parts_qkv), down_sums=down_sums)

    line_step(live, new=names[3] if chips > 3 else None, cross=names[2], out=names[1])
    for k in evens[4:]:
        line_step(live, new=str(k))
    gate_up_sums = placed_in(gate_up_sums, 0)
    inputs = live["hidden"].astype(f32)
    factor_one = norm_factor(inputs)
    grad_normed_one = dot_last(live.pop("grad_joined"), live.pop("qkv"))
    grad_gain_one, grad_norm_one = norm_back(
        grad_normed_one, inputs, factor_one, live["gains"][:1].astype(f32)
    )
    grad_input = (live["grad_middle"] + grad_norm_one).astype(bf16)
    fence(
        near_qkv=near_sends(live["parts_qkv"], live["far_qkv"]),
        zout=out_total,
        sums=gate_up_sums,
        grad_input=grad_input,
        grad_gains=jnp.stack([grad_gain_one, live.pop("grad_gain_two")]),
    )

    line_step(live, new="out", cross=names[3], out=names[2])
    gate_up_sums = placed_in(live.pop("sums"), evens[1])
    total = total_of(live.pop("parts_qkv"), live.pop("far_qkv"), live.pop("near_qkv")).astype(bf16)
    fence(far=far_sends(live["parts"]), sums=gate_up_sums, zq=total[:half], zr=total[half:])

    line_step(live, new="q", cross="out", out=names[3])
    gate_up_sums = placed_in(live.pop("sums"), evens[2])
    fence(near=near_sends(live["parts"], live["far"]), sums=gate_up_sums)

    line_step(live, new="r", cross="q", out="out")
    gate_up_sums = live.pop("sums")
    for k in evens[3:]:
        gate_up_sums = placed_in(gate_up_sums, k)
    grad_gains = small_sum(live.pop("grad_gains"), "fsdp")
    out = total_of(live.pop("parts"), live.pop("far"), live.pop("near"))
    out = (live["middle"] + out).astype(bf16)
    fence(sums=gate_up_sums, grad_gains=grad_gains, out_final=out)

    line_step(live, cross="r", out="q")
    fence(out_sums=summed("out"))

    line_step(live, out="r")
    grad_gains = small_sum(live.pop("grad_gains"), "seq")
    qkv_sums = jnp.concatenate([summed("q"), summed("r")], 0)
    grad_gains = lax.dynamic_slice_in_dim(grad_gains, me * block, block, 1)
    return (
        live["out_final"].reshape(hidden_in.shape),
        live["grad_input"].reshape(hidden_in.shape),
        grad_gains[0],
        qkv_sums,
        live["out_sums"],
        grad_gains[1],
        live["sums"],
        live["down_sums"],
    )


def solution(mesh):
    placed = (
        P("fsdp", "seq", None),
        P("fsdp"),
        P("fsdp", None),
        P("fsdp", None),
        P("fsdp"),
        P("fsdp", None),
        P("fsdp", None),
        P("fsdp", "seq", None),
    )
    return jax.shard_map(
        on_device,
        mesh=mesh,
        in_specs=placed,
        out_specs=(
            P("fsdp", "seq", None),
            P("fsdp", "seq", None),
            P("fsdp"),
            P("fsdp", None),
            P("fsdp", None),
            P("fsdp"),
            P("fsdp", None),
            P("fsdp", None),
        ),
        check_vma=False,
    )
```

```python
import functools

import jax
import jax.numpy as jnp
from jax import lax
from jax.experimental import pallas as pl
from jax.experimental.pallas import tpu as pltpu
from jax.sharding import PartitionSpec as P

HEADS = 32
KVH = 4
HD = 64
FF = 5632

epsilon = 1e-05
masked_value = -1e30
log2e = 1.4426950408889634
contract_last = (((1,), (1,)), ((), ()))
contract_first = (((0,), (0,)), ((), ()))
bf16 = jnp.bfloat16
f32 = jnp.float32


def send(x, k):
    n = lax.axis_size("fsdp")
    return lax.ppermute(x, "fsdp", [(i, i ^ k) for i in range(n)])


def chip_bits():
    n = lax.axis_size("fsdp")
    return [1 << i for i in range(1, n.bit_length() - 1)]


def piece_order():
    n = lax.axis_size("fsdp")
    return list(range(0, n, 2)) + list(range(1, n, 2))


def gather_small(x):
    n, me = lax.axis_size("fsdp"), lax.axis_index("fsdp")
    for k in (1 << i for i in range(n.bit_length() - 1)):
        got = send(x, k)
        x = jnp.where(
            me & k == 0, jnp.concatenate([x, got], 1), jnp.concatenate([got, x], 1)
        )
    return x


def neighbour(x):
    n = lax.axis_size("seq")
    return lax.ppermute(x, "seq", [(i, i ^ 1) for i in range(n)])


def after(x, *others):
    return lax.optimization_barrier((x, *others))[0]


def added(one, two):
    return (one.astype(f32) + two.astype(f32)).astype(bf16)


def line_sum(x):
    n = lax.axis_size("seq")
    if n == 1:
        return x
    if n % 2:
        return lax.psum(x.astype(f32), "seq").astype(bf16)
    me = lax.axis_index("seq")
    mid = n // 2
    total = x
    for i in range(mid - 1):
        total = added(total, lax.ppermute(total, "seq", [(i, i + 1), (n - 1 - i, n - 2 - i)]))
    total = added(total, lax.ppermute(total, "seq", [(mid - 1, mid), (mid, mid - 1)]))
    for i in range(mid - 1):
        got = lax.ppermute(total, "seq", [(mid - 1 - i, mid - 2 - i), (mid + i, mid + 1 + i)])
        taken = (me == mid - 2 - i) | (me == mid + 1 + i)
        total = jnp.where(taken, got, total)
    return total


def line_step(live, new=None, cross=None, out=None):
    if lax.axis_size("seq") != 4:
        if new is not None:
            live["o" + new] = live["t" + new] = line_sum(live["z" + new])
        return
    inward, outward, across = [(0, 1), (3, 2)], [(1, 0), (2, 3)], [(1, 2), (2, 1)]
    x = None if new is None else live["z" + new]
    part = None
    if cross is not None:
        part = live["p" + cross] = added(live["z" + cross], live["i" + cross])
        live["x" + cross] = lax.ppermute(part, "seq", across)
        others = {k: v for k, v in live.items() if not k.endswith(cross)}
        live.update(lax.optimization_barrier((others, part))[0])
    if x is not None:
        live["i" + new] = lax.ppermute(x, "seq", inward)
    if out is not None:
        total = live["t" + out] = added(live["p" + out], live["x" + out])
        live["o" + out] = lax.ppermute(total, "seq", outward)


def is_outer():
    me, n = lax.axis_index("seq"), lax.axis_size("seq")
    return (me == 0) | (me == n - 1)


def small_sum(x, axis):
    n = lax.axis_size(axis)
    if n & (n - 1):
        return lax.psum(x, axis)
    for k in (1 << i for i in range(n.bit_length() - 1)):
        x = x + lax.ppermute(x, axis, [(i, i ^ k) for i in range(n)])
    return x


def copy_kernel(table_ref, x_ref, o_ref):
    o_ref[...] = x_ref[...].astype(o_ref.dtype)


def pick(x, table, size, dtype=None, rows_at=None):
    rows, count = x.shape[0], table.shape[0]
    if size % 128:
        return jnp.concatenate(
            [lax.dynamic_slice_in_dim(x, table[i] * size, size, 1) for i in range(count)], 1
        ).astype(dtype or x.dtype)
    if rows_at is not None:
        rows = rows_at[1]
    row = jnp.zeros((), jnp.int32) if rows_at is None else rows_at[0]
    table = jnp.concatenate([table, row.reshape(1)]).astype(jnp.int32)
    return pl.pallas_call(
        copy_kernel,
        out_shape=jax.ShapeDtypeStruct((rows, count * size), dtype or x.dtype),
        grid_spec=pltpu.PrefetchScalarGridSpec(
            num_scalar_prefetch=1,
            grid=(count,),
            in_specs=[pl.BlockSpec((rows, size), lambda i, table: (table[count], table[i]))],
            out_specs=pl.BlockSpec((rows, size), lambda i, table: (0, i)),
        ),
        cost_estimate=pl.CostEstimate(
            flops=0, transcendentals=0, bytes_accessed=rows * count * size * 4
        ),
    )(table, x)


def blank_kernel(o_ref):
    pass


def blank(shape, dtype):
    return pl.pallas_call(
        blank_kernel,
        out_shape=jax.ShapeDtypeStruct(shape, dtype),
        out_specs=pl.BlockSpec(memory_space=pl.ANY),
    )()


def turn_kernel(sign, x_ref, cos_ref, sin_ref, o_ref):
    x = x_ref[...].astype(f32)
    width = x.shape[1]
    lane = lax.broadcasted_iota(jnp.int32, x.shape, 1)
    first = (lane % HD) < HD // 2
    other = jnp.where(
        first, -pltpu.roll(x, width - HD // 2, 1), pltpu.roll(x, HD // 2, 1)
    )
    o_ref[...] = (x * cos_ref[...] + sign * other * sin_ref[...]).astype(o_ref.dtype)


def turn(x, cos_wide, sin_wide, sign):
    return pl.pallas_call(
        functools.partial(turn_kernel, float(sign)),
        out_shape=jax.ShapeDtypeStruct(x.shape, bf16),
    )(x, cos_wide, sin_wide)


def place_kernel(info_ref, buffer_ref, got_ref, total_ref, o_ref):
    o_ref[...] = jnp.where(info_ref[0] == 1, got_ref[...], total_ref[...]).astype(f32)


def place(buffer, pair, outer, where, size):
    got, total = pair
    rows = got.shape[0]
    if size % 128:
        picked = jnp.where(outer, got, total).astype(f32)
        for i in range(2):
            buffer = lax.dynamic_update_slice_in_dim(
                buffer, picked[:, i * size : (i + 1) * size], where[i] * size, 1
            )
        return buffer
    info = jnp.concatenate([outer.astype(jnp.int32).reshape(1), where.astype(jnp.int32)])
    own = pl.BlockSpec((rows, size), lambda i, info: (0, i))
    return pl.pallas_call(
        place_kernel,
        out_shape=jax.ShapeDtypeStruct(buffer.shape, f32),
        grid_spec=pltpu.PrefetchScalarGridSpec(
            num_scalar_prefetch=1,
            grid=(2,),
            in_specs=[pl.BlockSpec(memory_space=pl.ANY), own, own],
            out_specs=pl.BlockSpec((rows, size), lambda i, info: (0, info[1 + i])),
        ),
        input_output_aliases={1: 0},
    )(info, buffer, got, total)


def mask_bias(start, length, rows):
    key_place = lax.broadcasted_iota(jnp.int32, (length, rows), 0)
    query_place = start + lax.broadcasted_iota(jnp.int32, (length, rows), 1)
    return jnp.where(key_place <= query_place, 0.0, masked_value).astype(f32)


def turned_t(x, cos, sin):
    one, two = x[: HD // 2], x[HD // 2 :]
    return jnp.concatenate([one * cos - two * sin, two * cos + one * sin], 0)


def kv_head(ref, index):
    both = ref[...]
    return jnp.where(index % 2 == 0, both[:, :HD], both[:, HD:])


def attend_kernel(
    heads, per_kv, info_ref, q_ref, k_ref, v_ref, cos_ref, sin_ref, o_ref, lse_ref, bias_ref
):
    length, rows = k_ref.shape[0], q_ref.shape[0]
    scale2 = HD**-0.5 * log2e
    step = pl.program_id(0)

    @pl.when(step == 0)
    def _():
        bias_ref[...] = mask_bias(info_ref[0], length, rows)

    kv = step * heads // per_kv
    keys = kv_head(k_ref, kv)
    values_t = kv_head(v_ref, kv).astype(f32).T.astype(bf16)
    q_t = q_ref[...].T
    cos, sin = cos_ref[...], sin_ref[...]
    q_all = [
        turned_t(q_t[h * HD : (h + 1) * HD], cos, sin).astype(bf16) for h in range(heads)
    ]

    key_size = jnp.max(jnp.sum(jnp.square(keys.astype(f32)), axis=1))
    query_size = jnp.max(
        sum(
            jnp.sum(jnp.square(q.astype(f32)), axis=0, keepdims=True) for q in q_all
        )
    )
    small = key_size * query_size * scale2**2 < 80.0**2

    def run(shift):
        outs = []
        for h in range(heads):
            scores = jnp.dot(keys, q_all[h], preferred_element_type=f32) + bias_ref[...]
            if shift:
                top = jnp.max(scores, axis=0, keepdims=True)
                weights = jnp.exp2((scores - top) * scale2)
            else:
                weights = jnp.exp2(scores * scale2)
            total = jnp.sum(weights, axis=0, keepdims=True)
            out = jnp.dot(values_t, weights.astype(bf16), preferred_element_type=f32)
            outs.append(out * (1.0 / total))
            lse = jnp.log2(total)
            lse_ref[0, h : h + 1, :] = lse + top * scale2 if shift else lse
        o_ref[...] = jnp.concatenate(outs, 0).T.astype(bf16)

    pl.when(small)(lambda: run(False))
    pl.when(jnp.logical_not(small))(lambda: run(True))


def attend_specs(n, rows, length):
    heads = HEADS // n
    per_kv = HEADS // KVH
    kv_at = lambda i: (i * heads // per_kv) // 2
    return dict(
        plain=pl.BlockSpec((rows, heads * HD), lambda i, info: (0, i)),
        ordered=pl.BlockSpec((rows, heads * HD), lambda i, info: (0, info[1 + i])),
        keys=pl.BlockSpec((length, 2 * HD), lambda i, info: (0, kv_at(i))),
        values=pl.BlockSpec((length, 2 * HD), lambda i, info: (0, KVH // 2 + kv_at(i))),
        table=pl.BlockSpec((HD // 2, rows), lambda i, info: (0, 0)),
        lse=pl.BlockSpec((1, heads, rows), lambda i, info: (i, 0, 0)),
    )


def attend(info, joined, all_kv, cos_t, sin_t):
    n = lax.axis_size("fsdp")
    rows, length = joined.shape[0], all_kv.shape[0]
    heads = HEADS // n
    spec = attend_specs(n, rows, length)
    return pl.pallas_call(
        functools.partial(attend_kernel, heads, HEADS // KVH),
        out_shape=(
            jax.ShapeDtypeStruct((rows, HEADS * HD), bf16),
            jax.ShapeDtypeStruct((n, heads, rows), f32),
        ),
        grid_spec=pltpu.PrefetchScalarGridSpec(
            num_scalar_prefetch=1,
            grid=(n,),
            in_specs=[spec[k] for k in ("plain", "keys", "values", "table", "table")],
            out_specs=(spec["ordered"], spec["lse"]),
            scratch_shapes=[pltpu.VMEM((length, rows), f32)],
        ),
        compiler_params=pltpu.CompilerParams(vmem_limit_bytes=40 << 20),
        cost_estimate=pl.CostEstimate(
            flops=4 * HEADS * rows * length * HD * 4,
            bytes_accessed=6 * rows * HEADS * HD,
            transcendentals=HEADS * rows * length,
        ),
    )(info, joined, all_kv, all_kv, cos_t, sin_t)


def attend_back_kernel(
    heads, per_kv, info_ref, q_ref, k_ref, v_ref, g_ref, o_ref, cos_ref, sin_ref, lse_ref,
    dq_ref, dkv_ref, bias_ref, dk_ref, dv_ref,
):
    length, rows = k_ref.shape[0], q_ref.shape[0]
    scale = HD**-0.5
    scale2 = scale * log2e
    step = pl.program_id(0)
    steps = per_kv // heads

    @pl.when(step == 0)
    def _():
        bias_ref[...] = mask_bias(info_ref[0], length, rows)

    @pl.when(step % steps == 0)
    def _():
        dk_ref[...] = jnp.zeros_like(dk_ref)
        dv_ref[...] = jnp.zeros_like(dv_ref)

    kv = step * heads // per_kv
    keys, values = kv_head(k_ref, kv), kv_head(v_ref, kv)
    keys_t = keys.astype(f32).T.astype(bf16)
    q_t = q_ref[...].T
    g_t = g_ref[...].astype(f32).T
    deltas = g_t * o_ref[...].astype(f32).T
    g_t = g_t.astype(bf16)
    cos, sin = cos_ref[...], sin_ref[...]
    outs = []
    dk, dv = dk_ref[...], dv_ref[...]
    for h in range(heads):
        q_h = turned_t(q_t[h * HD : (h + 1) * HD], cos, sin).astype(bf16)
        g_h = g_t[h * HD : (h + 1) * HD]
        scores = jnp.dot(keys, q_h, preferred_element_type=f32) + bias_ref[...]
        weights = jnp.exp2(scores * scale2 - lse_ref[0, h : h + 1, :])
        grad_p = jnp.dot(values, g_h, preferred_element_type=f32)
        delta = jnp.sum(deltas[h * HD : (h + 1) * HD], axis=0, keepdims=True)
        grad_s = (weights * (grad_p - delta)).astype(bf16)
        grad_q = jnp.dot(keys_t, grad_s, preferred_element_type=f32) * scale
        outs.append(turned_t(grad_q.astype(bf16).astype(f32), cos, -sin))
        dk += lax.dot_general(grad_s, q_h, contract_last, preferred_element_type=f32)
        dv += lax.dot_general(
            weights.astype(bf16), g_h, contract_last, preferred_element_type=f32
        )
    dk_ref[...], dv_ref[...] = dk, dv
    dq_ref[...] = jnp.concatenate(outs, 0).T.astype(bf16)

    @pl.when(step % steps == steps - 1)
    def _():
        dkv_ref[...] = jnp.concatenate([dk * scale, dv], 1).astype(bf16)


def attend_back(info, joined, all_kv, cos_t, sin_t, grads, outs, lse):
    n = lax.axis_size("fsdp")
    rows, length = joined.shape[0], all_kv.shape[0]
    heads, per_kv = HEADS // n, HEADS // KVH
    spec = attend_specs(n, rows, length)
    names = ("plain", "keys", "values", "ordered", "ordered", "table", "table", "lse")
    return pl.pallas_call(
        functools.partial(attend_back_kernel, heads, per_kv),
        out_shape=(
            jax.ShapeDtypeStruct((rows, HEADS * HD), bf16),
            jax.ShapeDtypeStruct((length, 2 * KVH * HD), bf16),
        ),
        grid_spec=pltpu.PrefetchScalarGridSpec(
            num_scalar_prefetch=1,
            grid=(n,),
            in_specs=[spec[k] for k in names],
            out_specs=(
                spec["plain"],
                pl.BlockSpec((length, 2 * HD), lambda i, info: (0, i * heads // per_kv)),
            ),
            scratch_shapes=[
                pltpu.VMEM((length, rows), f32),
                pltpu.VMEM((length, HD), f32),
                pltpu.VMEM((length, HD), f32),
            ],
        ),
        compiler_params=pltpu.CompilerParams(vmem_limit_bytes=48 << 20),
        cost_estimate=pl.CostEstimate(
            flops=10 * HEADS * rows * length * HD * 4,
            bytes_accessed=8 * rows * HEADS * HD,
            transcendentals=HEADS * rows * length,
        ),
    )(info, joined, all_kv, all_kv, grads, outs, cos_t, sin_t, lse)


def column_chunks(total, size=256):
    return [(c, min(size, total - c)) for c in range(0, total, size)]


def part_pieces(n):
    evens = list(range(0, n, 2))
    return evens[:3], evens[3:], [k | 1 for k in evens[:3]], [k | 1 for k in evens[3:]]


def ffn_kernel(n, count, info_ref, *refs):
    x_refs, g_refs, refs = refs[:count], refs[count : 2 * count], refs[2 * count :]
    parts, (d_own, d_other), refs = refs[:4], refs[4:6], refs[6:]
    outs, (x, g, w, d, both, mid, sems) = refs[: 4 * count], refs[4 * count :]
    mixed_refs, both_refs = outs[:count], outs[count : 2 * count]
    back_refs, out_refs = outs[2 * count : 3 * count], outs[3 * count :]
    me, part = info_ref[0], info_ref[1]
    rows, width = x_refs[0].shape
    cols = d.shape[0]
    share = cols // 2
    block = width // n
    half = block // 2

    copies = []
    for source, ks in zip(parts, part_pieces(n), strict=True):
        for i, k in enumerate(ks):
            owner = (me ^ k) * block
            for j in range(2):
                at = owner if k < 2 else owner + (part if j == 0 else 1 - part) * half
                if k < 2:
                    at = at + j * half
                copies.append(
                    pltpu.make_async_copy(
                        source.at[pl.ds(i * block + j * half, half)],
                        w.at[pl.ds(pl.multiple_of(at, half), half)],
                        sems.at[len(copies)],
                    )
                )
    core = me % 2
    for source, at in ((d_own, core), (d_other, 1 - core)):
        copies.append(
            pltpu.make_async_copy(
                source, d.at[pl.ds(pl.multiple_of(at * share, share), share)], sems.at[len(copies)]
            )
        )
    for copy in copies:
        copy.start()
    for i in range(count):
        x[i * rows : (i + 1) * rows] = x_refs[i][...]
        g[i * rows : (i + 1) * rows] = g_refs[i][...]
    for copy in copies:
        copy.wait()

    def columns(at, size):
        gate_w, up_w = w[:, pl.ds(at, size)], w[:, pl.ds(cols + at, size)]
        gate = jnp.dot(x[...], gate_w, preferred_element_type=f32)
        up = jnp.dot(x[...], up_w, preferred_element_type=f32)
        grad = lax.dot_general(
            g[...], d[pl.ds(at, size)], contract_last, preferred_element_type=f32
        )
        sig = 1.0 / (1.0 + jnp.exp(-gate))
        act = gate * sig
        mid[:, pl.ds(at, size)] = (act * up).astype(bf16)
        both[:, pl.ds(at, size)] = (grad * up * (sig * (1.0 + gate * (1.0 - sig)))).astype(bf16)
        both[:, pl.ds(cols + at, size)] = (grad * act).astype(bf16)

    full = cols // 256
    pl.loop(0, full)(lambda c: columns(pl.multiple_of(c * 256, 256), 256))
    if cols % 256:
        columns(full * 256, cols % 256)
    for i in range(count):
        at = slice(i * rows, (i + 1) * rows)
        mixed_refs[i][...] = mid[at].astype(f32).T.astype(bf16)
        both_refs[i][...] = both[at]

    @pl.loop(0, width // 256)
    def _(t):
        at = pl.multiple_of(t * 256, 256)
        back = lax.dot_general(
            both[...], w[pl.ds(at, 256)], contract_last, preferred_element_type=f32
        ).astype(bf16)
        out = jnp.dot(mid[...], d[:, pl.ds(at, 256)], preferred_element_type=f32).astype(bf16)
        for i in range(count):
            back_refs[i][:, pl.ds(at, 256)] = back[i * rows : (i + 1) * rows]
            out_refs[i][:, pl.ds(at, 256)] = out[i * rows : (i + 1) * rows]


def ffn(info, xs, gs, parts, d_own, d_other):
    n = lax.axis_size("fsdp")
    count = len(xs)
    rows, width = xs[0].shape
    cols = 2 * d_own.shape[0]
    if cols % 128:
        return ffn_plain(info, xs, gs, parts, d_own, d_other)
    shapes = (
        [jax.ShapeDtypeStruct((cols, rows), bf16)] * count
        + [jax.ShapeDtypeStruct((rows, 2 * cols), bf16)] * count
        + [jax.ShapeDtypeStruct((rows, width), bf16)] * (2 * count)
    )
    vmem, hbm = pl.BlockSpec(memory_space=pltpu.VMEM), pl.BlockSpec(memory_space=pl.ANY)
    outs = pl.pallas_call(
        functools.partial(ffn_kernel, n, count),
        out_shape=shapes,
        in_specs=[pl.BlockSpec(memory_space=pltpu.SMEM)] + [vmem] * (2 * count) + [hbm] * 6,
        out_specs=[vmem] * (4 * count),
        scratch_shapes=[
            pltpu.VMEM((count * rows, width), bf16),
            pltpu.VMEM((count * rows, width), bf16),
            pltpu.VMEM((width, 2 * cols), bf16),
            pltpu.VMEM((cols, width), bf16),
            pltpu.VMEM((count * rows, 2 * cols), bf16),
            pltpu.VMEM((count * rows, cols), bf16),
            pltpu.SemaphoreType.DMA((2 * n + 2,)),
        ],
        compiler_params=pltpu.CompilerParams(vmem_limit_bytes=56 << 20),
        cost_estimate=pl.CostEstimate(
            flops=2 * count * rows * width * cols * 6,
            bytes_accessed=6 * width * cols,
            transcendentals=count * rows * cols,
        ),
    )(info, *xs, *gs, *parts, d_own, d_other)
    return [outs[i * count : (i + 1) * count] for i in range(4)]


def ffn_plain(info, xs, gs, parts, d_own, d_other):
    n = lax.axis_size("fsdp")
    me, part = info[0], info[1]
    width, share = xs[0].shape[1], d_own.shape[0]
    block, cols = width // n, 2 * share
    half = block // 2
    w = jnp.zeros((width, 2 * cols), bf16)
    for source, ks in zip(parts, part_pieces(n), strict=True):
        for i, k in enumerate(ks):
            for j in range(2):
                at = j if k < 2 else (part if j == 0 else 1 - part)
                rows = source[i * block + j * half : i * block + (j + 1) * half]
                w = lax.dynamic_update_slice_in_dim(w, rows, (me ^ k) * block + at * half, 0)
    d = jnp.where(
        me % 2 == 0, jnp.concatenate([d_own, d_other], 0), jnp.concatenate([d_other, d_own], 0)
    )
    mixed, both, back, out = [], [], [], []
    for x, g in zip(xs, gs, strict=True):
        gate, up = dot(x, w[:, :cols]), dot(x, w[:, cols:])
        sig = jax.nn.sigmoid(gate)
        act = gate * sig
        grad = dot_last(g, d)
        mid = (act * up).astype(bf16)
        two = jnp.concatenate(
            [grad * up * (sig * (1.0 + gate * (1.0 - sig))), grad * act], 1
        ).astype(bf16)
        mixed.append(mid.T)
        both.append(two)
        back.append(dot_last(two, w).astype(bf16))
        out.append(dot(mid, d).astype(bf16))
    return mixed, both, back, out


def down_grad_kernel(count, info_ref, *refs):
    lefts, rights, rest = refs[:count], refs[count : 2 * count], refs[2 * count :]
    total = sum(
        jnp.dot(one[...], two[...], preferred_element_type=f32)
        for one, two in zip(lefts, rights, strict=True)
    )
    if len(rest) == 2:
        total = total.astype(bf16).astype(f32) + rest[0][...].astype(f32)
    rest[-1][...] = total.astype(bf16)


def down_grad(info, at, mixed, gs, got=None):
    count = len(mixed)
    cols, rows = mixed[0].shape
    width = gs[0].shape[1]
    size = min(512, width)
    out = pl.BlockSpec((cols // 2, size), lambda i, info: (0, i))
    return pl.pallas_call(
        functools.partial(down_grad_kernel, count),
        out_shape=jax.ShapeDtypeStruct((cols // 2, width), bf16),
        grid_spec=pltpu.PrefetchScalarGridSpec(
            num_scalar_prefetch=1,
            grid=(width // size,),
            in_specs=[pl.BlockSpec((cols // 2, rows), lambda i, info: (info[at], 0))] * count
            + [pl.BlockSpec((rows, size), lambda i, info: (0, i))] * count
            + ([] if got is None else [out]),
            out_specs=out,
        ),
        compiler_params=pltpu.CompilerParams(vmem_limit_bytes=40 << 20),
        cost_estimate=pl.CostEstimate(
            flops=count * rows * width * cols,
            bytes_accessed=4 * width * cols,
            transcendentals=0,
        ),
    )(info, *mixed, *gs, *([] if got is None else [got]))


def up_grad_kernel(count, split, info_ref, *refs):
    lefts, rights, rest = refs[:count], refs[count : 2 * count], refs[2 * count :]
    total = sum(
        lax.dot_general(one[...], two[...], contract_first, preferred_element_type=f32)
        for one, two in zip(lefts, rights, strict=True)
    ).astype(bf16)
    if not split:
        rest[0][...] = total
        return
    total = (total.astype(f32) + rest[0][...].astype(f32)).astype(bf16)
    for i, out in enumerate(rest[1:]):

        @pl.when(pl.program_id(1) == i)
        def _(out=out):
            out[...] = total


def up_grad(table, xs, both, got=None):
    count, chips = len(xs), table.shape[0]
    rows, width = xs[0].shape
    cols = both[0].shape[1] // 2
    block = width // lax.axis_size("fsdp")
    if cols % 128 or block % 128:
        whole = sum(dot_first(one, two) for one, two in zip(xs, both, strict=True))
        outs = [
            lax.dynamic_slice_in_dim(whole, table[i] * block, block, 0).astype(bf16)
            for i in range(chips)
        ]
        if got is None:
            return jnp.concatenate(outs, 0)
        return [added(x, got[i * block : (i + 1) * block]) for i, x in enumerate(outs)]
    one = pl.BlockSpec((block, cols), lambda h, b, table: (b, h))
    outs = [
        pl.BlockSpec(
            (block, cols), lambda h, b, table, i=i: (0, jnp.where(b >= i, h, jnp.maximum(h - 1, 0)))
        )
        for i in range(chips)
    ]
    split = got is not None
    shape = jax.ShapeDtypeStruct((block, 2 * cols), bf16)
    return pl.pallas_call(
        functools.partial(up_grad_kernel, count, split),
        out_shape=[shape] * chips
        if split
        else jax.ShapeDtypeStruct((chips * block, 2 * cols), bf16),
        grid_spec=pltpu.PrefetchScalarGridSpec(
            num_scalar_prefetch=1,
            grid=(2, chips),
            in_specs=[pl.BlockSpec((rows, block), lambda h, b, table: (0, table[b]))] * count
            + [pl.BlockSpec((rows, cols), lambda h, b, table: (0, h))] * count
            + ([one] if split else []),
            out_specs=outs if split else one,
        ),
        compiler_params=pltpu.CompilerParams(vmem_limit_bytes=48 << 20),
        cost_estimate=pl.CostEstimate(
            flops=4 * count * rows * chips * block * cols,
            bytes_accessed=4 * chips * block * cols * 2,
            transcendentals=0,
        ),
    )(table, *xs, *both, *([got] if split else []))


def angle_tables(positions):
    half_dim = HD // 2
    inverse = 10000.0 ** (-jnp.arange(half_dim, dtype=f32) * 2.0 / HD)
    angles = positions.astype(f32)[:, None] * inverse[None, :]
    return jnp.cos(angles), jnp.sin(angles)


def norm_factor(values):
    return lax.rsqrt(jnp.mean(values * values, axis=-1, keepdims=True) + epsilon)


def norm_back(incoming, inputs, factor, gain):
    weighted = incoming * gain
    gain_grad = jnp.sum(incoming * (inputs * factor), axis=0)
    input_grad = weighted * factor - inputs * (factor * factor * factor) * jnp.mean(
        weighted * inputs, axis=-1, keepdims=True
    )
    return (gain_grad, input_grad)


def dot(one, two):
    return jnp.dot(one, two, preferred_element_type=f32)


def dot_last(one, two):
    return lax.dot_general(one, two, contract_last, preferred_element_type=f32)


def dot_first(one, two):
    return lax.dot_general(one, two, contract_first, preferred_element_type=f32)


def on_device(
    hidden_in, norm_attn, qkv_weight, out_weight, norm_ffn, gate_up_weight, down_weight, cotangent
):
    n = lax.axis_size("fsdp")
    me = lax.axis_index("fsdp")
    chips, chip, core = n // 2, me // 2, me % 2
    order = piece_order()
    evens = order[:chips]
    near, rest = evens[1:3], evens[3:]
    width = hidden_in.shape[2]
    rows = hidden_in.shape[0] * hidden_in.shape[1]
    q_width = HEADS * HD
    kv_width = KVH * HD
    share = FF // n
    chip_share = 2 * share
    block = width // n
    half = block // 2
    seq_at = lax.axis_index("seq")
    rank = {k: i for i, k in enumerate(order)}
    to_table = (me ^ jnp.array(order, jnp.int32)).astype(jnp.int32)
    at_table = jnp.array([rank[k] for k in range(n)], jnp.int32)[
        me ^ jnp.arange(n, dtype=jnp.int32)
    ]
    odd_table, even_table = to_table[chips:], to_table[:chips]
    assisted = lax.axis_size("seq") % 2 == 0
    part_at = seq_at % 2 if assisted else jnp.zeros_like(seq_at)

    live = {}

    def fence(**more):
        live.update(more)
        new = lax.optimization_barrier(live)
        live.clear()
        live.update(new)

    def two_hops(pieces):
        if len(rest) != 1:
            return {k: send(pieces[0], k) for k in rest}
        a, b = near
        size = pieces[0].shape[0] // 2
        lower, upper = send(pieces[b][:size], a), send(pieces[a][size:], b)
        return {rest[0]: (lower, upper)}

    def whole_piece(x):
        return jnp.concatenate(x, 0) if isinstance(x, tuple) else x

    def my_columns(k, at):
        cols = chip ^ (k // 2)
        spots = jnp.stack([cols, cols + chips]).astype(jnp.int32)
        if at is None:
            return pick(live["gate_up"], spots, chip_share)
        if chip_share % 128:
            part = pick(live["gate_up"], spots, chip_share)
            return lax.dynamic_slice_in_dim(part, at * half, half, 0)
        return pick(live["gate_up"], spots, chip_share, rows_at=(at, half))

    def other_half(k, first):
        return neighbour(first) if assisted else send(live["others"][k], k)

    full_qkv = lax.all_gather(qkv_weight, "fsdp", axis=0, tiled=True)
    fence(
        gains=gather_small(jnp.stack([norm_attn, norm_ffn])),
        hidden=hidden_in.reshape(rows, width),
        grad=cotangent.reshape(rows, width),
        gate_up=gate_up_weight,
        down=down_weight,
        out=out_weight,
    )

    firsts = {k: send(my_columns(k, part_at), k) for k in near}
    fence(
        firsts=firsts,
        others={} if assisted else {k: my_columns(k, 1 - part_at) for k in evens[1:]},
        own=my_columns(0, None),
        d_other=send(live["down"], 1),
    )
    inputs = live["hidden"].astype(f32)
    factor_one = norm_factor(inputs)
    gains = live["gains"].astype(f32)
    normed_one = (inputs * factor_one * gains[:1]).astype(bf16)
    fence(
        seconds={k: other_half(k, live["firsts"][k]) for k in near},
        mine={k: my_columns(k, part_at) for k in rest},
        qkv=full_qkv,
        normed_one=normed_one,
        normed_one_x=pick(normed_one, to_table, block),
    )
    del live["gate_up"]

    normed_one = live.pop("normed_one")
    joined = dot(normed_one, live["qkv"][:, q_width:])
    positions = seq_at * rows + jnp.arange(rows, dtype=jnp.int32)
    cosine, sine = angle_tables(positions)
    cos_wide, sin_wide = jnp.tile(cosine, (1, 2 * KVH)), jnp.tile(sine, (1, 2 * KVH))
    cos_t, sin_t = cosine.T, sine.T
    keys_values = jnp.concatenate(
        [turn(joined[:, :kv_width], cos_wide, sin_wide, 1), joined[:, kv_width:].astype(bf16)], 1
    )
    all_kv = lax.all_gather(keys_values, "seq", axis=0, tiled=True)
    joined = dot(normed_one, live["qkv"][:, :q_width])
    outs = {0: live.pop("out")}
    outs |= {k: send(outs[0], k) for k in near}
    firsts, seconds = live.pop("firsts"), live.pop("seconds")
    w_own = jnp.concatenate(sum([[firsts[k], seconds[k]] for k in near], [live.pop("own")]), 0)
    firsts = {k: send(x, k) for k, x in live.pop("mine").items()}
    fence(w_own=w_own, joined=joined, kv=all_kv, outs=outs, firsts=firsts)

    outs = live.pop("outs")
    outs |= two_hops(outs)
    firsts = live.pop("firsts")
    seconds = {k: other_half(k, firsts[k]) for k in rest}
    info = jnp.concatenate([(seq_at * rows).reshape(1), at_table]).astype(jnp.int32)
    attended, lse = attend(info, live["joined"], live["kv"], cos_t, sin_t)
    fence(
        firsts=firsts,
        seconds=seconds,
        outs=outs,
        attended=attended,
        lse=lse,
        w_other=send(live["w_own"], 1),
    )

    outs, firsts, seconds = live.pop("outs"), live.pop("firsts"), live.pop("seconds")
    out_even = jnp.concatenate([whole_piece(outs[k]) for k in evens], 0)
    out_odd = send(out_even, 1)
    grads = {0: live["grad"]}
    grads |= {k: send(grads[0], k) for k in near}
    w_rest = sum([[firsts[k], seconds[k]] for k in rest], [])
    w_rest = jnp.concatenate(w_rest or [live["w_own"]], 0)
    middle = dot(live["attended"][:, : q_width // 2], out_even)
    middle = live["hidden"].astype(f32) + (
        middle + dot(live["attended"][:, q_width // 2 :], out_odd)
    )
    factor_two = norm_factor(middle)
    gain_two = live["gains"][1:].astype(f32)
    normed_two = (middle * factor_two * gain_two).astype(bf16)
    fence(
        w_rest=w_rest,
        w_rest_other=send(w_rest, 1),
        out_even=out_even,
        out_odd=out_odd,
        grads=grads,
        middle=middle,
        tokens={0: normed_two},
    )

    ffn_info = jnp.stack([me, part_at, core, 1 - core]).astype(jnp.int32)

    def ffn_of(group):
        names = ("mixed", "both", "back", "parts")
        weights = [live[k] for k in ("w_own", "w_rest", "w_other", "w_rest_other")]
        results = ffn(
            ffn_info,
            [whole_piece(live["tokens"][k]) for k in group],
            [whole_piece(live["grads"][k]) for k in group],
            weights,
            live["down"],
            live["d_other"],
        )
        for name, new in zip(names, results, strict=True):
            live[name] = live.get(name, {}) | dict(zip(group, new, strict=True))

    new = {k: send(live["tokens"][0], k) for k in near}
    ffn_of([0])
    live["tokens"] |= new
    fence()
    far_tokens, far_grads = two_hops(live["tokens"]), two_hops(live["grads"])
    ffn_of(near)
    live["tokens"] |= far_tokens
    live["grads"] |= far_grads
    fence()
    new = {k: send(live["back"][k], k) for k in near}
    if rest:
        ffn_of(rest)
    fence(returned=new)

    live["returned"] |= {k: send(live["back"][k], k) for k in rest}

    def each(name):
        return [whole_piece(live[name][k]) for k in evens]

    theirs = down_grad(ffn_info, 3, each("mixed"), each("grads"))
    gots = up_grad(after(odd_table, theirs), each("tokens"), each("both"))
    got = send(theirs, 1)
    grad_down = down_grad(after(ffn_info, gots), 2, each("mixed"), each("grads"), got)
    fence(gots=gots, zd=grad_down[: share // 2], ze=grad_down[share // 2 :])

    line_step(live, new="d")
    gots = send(live.pop("gots"), 1)
    grad_normed_two = live["back"][0].astype(f32)
    for k in evens[1:]:
        grad_normed_two = grad_normed_two + live["returned"][k].astype(f32)
    middle = live["middle"]
    factor_two = norm_factor(middle)
    gain_two = live["gains"][1:].astype(f32)
    grad_gain_two, grad_norm_two = norm_back(grad_normed_two, middle, factor_two, gain_two)
    grad_middle = live["grad"].astype(f32) + grad_norm_two
    grad_branch = grad_middle.astype(bf16)
    grad_attended = jnp.concatenate(
        [dot_last(grad_branch, live[k]).astype(bf16) for k in ("out_even", "out_odd")], 1
    )
    parts = up_grad(even_table, each("tokens"), each("both"), gots)
    for k in ("tokens", "grads", "both", "mixed", "back", "returned", "d_other"):
        del live[k]
    for k in ("w_own", "w_rest", "w_other", "w_rest_other"):
        del live[k]
    del live["out_even"], live["out_odd"], live["down"], live["grad"]
    fence(
        ups=dict(zip(evens, parts, strict=True)),
        grad_gain_two=grad_gain_two,
        grad_middle=grad_middle,
        grad_branch=grad_branch,
        grad_attended=grad_attended,
    )

    names = [str(k) for k in evens]

    def blocks(whole, got):
        return {
            k: added(whole[i * block : (i + 1) * block], got[i * block : (i + 1) * block])
            for i, k in enumerate(evens)
        }

    def far_sends(parts):
        if len(rest) != 1:
            return [send(parts[k], k) for k in rest]
        far = parts[rest[0]]
        size = far.shape[0] // 2
        return [send(far[:size], near[0]), send(far[size:], near[1])]

    def near_sends(parts, got):
        if len(rest) != 1:
            return [send(parts[k], k) for k in near]
        size = parts[0].shape[0] // 2
        lower, upper = got
        one, two = parts[near[0]], parts[near[1]]
        one = jnp.concatenate([one[:size], added(one[size:], upper)], 0)
        two = jnp.concatenate([added(two[:size], lower), two[size:]], 0)
        return [send(one, near[0]), send(two, near[1])]

    def total_of(parts, *got):
        total = parts[0].astype(f32)
        for x in sum([g for g in got if g[0].shape == parts[0].shape], []):
            total = total + x.astype(f32)
        return total

    line_step(live, new="e", cross="d")
    sent = {k: send(live["ups"][k], k) for k in near}
    grad_queries, kv_parts = attend_back(
        info,
        live["joined"],
        live["kv"],
        cos_t,
        sin_t,
        live["grad_attended"],
        live["attended"],
        live["lse"],
    )
    fence(sent=sent, grad_queries=grad_queries, kv_parts=kv_parts)
    for k in ("grad_attended", "joined", "kv", "lse"):
        del live[k]

    ups = live.pop("ups")
    live["z0"] = ups[0]
    for k, x in live.pop("sent").items():
        live[f"z{k}"] = x
    line_step(live, new=names[0], cross="e", out="d")
    sent = {k: send(ups[k], k) for k in rest}
    kv_sums = lax.psum_scatter(live.pop("kv_parts"), "seq", scatter_dimension=0, tiled=True)
    kv_sums = kv_sums.reshape(rows, KVH, 2, HD).transpose(0, 2, 1, 3).reshape(rows, 2 * kv_width)
    grad_joined = jnp.concatenate(
        [
            live.pop("grad_queries"),
            turn(kv_sums[:, :kv_width], cos_wide, sin_wide, -1),
            kv_sums[:, kv_width:],
        ],
        1,
    )
    normed_one_x = live.pop("normed_one_x")
    theirs = dot_first(normed_one_x[:, width // 2 :], grad_joined).astype(bf16)
    attended = pick(live.pop("attended"), at_table, block)
    grad_out = dot_first(attended, live.pop("grad_branch")).astype(bf16)
    fence(
        sent=sent,
        grad_out=grad_out,
        grad_joined=grad_joined,
        normed_one_x=normed_one_x,
        theirs=theirs,
    )

    for k, x in live.pop("sent").items():
        live[f"z{k}"] = x
    line_step(live, new=names[1], cross=names[0], out="e")
    out_total = lax.psum_scatter(live.pop("grad_out"), "fsdp", scatter_dimension=0, tiled=True)
    mine = dot_first(live.pop("normed_one_x")[:, : width // 2], live["grad_joined"])
    fence(got_qkv=send(live.pop("theirs"), 1), mine=mine.astype(bf16))

    gate_up_sums = blank((block, 2 * FF), f32)
    outer = is_outer()

    def summed(k):
        return jnp.where(outer, live.pop("o" + k), live.pop("t" + k)).astype(f32)

    def placed_in(buffer, k):
        cols = chip ^ (k // 2)
        spots = jnp.stack([cols, cols + chips])
        return place(buffer, (live.pop(f"o{k}"), live.pop(f"t{k}")), outer, spots, chip_share)

    line_step(live, new=names[2] if chips > 2 else None, cross=names[1], out=names[0])
    parts_qkv = blocks(live.pop("mine"), live.pop("got_qkv"))
    down_sums = jnp.concatenate([summed("d"), summed("e")], 0)
    fence(parts_qkv=parts_qkv, far_qkv=far_sends(parts_qkv), down_sums=down_sums)

    line_step(live, new=names[3] if chips > 3 else None, cross=names[2], out=names[1])
    for k in evens[4:]:
        line_step(live, new=str(k))
    gate_up_sums = placed_in(gate_up_sums, 0)
    inputs = live["hidden"].astype(f32)
    factor_one = norm_factor(inputs)
    grad_normed_one = dot_last(live.pop("grad_joined"), live.pop("qkv"))
    grad_gain_one, grad_norm_one = norm_back(
        grad_normed_one, inputs, factor_one, live["gains"][:1].astype(f32)
    )
    grad_input = (live["grad_middle"] + grad_norm_one).astype(bf16)
    fence(
        near_qkv=near_sends(live["parts_qkv"], live["far_qkv"]),
        zout=out_total,
        sums=gate_up_sums,
        grad_input=grad_input,
        grad_gains=jnp.stack([grad_gain_one, live.pop("grad_gain_two")]),
    )

    line_step(live, new="out", cross=names[3], out=names[2])
    gate_up_sums = placed_in(live.pop("sums"), evens[1])
    total = total_of(live.pop("parts_qkv"), live.pop("far_qkv"), live.pop("near_qkv")).astype(bf16)
    fence(far=far_sends(live["parts"]), sums=gate_up_sums, zq=total)

    line_step(live, new="q", cross="out", out=names[3])
    gate_up_sums = placed_in(live.pop("sums"), evens[2])
    fence(near=near_sends(live["parts"], live["far"]), sums=gate_up_sums)

    line_step(live, cross="q", out="out")
    gate_up_sums = live.pop("sums")
    for k in evens[3:]:
        gate_up_sums = placed_in(gate_up_sums, k)
    grad_gains = small_sum(live.pop("grad_gains"), "fsdp")
    out = total_of(live.pop("parts"), live.pop("far"), live.pop("near"))
    out = (live["middle"] + out).astype(bf16)
    fence(sums=gate_up_sums, grad_gains=grad_gains, out_final=out)

    line_step(live, out="q")
    out_sums = summed("out")
    grad_gains = small_sum(live.pop("grad_gains"), "seq")
    qkv_sums = summed("q")
    grad_gains = lax.dynamic_slice_in_dim(grad_gains, me * block, block, 1)
    return (
        live["out_final"].reshape(hidden_in.shape),
        live["grad_input"].reshape(hidden_in.shape),
        grad_gains[0],
        qkv_sums,
        out_sums,
        grad_gains[1],
        live["sums"],
        live["down_sums"],
    )


def solution(mesh):
    placed = (
        P("fsdp", "seq", None),
        P("fsdp"),
        P("fsdp", None),
        P("fsdp", None),
        P("fsdp"),
        P("fsdp", None),
        P("fsdp", None),
        P("fsdp", "seq", None),
    )
    return jax.shard_map(
        on_device,
        mesh=mesh,
        in_specs=placed,
        out_specs=(
            P("fsdp", "seq", None),
            P("fsdp", "seq", None),
            P("fsdp"),
            P("fsdp", None),
            P("fsdp", None),
            P("fsdp"),
            P("fsdp", None),
            P("fsdp", None),
        ),
        check_vma=False,
    )
```

```python
import functools

import jax
import jax.numpy as jnp
from jax import lax
from jax.experimental import pallas as pl
from jax.experimental.pallas import tpu as pltpu
from jax.sharding import PartitionSpec as P

HEADS = 32
KVH = 4
HD = 64
FF = 5632

epsilon = 1e-05
masked_value = -1e30
log2e = 1.4426950408889634
contract_last = (((1,), (1,)), ((), ()))
contract_first = (((0,), (0,)), ((), ()))
bf16 = jnp.bfloat16
f32 = jnp.float32


def send(x, k):
    n = lax.axis_size("fsdp")
    return lax.ppermute(x, "fsdp", [(i, i ^ k) for i in range(n)])


def chip_bits():
    n = lax.axis_size("fsdp")
    return [1 << i for i in range(1, n.bit_length() - 1)]


def piece_order():
    n = lax.axis_size("fsdp")
    return list(range(0, n, 2)) + list(range(1, n, 2))


def gather_small(x):
    n, me = lax.axis_size("fsdp"), lax.axis_index("fsdp")
    for k in (1 << i for i in range(n.bit_length() - 1)):
        got = send(x, k)
        x = jnp.where(
            me & k == 0, jnp.concatenate([x, got], 1), jnp.concatenate([got, x], 1)
        )
    return x


def neighbour(x):
    n = lax.axis_size("seq")
    return lax.ppermute(x, "seq", [(i, i ^ 1) for i in range(n)])


def after(x, *others):
    return lax.optimization_barrier((x, *others))[0]


def added(one, two):
    return (one.astype(f32) + two.astype(f32)).astype(bf16)


def line_sum(x):
    n = lax.axis_size("seq")
    if n == 1:
        return x
    if n % 2:
        return lax.psum(x.astype(f32), "seq").astype(bf16)
    me = lax.axis_index("seq")
    mid = n // 2
    total = x
    for i in range(mid - 1):
        total = added(total, lax.ppermute(total, "seq", [(i, i + 1), (n - 1 - i, n - 2 - i)]))
    total = added(total, lax.ppermute(total, "seq", [(mid - 1, mid), (mid, mid - 1)]))
    for i in range(mid - 1):
        got = lax.ppermute(total, "seq", [(mid - 1 - i, mid - 2 - i), (mid + i, mid + 1 + i)])
        taken = (me == mid - 2 - i) | (me == mid + 1 + i)
        total = jnp.where(taken, got, total)
    return total


def line_step(live, new=None, cross=None, out=None):
    if lax.axis_size("seq") != 4:
        if new is not None:
            live["o" + new] = live["t" + new] = line_sum(live["z" + new])
        return
    inward, outward, across = [(0, 1), (3, 2)], [(1, 0), (2, 3)], [(1, 2), (2, 1)]
    x = None if new is None else live["z" + new]
    part = None
    if cross is not None:
        part = live["p" + cross] = added(live["z" + cross], live["i" + cross])
        live["x" + cross] = lax.ppermute(part, "seq", across)
        others = {k: v for k, v in live.items() if not k.endswith(cross)}
        live.update(lax.optimization_barrier((others, part))[0])
    if x is not None:
        live["i" + new] = lax.ppermute(x, "seq", inward)
    if out is not None:
        total = live["t" + out] = added(live["p" + out], live["x" + out])
        live["o" + out] = lax.ppermute(total, "seq", outward)


def is_outer():
    me, n = lax.axis_index("seq"), lax.axis_size("seq")
    return (me == 0) | (me == n - 1)


def small_sum(x, axis):
    n = lax.axis_size(axis)
    if n & (n - 1):
        return lax.psum(x, axis)
    for k in (1 << i for i in range(n.bit_length() - 1)):
        x = x + lax.ppermute(x, axis, [(i, i ^ k) for i in range(n)])
    return x


def copy_kernel(table_ref, x_ref, o_ref):
    o_ref[...] = x_ref[...].astype(o_ref.dtype)


def pick(x, table, size, dtype=None, rows_at=None):
    rows, count = x.shape[0], table.shape[0]
    if size % 128:
        return jnp.concatenate(
            [lax.dynamic_slice_in_dim(x, table[i] * size, size, 1) for i in range(count)], 1
        ).astype(dtype or x.dtype)
    if rows_at is not None:
        rows = rows_at[1]
    row = jnp.zeros((), jnp.int32) if rows_at is None else rows_at[0]
    table = jnp.concatenate([table, row.reshape(1)]).astype(jnp.int32)
    return pl.pallas_call(
        copy_kernel,
        out_shape=jax.ShapeDtypeStruct((rows, count * size), dtype or x.dtype),
        grid_spec=pltpu.PrefetchScalarGridSpec(
            num_scalar_prefetch=1,
            grid=(count,),
            in_specs=[pl.BlockSpec((rows, size), lambda i, table: (table[count], table[i]))],
            out_specs=pl.BlockSpec((rows, size), lambda i, table: (0, i)),
        ),
        cost_estimate=pl.CostEstimate(
            flops=0, transcendentals=0, bytes_accessed=rows * count * size * 4
        ),
    )(table, x)


def blank_kernel(o_ref):
    pass


def blank(shape, dtype):
    return pl.pallas_call(
        blank_kernel,
        out_shape=jax.ShapeDtypeStruct(shape, dtype),
        out_specs=pl.BlockSpec(memory_space=pl.ANY),
    )()


def turn_kernel(sign, x_ref, cos_ref, sin_ref, o_ref):
    x = x_ref[...].astype(f32)
    width = x.shape[1]
    lane = lax.broadcasted_iota(jnp.int32, x.shape, 1)
    first = (lane % HD) < HD // 2
    other = jnp.where(
        first, -pltpu.roll(x, width - HD // 2, 1), pltpu.roll(x, HD // 2, 1)
    )
    o_ref[...] = (x * cos_ref[...] + sign * other * sin_ref[...]).astype(o_ref.dtype)


def turn(x, cos_wide, sin_wide, sign):
    return pl.pallas_call(
        functools.partial(turn_kernel, float(sign)),
        out_shape=jax.ShapeDtypeStruct(x.shape, bf16),
    )(x, cos_wide, sin_wide)


def place_kernel(info_ref, buffer_ref, got_ref, total_ref, o_ref):
    o_ref[...] = jnp.where(info_ref[0] == 1, got_ref[...], total_ref[...]).astype(f32)


def place(buffer, pair, outer, where, size):
    got, total = pair
    rows = got.shape[0]
    if size % 128:
        picked = jnp.where(outer, got, total).astype(f32)
        for i in range(2):
            buffer = lax.dynamic_update_slice_in_dim(
                buffer, picked[:, i * size : (i + 1) * size], where[i] * size, 1
            )
        return buffer
    info = jnp.concatenate([outer.astype(jnp.int32).reshape(1), where.astype(jnp.int32)])
    own = pl.BlockSpec((rows, size), lambda i, info: (0, i))
    return pl.pallas_call(
        place_kernel,
        out_shape=jax.ShapeDtypeStruct(buffer.shape, f32),
        grid_spec=pltpu.PrefetchScalarGridSpec(
            num_scalar_prefetch=1,
            grid=(2,),
            in_specs=[pl.BlockSpec(memory_space=pl.ANY), own, own],
            out_specs=pl.BlockSpec((rows, size), lambda i, info: (0, info[1 + i])),
        ),
        input_output_aliases={1: 0},
    )(info, buffer, got, total)


def mask_bias(start, length, rows):
    key_place = lax.broadcasted_iota(jnp.int32, (length, rows), 0)
    query_place = start + lax.broadcasted_iota(jnp.int32, (length, rows), 1)
    return jnp.where(key_place <= query_place, 0.0, masked_value).astype(f32)


def turned_t(x, cos, sin):
    one, two = x[: HD // 2], x[HD // 2 :]
    return jnp.concatenate([one * cos - two * sin, two * cos + one * sin], 0)


def kv_head(ref, index):
    both = ref[...]
    return jnp.where(index % 2 == 0, both[:, :HD], both[:, HD:])


def attend_kernel(
    heads, per_kv, info_ref, q_ref, k_ref, v_ref, cos_ref, sin_ref, o_ref, lse_ref, bias_ref
):
    length, rows = k_ref.shape[0], q_ref.shape[0]
    scale2 = HD**-0.5 * log2e
    step = pl.program_id(0)

    @pl.when(step == 0)
    def _():
        bias_ref[...] = mask_bias(info_ref[0], length, rows)

    kv = step * heads // per_kv
    keys = kv_head(k_ref, kv)
    values_t = kv_head(v_ref, kv).astype(f32).T.astype(bf16)
    q_t = q_ref[...].T
    cos, sin = cos_ref[...], sin_ref[...]
    q_all = [
        turned_t(q_t[h * HD : (h + 1) * HD], cos, sin).astype(bf16) for h in range(heads)
    ]

    key_size = jnp.max(jnp.sum(jnp.square(keys.astype(f32)), axis=1))
    query_size = jnp.max(
        sum(
            jnp.sum(jnp.square(q.astype(f32)), axis=0, keepdims=True) for q in q_all
        )
    )
    small = key_size * query_size * scale2**2 < 80.0**2

    def run(shift):
        outs = []
        for h in range(heads):
            scores = jnp.dot(keys, q_all[h], preferred_element_type=f32) + bias_ref[...]
            if shift:
                top = jnp.max(scores, axis=0, keepdims=True)
                weights = jnp.exp2((scores - top) * scale2)
            else:
                weights = jnp.exp2(scores * scale2)
            total = jnp.sum(weights, axis=0, keepdims=True)
            out = jnp.dot(values_t, weights.astype(bf16), preferred_element_type=f32)
            outs.append(out * (1.0 / total))
            lse = jnp.log2(total)
            lse_ref[0, h : h + 1, :] = lse + top * scale2 if shift else lse
        o_ref[...] = jnp.concatenate(outs, 0).T.astype(bf16)

    pl.when(small)(lambda: run(False))
    pl.when(jnp.logical_not(small))(lambda: run(True))


def attend_specs(n, rows, length):
    heads = HEADS // n
    per_kv = HEADS // KVH
    kv_at = lambda i: (i * heads // per_kv) // 2
    return dict(
        plain=pl.BlockSpec((rows, heads * HD), lambda i, info: (0, i)),
        ordered=pl.BlockSpec((rows, heads * HD), lambda i, info: (0, info[1 + i])),
        keys=pl.BlockSpec((length, 2 * HD), lambda i, info: (0, kv_at(i))),
        values=pl.BlockSpec((length, 2 * HD), lambda i, info: (0, KVH // 2 + kv_at(i))),
        table=pl.BlockSpec((HD // 2, rows), lambda i, info: (0, 0)),
        lse=pl.BlockSpec((1, heads, rows), lambda i, info: (i, 0, 0)),
    )


def attend(info, joined, all_kv, cos_t, sin_t):
    n = lax.axis_size("fsdp")
    rows, length = joined.shape[0], all_kv.shape[0]
    heads = HEADS // n
    spec = attend_specs(n, rows, length)
    return pl.pallas_call(
        functools.partial(attend_kernel, heads, HEADS // KVH),
        out_shape=(
            jax.ShapeDtypeStruct((rows, HEADS * HD), bf16),
            jax.ShapeDtypeStruct((n, heads, rows), f32),
        ),
        grid_spec=pltpu.PrefetchScalarGridSpec(
            num_scalar_prefetch=1,
            grid=(n,),
            in_specs=[spec[k] for k in ("plain", "keys", "values", "table", "table")],
            out_specs=(spec["ordered"], spec["lse"]),
            scratch_shapes=[pltpu.VMEM((length, rows), f32)],
        ),
        compiler_params=pltpu.CompilerParams(vmem_limit_bytes=40 << 20),
        cost_estimate=pl.CostEstimate(
            flops=4 * HEADS * rows * length * HD * 4,
            bytes_accessed=6 * rows * HEADS * HD,
            transcendentals=HEADS * rows * length,
        ),
    )(info, joined, all_kv, all_kv, cos_t, sin_t)


def attend_back_kernel(
    heads, per_kv, info_ref, q_ref, k_ref, v_ref, g_ref, o_ref, cos_ref, sin_ref, lse_ref,
    dq_ref, dkv_ref, bias_ref, dk_ref, dv_ref,
):
    length, rows = k_ref.shape[0], q_ref.shape[0]
    scale = HD**-0.5
    scale2 = scale * log2e
    step = pl.program_id(0)
    steps = per_kv // heads

    @pl.when(step == 0)
    def _():
        bias_ref[...] = mask_bias(info_ref[0], length, rows)

    @pl.when(step % steps == 0)
    def _():
        dk_ref[...] = jnp.zeros_like(dk_ref)
        dv_ref[...] = jnp.zeros_like(dv_ref)

    kv = step * heads // per_kv
    keys, values = kv_head(k_ref, kv), kv_head(v_ref, kv)
    keys_t = keys.astype(f32).T.astype(bf16)
    q_t = q_ref[...].T
    g_t = g_ref[...].astype(f32).T
    deltas = g_t * o_ref[...].astype(f32).T
    g_t = g_t.astype(bf16)
    cos, sin = cos_ref[...], sin_ref[...]
    outs = []
    dk, dv = dk_ref[...], dv_ref[...]
    for h in range(heads):
        q_h = turned_t(q_t[h * HD : (h + 1) * HD], cos, sin).astype(bf16)
        g_h = g_t[h * HD : (h + 1) * HD]
        scores = jnp.dot(keys, q_h, preferred_element_type=f32) + bias_ref[...]
        weights = jnp.exp2(scores * scale2 - lse_ref[0, h : h + 1, :])
        grad_p = jnp.dot(values, g_h, preferred_element_type=f32)
        delta = jnp.sum(deltas[h * HD : (h + 1) * HD], axis=0, keepdims=True)
        grad_s = (weights * (grad_p - delta)).astype(bf16)
        grad_q = jnp.dot(keys_t, grad_s, preferred_element_type=f32) * scale
        outs.append(turned_t(grad_q.astype(bf16).astype(f32), cos, -sin))
        dk += lax.dot_general(grad_s, q_h, contract_last, preferred_element_type=f32)
        dv += lax.dot_general(
            weights.astype(bf16), g_h, contract_last, preferred_element_type=f32
        )
    dk_ref[...], dv_ref[...] = dk, dv
    dq_ref[...] = jnp.concatenate(outs, 0).T.astype(bf16)

    @pl.when(step % steps == steps - 1)
    def _():
        dkv_ref[...] = jnp.concatenate([dk * scale, dv], 1).astype(bf16)


def attend_back(info, joined, all_kv, cos_t, sin_t, grads, outs, lse):
    n = lax.axis_size("fsdp")
    rows, length = joined.shape[0], all_kv.shape[0]
    heads, per_kv = HEADS // n, HEADS // KVH
    spec = attend_specs(n, rows, length)
    names = ("plain", "keys", "values", "ordered", "ordered", "table", "table", "lse")
    return pl.pallas_call(
        functools.partial(attend_back_kernel, heads, per_kv),
        out_shape=(
            jax.ShapeDtypeStruct((rows, HEADS * HD), bf16),
            jax.ShapeDtypeStruct((length, 2 * KVH * HD), bf16),
        ),
        grid_spec=pltpu.PrefetchScalarGridSpec(
            num_scalar_prefetch=1,
            grid=(n,),
            in_specs=[spec[k] for k in names],
            out_specs=(
                spec["plain"],
                pl.BlockSpec((length, 2 * HD), lambda i, info: (0, i * heads // per_kv)),
            ),
            scratch_shapes=[
                pltpu.VMEM((length, rows), f32),
                pltpu.VMEM((length, HD), f32),
                pltpu.VMEM((length, HD), f32),
            ],
        ),
        compiler_params=pltpu.CompilerParams(vmem_limit_bytes=48 << 20),
        cost_estimate=pl.CostEstimate(
            flops=10 * HEADS * rows * length * HD * 4,
            bytes_accessed=8 * rows * HEADS * HD,
            transcendentals=HEADS * rows * length,
        ),
    )(info, joined, all_kv, all_kv, grads, outs, cos_t, sin_t, lse)


def column_chunks(total, size=256):
    return [(c, min(size, total - c)) for c in range(0, total, size)]


def part_pieces(n):
    evens = list(range(0, n, 2))
    return evens[:3], evens[3:], [k | 1 for k in evens[:3]], [k | 1 for k in evens[3:]]


def ffn_kernel(n, count, info_ref, *refs):
    x_refs, g_refs, refs = refs[:count], refs[count : 2 * count], refs[2 * count :]
    parts, (d_own, d_other), refs = refs[:4], refs[4:6], refs[6:]
    outs, (x, g, w, d, both, mid, sems) = refs[: 4 * count], refs[4 * count :]
    mixed_refs, both_refs = outs[:count], outs[count : 2 * count]
    back_refs, out_refs = outs[2 * count : 3 * count], outs[3 * count :]
    me, part = info_ref[0], info_ref[1]
    rows, width = x_refs[0].shape
    cols = d.shape[0]
    share = cols // 2
    block = width // n
    half = block // 2

    copies = []
    for source, ks in zip(parts, part_pieces(n), strict=True):
        for i, k in enumerate(ks):
            owner = (me ^ k) * block
            for j in range(2):
                at = owner if k < 2 else owner + (part if j == 0 else 1 - part) * half
                if k < 2:
                    at = at + j * half
                copies.append(
                    pltpu.make_async_copy(
                        source.at[pl.ds(i * block + j * half, half)],
                        w.at[pl.ds(pl.multiple_of(at, half), half)],
                        sems.at[len(copies)],
                    )
                )
    core = me % 2
    for source, at in ((d_own, core), (d_other, 1 - core)):
        copies.append(
            pltpu.make_async_copy(
                source, d.at[pl.ds(pl.multiple_of(at * share, share), share)], sems.at[len(copies)]
            )
        )
    for copy in copies:
        copy.start()
    for i in range(count):
        x[i * rows : (i + 1) * rows] = x_refs[i][...]
        g[i * rows : (i + 1) * rows] = g_refs[i][...]
    for copy in copies:
        copy.wait()

    def columns(at, size):
        gate_w, up_w = w[:, pl.ds(at, size)], w[:, pl.ds(cols + at, size)]
        gate = jnp.dot(x[...], gate_w, preferred_element_type=f32)
        up = jnp.dot(x[...], up_w, preferred_element_type=f32)
        grad = lax.dot_general(
            g[...], d[pl.ds(at, size)], contract_last, preferred_element_type=f32
        )
        sig = 1.0 / (1.0 + jnp.exp(-gate))
        act = gate * sig
        mid[:, pl.ds(at, size)] = (act * up).astype(bf16)
        both[:, pl.ds(at, size)] = (grad * up * (sig * (1.0 + gate * (1.0 - sig)))).astype(bf16)
        both[:, pl.ds(cols + at, size)] = (grad * act).astype(bf16)

    full = cols // 256
    pl.loop(0, full)(lambda c: columns(pl.multiple_of(c * 256, 256), 256))
    if cols % 256:
        columns(full * 256, cols % 256)
    for i in range(count):
        at = slice(i * rows, (i + 1) * rows)
        mixed_refs[i][...] = mid[at].astype(f32).T.astype(bf16)
        both_refs[i][...] = both[at]

    @pl.loop(0, width // 256)
    def _(t):
        at = pl.multiple_of(t * 256, 256)
        back = lax.dot_general(
            both[...], w[pl.ds(at, 256)], contract_last, preferred_element_type=f32
        ).astype(bf16)
        out = jnp.dot(mid[...], d[:, pl.ds(at, 256)], preferred_element_type=f32).astype(bf16)
        for i in range(count):
            back_refs[i][:, pl.ds(at, 256)] = back[i * rows : (i + 1) * rows]
            out_refs[i][:, pl.ds(at, 256)] = out[i * rows : (i + 1) * rows]


def ffn(info, xs, gs, parts, d_own, d_other):
    n = lax.axis_size("fsdp")
    count = len(xs)
    rows, width = xs[0].shape
    cols = 2 * d_own.shape[0]
    if cols % 128:
        return ffn_plain(info, xs, gs, parts, d_own, d_other)
    shapes = (
        [jax.ShapeDtypeStruct((cols, rows), bf16)] * count
        + [jax.ShapeDtypeStruct((rows, 2 * cols), bf16)] * count
        + [jax.ShapeDtypeStruct((rows, width), bf16)] * (2 * count)
    )
    vmem, hbm = pl.BlockSpec(memory_space=pltpu.VMEM), pl.BlockSpec(memory_space=pl.ANY)
    outs = pl.pallas_call(
        functools.partial(ffn_kernel, n, count),
        out_shape=shapes,
        in_specs=[pl.BlockSpec(memory_space=pltpu.SMEM)] + [vmem] * (2 * count) + [hbm] * 6,
        out_specs=[vmem] * (4 * count),
        scratch_shapes=[
            pltpu.VMEM((count * rows, width), bf16),
            pltpu.VMEM((count * rows, width), bf16),
            pltpu.VMEM((width, 2 * cols), bf16),
            pltpu.VMEM((cols, width), bf16),
            pltpu.VMEM((count * rows, 2 * cols), bf16),
            pltpu.VMEM((count * rows, cols), bf16),
            pltpu.SemaphoreType.DMA((2 * n + 2,)),
        ],
        compiler_params=pltpu.CompilerParams(vmem_limit_bytes=56 << 20),
        cost_estimate=pl.CostEstimate(
            flops=2 * count * rows * width * cols * 6,
            bytes_accessed=6 * width * cols,
            transcendentals=count * rows * cols,
        ),
    )(info, *xs, *gs, *parts, d_own, d_other)
    return [outs[i * count : (i + 1) * count] for i in range(4)]


def ffn_plain(info, xs, gs, parts, d_own, d_other):
    n = lax.axis_size("fsdp")
    me, part = info[0], info[1]
    width, share = xs[0].shape[1], d_own.shape[0]
    block, cols = width // n, 2 * share
    half = block // 2
    w = jnp.zeros((width, 2 * cols), bf16)
    for source, ks in zip(parts, part_pieces(n), strict=True):
        for i, k in enumerate(ks):
            for j in range(2):
                at = j if k < 2 else (part if j == 0 else 1 - part)
                rows = source[i * block + j * half : i * block + (j + 1) * half]
                w = lax.dynamic_update_slice_in_dim(w, rows, (me ^ k) * block + at * half, 0)
    d = jnp.where(
        me % 2 == 0, jnp.concatenate([d_own, d_other], 0), jnp.concatenate([d_other, d_own], 0)
    )
    mixed, both, back, out = [], [], [], []
    for x, g in zip(xs, gs, strict=True):
        gate, up = dot(x, w[:, :cols]), dot(x, w[:, cols:])
        sig = jax.nn.sigmoid(gate)
        act = gate * sig
        grad = dot_last(g, d)
        mid = (act * up).astype(bf16)
        two = jnp.concatenate(
            [grad * up * (sig * (1.0 + gate * (1.0 - sig))), grad * act], 1
        ).astype(bf16)
        mixed.append(mid.T)
        both.append(two)
        back.append(dot_last(two, w).astype(bf16))
        out.append(dot(mid, d).astype(bf16))
    return mixed, both, back, out


def down_grad_kernel(count, info_ref, *refs):
    lefts, rights, rest = refs[:count], refs[count : 2 * count], refs[2 * count :]
    total = sum(
        jnp.dot(one[...], two[...], preferred_element_type=f32)
        for one, two in zip(lefts, rights, strict=True)
    )
    if len(rest) == 2:
        total = total.astype(bf16).astype(f32) + rest[0][...].astype(f32)
    rest[-1][...] = total.astype(bf16)


def down_grad(info, at, mixed, gs, got=None):
    count = len(mixed)
    cols, rows = mixed[0].shape
    width = gs[0].shape[1]
    size = min(512, width)
    out = pl.BlockSpec((cols // 2, size), lambda i, info: (0, i))
    return pl.pallas_call(
        functools.partial(down_grad_kernel, count),
        out_shape=jax.ShapeDtypeStruct((cols // 2, width), bf16),
        grid_spec=pltpu.PrefetchScalarGridSpec(
            num_scalar_prefetch=1,
            grid=(width // size,),
            in_specs=[pl.BlockSpec((cols // 2, rows), lambda i, info: (info[at], 0))] * count
            + [pl.BlockSpec((rows, size), lambda i, info: (0, i))] * count
            + ([] if got is None else [out]),
            out_specs=out,
        ),
        compiler_params=pltpu.CompilerParams(vmem_limit_bytes=40 << 20),
        cost_estimate=pl.CostEstimate(
            flops=count * rows * width * cols,
            bytes_accessed=4 * width * cols,
            transcendentals=0,
        ),
    )(info, *mixed, *gs, *([] if got is None else [got]))


def up_grad_kernel(count, split, info_ref, *refs):
    lefts, rights, rest = refs[:count], refs[count : 2 * count], refs[2 * count :]
    total = sum(
        lax.dot_general(one[...], two[...], contract_first, preferred_element_type=f32)
        for one, two in zip(lefts, rights, strict=True)
    ).astype(bf16)
    if not split:
        rest[0][...] = total
        return
    total = (total.astype(f32) + rest[0][...].astype(f32)).astype(bf16)
    for i, out in enumerate(rest[1:]):

        @pl.when(pl.program_id(1) == i)
        def _(out=out):
            out[...] = total


def up_grad(table, xs, both, got=None):
    count, chips = len(xs), table.shape[0]
    rows, width = xs[0].shape
    cols = both[0].shape[1] // 2
    block = width // lax.axis_size("fsdp")
    if cols % 128 or block % 128:
        whole = sum(dot_first(one, two) for one, two in zip(xs, both, strict=True))
        outs = [
            lax.dynamic_slice_in_dim(whole, table[i] * block, block, 0).astype(bf16)
            for i in range(chips)
        ]
        if got is None:
            return jnp.concatenate(outs, 0)
        return [added(x, got[i * block : (i + 1) * block]) for i, x in enumerate(outs)]
    one = pl.BlockSpec((block, cols), lambda h, b, table: (b, h))
    outs = [
        pl.BlockSpec(
            (block, cols), lambda h, b, table, i=i: (0, jnp.where(b >= i, h, jnp.maximum(h - 1, 0)))
        )
        for i in range(chips)
    ]
    split = got is not None
    shape = jax.ShapeDtypeStruct((block, 2 * cols), bf16)
    return pl.pallas_call(
        functools.partial(up_grad_kernel, count, split),
        out_shape=[shape] * chips
        if split
        else jax.ShapeDtypeStruct((chips * block, 2 * cols), bf16),
        grid_spec=pltpu.PrefetchScalarGridSpec(
            num_scalar_prefetch=1,
            grid=(2, chips),
            in_specs=[pl.BlockSpec((rows, block), lambda h, b, table: (0, table[b]))] * count
            + [pl.BlockSpec((rows, cols), lambda h, b, table: (0, h))] * count
            + ([one] if split else []),
            out_specs=outs if split else one,
        ),
        compiler_params=pltpu.CompilerParams(vmem_limit_bytes=48 << 20),
        cost_estimate=pl.CostEstimate(
            flops=4 * count * rows * chips * block * cols,
            bytes_accessed=4 * chips * block * cols * 2,
            transcendentals=0,
        ),
    )(table, *xs, *both, *([got] if split else []))


def angle_tables(positions):
    half_dim = HD // 2
    inverse = 10000.0 ** (-jnp.arange(half_dim, dtype=f32) * 2.0 / HD)
    angles = positions.astype(f32)[:, None] * inverse[None, :]
    return jnp.cos(angles), jnp.sin(angles)


def norm_factor(values):
    return lax.rsqrt(jnp.mean(values * values, axis=-1, keepdims=True) + epsilon)


def norm_back(incoming, inputs, factor, gain):
    weighted = incoming * gain
    gain_grad = jnp.sum(incoming * (inputs * factor), axis=0)
    input_grad = weighted * factor - inputs * (factor * factor * factor) * jnp.mean(
        weighted * inputs, axis=-1, keepdims=True
    )
    return (gain_grad, input_grad)


def dot(one, two):
    return jnp.dot(one, two, preferred_element_type=f32)


def dot_last(one, two):
    return lax.dot_general(one, two, contract_last, preferred_element_type=f32)


def dot_first(one, two):
    return lax.dot_general(one, two, contract_first, preferred_element_type=f32)


def on_device(
    hidden_in, norm_attn, qkv_weight, out_weight, norm_ffn, gate_up_weight, down_weight, cotangent
):
    n = lax.axis_size("fsdp")
    me = lax.axis_index("fsdp")
    chips, chip, core = n // 2, me // 2, me % 2
    order = piece_order()
    evens = order[:chips]
    near, rest = evens[1:3], evens[3:]
    width = hidden_in.shape[2]
    rows = hidden_in.shape[0] * hidden_in.shape[1]
    q_width = HEADS * HD
    kv_width = KVH * HD
    share = FF // n
    chip_share = 2 * share
    block = width // n
    half = block // 2
    seq_at = lax.axis_index("seq")
    rank = {k: i for i, k in enumerate(order)}
    to_table = (me ^ jnp.array(order, jnp.int32)).astype(jnp.int32)
    at_table = jnp.array([rank[k] for k in range(n)], jnp.int32)[
        me ^ jnp.arange(n, dtype=jnp.int32)
    ]
    odd_table, even_table = to_table[chips:], to_table[:chips]
    assisted = lax.axis_size("seq") % 2 == 0
    part_at = seq_at % 2 if assisted else jnp.zeros_like(seq_at)

    live = {}

    def fence(**more):
        live.update(more)
        new = lax.optimization_barrier(live)
        live.clear()
        live.update(new)

    def two_hops(pieces):
        if len(rest) != 1:
            return {k: send(pieces[0], k) for k in rest}
        a, b = near
        size = pieces[0].shape[0] // 2
        lower, upper = send(pieces[b][:size], a), send(pieces[a][size:], b)
        return {rest[0]: (lower, upper)}

    def whole_piece(x):
        return jnp.concatenate(x, 0) if isinstance(x, tuple) else x

    def my_columns(k, at):
        cols = chip ^ (k // 2)
        spots = jnp.stack([cols, cols + chips]).astype(jnp.int32)
        if at is None:
            return pick(live["gate_up"], spots, chip_share)
        if chip_share % 128:
            part = pick(live["gate_up"], spots, chip_share)
            return lax.dynamic_slice_in_dim(part, at * half, half, 0)
        return pick(live["gate_up"], spots, chip_share, rows_at=(at, half))

    def other_half(k, first):
        return neighbour(first) if assisted else send(live["others"][k], k)

    full_qkv = lax.all_gather(qkv_weight, "fsdp", axis=0, tiled=True)
    fence(
        gains=gather_small(jnp.stack([norm_attn, norm_ffn])),
        hidden=hidden_in.reshape(rows, width),
        grad=cotangent.reshape(rows, width),
        gate_up=gate_up_weight,
        down=down_weight,
        out=out_weight,
    )

    firsts = {k: send(my_columns(k, part_at), k) for k in near}
    fence(
        firsts=firsts,
        others={} if assisted else {k: my_columns(k, 1 - part_at) for k in evens[1:]},
        own=my_columns(0, None),
        d_other=send(live["down"], 1),
    )
    inputs = live["hidden"].astype(f32)
    factor_one = norm_factor(inputs)
    gains = live["gains"].astype(f32)
    normed_one = (inputs * factor_one * gains[:1]).astype(bf16)
    fence(
        seconds={k: other_half(k, live["firsts"][k]) for k in near},
        mine={k: my_columns(k, part_at) for k in rest},
        qkv=full_qkv,
        normed_one=normed_one,
        normed_one_x=pick(normed_one, to_table, block),
    )
    del live["gate_up"]

    normed_one = live.pop("normed_one")
    joined = dot(normed_one, live["qkv"][:, q_width:])
    positions = seq_at * rows + jnp.arange(rows, dtype=jnp.int32)
    cosine, sine = angle_tables(positions)
    cos_wide, sin_wide = jnp.tile(cosine, (1, 2 * KVH)), jnp.tile(sine, (1, 2 * KVH))
    cos_t, sin_t = cosine.T, sine.T
    keys_values = jnp.concatenate(
        [turn(joined[:, :kv_width], cos_wide, sin_wide, 1), joined[:, kv_width:].astype(bf16)], 1
    )
    all_kv = lax.all_gather(keys_values, "seq", axis=0, tiled=True)
    joined = dot(normed_one, live["qkv"][:, :q_width])
    outs = {0: live.pop("out")}
    outs |= {k: send(outs[0], k) for k in near}
    firsts, seconds = live.pop("firsts"), live.pop("seconds")
    w_own = jnp.concatenate(sum([[firsts[k], seconds[k]] for k in near], [live.pop("own")]), 0)
    firsts = {k: send(x, k) for k, x in live.pop("mine").items()}
    fence(w_own=w_own, joined=joined, kv=all_kv, outs=outs, firsts=firsts)

    outs = live.pop("outs")
    outs |= two_hops(outs)
    firsts = live.pop("firsts")
    seconds = {k: other_half(k, firsts[k]) for k in rest}
    info = jnp.concatenate([(seq_at * rows).reshape(1), at_table]).astype(jnp.int32)
    attended, lse = attend(info, live["joined"], live["kv"], cos_t, sin_t)
    fence(
        firsts=firsts,
        seconds=seconds,
        outs=outs,
        attended=attended,
        lse=lse,
        w_other=send(live["w_own"], 1),
    )

    outs, firsts, seconds = live.pop("outs"), live.pop("firsts"), live.pop("seconds")
    out_even = jnp.concatenate([whole_piece(outs[k]) for k in evens], 0)
    out_odd = send(out_even, 1)
    grads = {0: live["grad"]}
    grads |= {k: send(grads[0], k) for k in near}
    w_rest = sum([[firsts[k], seconds[k]] for k in rest], [])
    w_rest = jnp.concatenate(w_rest or [live["w_own"]], 0)
    middle = dot(live["attended"][:, : q_width // 2], out_even)
    middle = live["hidden"].astype(f32) + (
        middle + dot(live["attended"][:, q_width // 2 :], out_odd)
    )
    factor_two = norm_factor(middle)
    gain_two = live["gains"][1:].astype(f32)
    normed_two = (middle * factor_two * gain_two).astype(bf16)
    fence(
        w_rest=w_rest,
        w_rest_other=send(w_rest, 1),
        out_even=out_even,
        out_odd=out_odd,
        grads=grads,
        middle=middle,
        tokens={0: normed_two},
    )

    ffn_info = jnp.stack([me, part_at, core, 1 - core]).astype(jnp.int32)

    def ffn_of(group):
        names = ("mixed", "both", "back", "parts")
        weights = [live[k] for k in ("w_own", "w_rest", "w_other", "w_rest_other")]
        results = ffn(
            ffn_info,
            [whole_piece(live["tokens"][k]) for k in group],
            [whole_piece(live["grads"][k]) for k in group],
            weights,
            live["down"],
            live["d_other"],
        )
        for name, new in zip(names, results, strict=True):
            live[name] = live.get(name, {}) | dict(zip(group, new, strict=True))

    new = {k: send(live["tokens"][0], k) for k in near}
    ffn_of([0])
    live["tokens"] |= new
    fence()
    far_tokens, far_grads = two_hops(live["tokens"]), two_hops(live["grads"])
    ffn_of(near)
    live["tokens"] |= far_tokens
    live["grads"] |= far_grads
    fence()
    new = {k: send(live["back"][k], k) for k in near}
    if rest:
        ffn_of(rest)
    fence(returned=new)

    live["returned"] |= {k: send(live["back"][k], k) for k in rest}

    def each(name):
        return [whole_piece(live[name][k]) for k in evens]

    theirs = down_grad(ffn_info, 3, each("mixed"), each("grads"))
    gots = up_grad(after(odd_table, theirs), each("tokens"), each("both"))
    got = send(theirs, 1)
    grad_down = down_grad(after(ffn_info, gots), 2, each("mixed"), each("grads"), got)
    fence(gots=gots, zd=grad_down[: share // 2], ze=grad_down[share // 2 :])

    line_step(live, new="d")
    gots = send(live.pop("gots"), 1)
    grad_normed_two = live["back"][0].astype(f32)
    for k in evens[1:]:
        grad_normed_two = grad_normed_two + live["returned"][k].astype(f32)
    middle = live["middle"]
    factor_two = norm_factor(middle)
    gain_two = live["gains"][1:].astype(f32)
    grad_gain_two, grad_norm_two = norm_back(grad_normed_two, middle, factor_two, gain_two)
    grad_middle = live["grad"].astype(f32) + grad_norm_two
    grad_branch = grad_middle.astype(bf16)
    grad_attended = jnp.concatenate(
        [dot_last(grad_branch, live[k]).astype(bf16) for k in ("out_even", "out_odd")], 1
    )
    parts = up_grad(even_table, each("tokens"), each("both"), gots)
    for k in ("tokens", "grads", "both", "mixed", "back", "returned", "d_other"):
        del live[k]
    for k in ("w_own", "w_rest", "w_other", "w_rest_other"):
        del live[k]
    del live["out_even"], live["out_odd"], live["down"], live["grad"]
    fence(
        ups=dict(zip(evens, parts, strict=True)),
        grad_gain_two=grad_gain_two,
        grad_middle=grad_middle,
        grad_branch=grad_branch,
        grad_attended=grad_attended,
    )

    names = [str(k) for k in evens]

    def blocks(whole, got):
        return {
            k: added(whole[i * block : (i + 1) * block], got[i * block : (i + 1) * block])
            for i, k in enumerate(evens)
        }

    def far_sends(parts):
        if len(rest) != 1:
            return [send(parts[k], k) for k in rest]
        far = parts[rest[0]]
        size = far.shape[0] // 2
        return [send(far[:size], near[0]), send(far[size:], near[1])]

    def near_sends(parts, got):
        if len(rest) != 1:
            return [send(parts[k], k) for k in near]
        size = parts[0].shape[0] // 2
        lower, upper = got
        one, two = parts[near[0]], parts[near[1]]
        one = jnp.concatenate([one[:size], added(one[size:], upper)], 0)
        two = jnp.concatenate([added(two[:size], lower), two[size:]], 0)
        return [send(one, near[0]), send(two, near[1])]

    def total_of(parts, *got):
        total = parts[0].astype(f32)
        for x in sum([g for g in got if g[0].shape == parts[0].shape], []):
            total = total + x.astype(f32)
        return total

    line_step(live, new="e", cross="d")
    sent = {k: send(live["ups"][k], k) for k in near}
    grad_queries, kv_parts = attend_back(
        info,
        live["joined"],
        live["kv"],
        cos_t,
        sin_t,
        live["grad_attended"],
        live["attended"],
        live["lse"],
    )
    fence(sent=sent, grad_queries=grad_queries, kv_parts=kv_parts)
    for k in ("grad_attended", "joined", "kv", "lse"):
        del live[k]

    ups = live.pop("ups")
    live["z0"] = ups[0]
    for k, x in live.pop("sent").items():
        live[f"z{k}"] = x
    line_step(live, new=names[0], cross="e", out="d")
    sent = {k: send(ups[k], k) for k in rest}
    kv_sums = lax.psum_scatter(live.pop("kv_parts"), "seq", scatter_dimension=0, tiled=True)
    kv_sums = kv_sums.reshape(rows, KVH, 2, HD).transpose(0, 2, 1, 3).reshape(rows, 2 * kv_width)
    grad_joined = jnp.concatenate(
        [
            live.pop("grad_queries"),
            turn(kv_sums[:, :kv_width], cos_wide, sin_wide, -1),
            kv_sums[:, kv_width:],
        ],
        1,
    )
    normed_one_x = live.pop("normed_one_x")
    theirs = dot_first(normed_one_x[:, width // 2 :], grad_joined).astype(bf16)
    attended = pick(live.pop("attended"), at_table, block)
    grad_out = dot_first(attended, live.pop("grad_branch")).astype(bf16)
    fence(
        sent=sent,
        grad_out=grad_out,
        grad_joined=grad_joined,
        normed_one_x=normed_one_x,
        theirs=theirs,
    )

    for k, x in live.pop("sent").items():
        live[f"z{k}"] = x
    line_step(live, new=names[1], cross=names[0], out="e")
    out_total = lax.psum_scatter(live.pop("grad_out"), "fsdp", scatter_dimension=0, tiled=True)
    mine = dot_first(live.pop("normed_one_x")[:, : width // 2], live["grad_joined"])
    fence(got_qkv=send(live.pop("theirs"), 1), mine=mine.astype(bf16))

    gate_up_sums = blank((block, 2 * FF), f32)
    outer = is_outer()

    def summed(k):
        return jnp.where(outer, live.pop("o" + k), live.pop("t" + k)).astype(f32)

    def placed_in(buffer, k):
        cols = chip ^ (k // 2)
        spots = jnp.stack([cols, cols + chips])
        return place(buffer, (live.pop(f"o{k}"), live.pop(f"t{k}")), outer, spots, chip_share)

    line_step(live, new=names[2] if chips > 2 else None, cross=names[1], out=names[0])
    parts_qkv = blocks(live.pop("mine"), live.pop("got_qkv"))
    down_sums = jnp.concatenate([summed("d"), summed("e")], 0)
    fence(parts_qkv=parts_qkv, far_qkv=far_sends(parts_qkv), down_sums=down_sums)

    line_step(live, new=names[3] if chips > 3 else None, cross=names[2], out=names[1])
    for k in evens[4:]:
        line_step(live, new=str(k))
    gate_up_sums = placed_in(gate_up_sums, 0)
    inputs = live["hidden"].astype(f32)
    factor_one = norm_factor(inputs)
    grad_normed_one = dot_last(live.pop("grad_joined"), live.pop("qkv"))
    grad_gain_one, grad_norm_one = norm_back(
        grad_normed_one, inputs, factor_one, live["gains"][:1].astype(f32)
    )
    grad_input = (live["grad_middle"] + grad_norm_one).astype(bf16)
    fence(
        near_qkv=near_sends(live["parts_qkv"], live["far_qkv"]),
        zout=out_total,
        sums=gate_up_sums,
        grad_input=grad_input,
        grad_gains=jnp.stack([grad_gain_one, live.pop("grad_gain_two")]),
    )

    total = total_of(live.pop("parts_qkv"), live.pop("far_qkv"), live.pop("near_qkv"))
    live["zq"] = total.astype(bf16)
    line_step(live, new="q", cross=names[3], out=names[2])
    gate_up_sums = placed_in(live.pop("sums"), evens[1])
    fence(far=far_sends(live["parts"]), sums=gate_up_sums)

    line_step(live, new="out", cross="q", out=names[3])
    gate_up_sums = placed_in(live.pop("sums"), evens[2])
    fence(near=near_sends(live["parts"], live["far"]), sums=gate_up_sums)

    line_step(live, cross="out", out="q")
    gate_up_sums = live.pop("sums")
    for k in evens[3:]:
        gate_up_sums = placed_in(gate_up_sums, k)
    grad_gains = small_sum(live.pop("grad_gains"), "fsdp")
    out = total_of(live.pop("parts"), live.pop("far"), live.pop("near"))
    out = (live["middle"] + out).astype(bf16)
    fence(sums=gate_up_sums, grad_gains=grad_gains, out_final=out)

    line_step(live, out="out")
    out_sums = summed("out")
    grad_gains = small_sum(live.pop("grad_gains"), "seq")
    qkv_sums = summed("q")
    grad_gains = lax.dynamic_slice_in_dim(grad_gains, me * block, block, 1)
    return (
        live["out_final"].reshape(hidden_in.shape),
        live["grad_input"].reshape(hidden_in.shape),
        grad_gains[0],
        qkv_sums,
        out_sums,
        grad_gains[1],
        live["sums"],
        live["down_sums"],
    )


def solution(mesh):
    placed = (
        P("fsdp", "seq", None),
        P("fsdp"),
        P("fsdp", None),
        P("fsdp", None),
        P("fsdp"),
        P("fsdp", None),
        P("fsdp", None),
        P("fsdp", "seq", None),
    )
    return jax.shard_map(
        on_device,
        mesh=mesh,
        in_specs=placed,
        out_specs=(
            P("fsdp", "seq", None),
            P("fsdp", "seq", None),
            P("fsdp"),
            P("fsdp", None),
            P("fsdp", None),
            P("fsdp"),
            P("fsdp", None),
            P("fsdp", None),
        ),
        check_vma=False,
    )
```

```python
import functools

import jax
import jax.numpy as jnp
from jax import lax
from jax.experimental import pallas as pl
from jax.experimental.pallas import tpu as pltpu
from jax.sharding import PartitionSpec as P

HEADS = 32
KVH = 4
HD = 64
FF = 5632

epsilon = 1e-05
masked_value = -1e30
log2e = 1.4426950408889634
contract_last = (((1,), (1,)), ((), ()))
contract_first = (((0,), (0,)), ((), ()))
bf16 = jnp.bfloat16
f32 = jnp.float32


def send(x, k):
    n = lax.axis_size("fsdp")
    return lax.ppermute(x, "fsdp", [(i, i ^ k) for i in range(n)])


def chip_bits():
    n = lax.axis_size("fsdp")
    return [1 << i for i in range(1, n.bit_length() - 1)]


def piece_order():
    n = lax.axis_size("fsdp")
    return list(range(0, n, 2)) + list(range(1, n, 2))


def gather_small(x):
    n, me = lax.axis_size("fsdp"), lax.axis_index("fsdp")
    for k in (1 << i for i in range(n.bit_length() - 1)):
        got = send(x, k)
        x = jnp.where(
            me & k == 0, jnp.concatenate([x, got], 1), jnp.concatenate([got, x], 1)
        )
    return x


def neighbour(x):
    n = lax.axis_size("seq")
    return lax.ppermute(x, "seq", [(i, i ^ 1) for i in range(n)])


def after(x, *others):
    return lax.optimization_barrier((x, *others))[0]


def added(one, two):
    return (one.astype(f32) + two.astype(f32)).astype(bf16)


def line_sum(x):
    n = lax.axis_size("seq")
    if n == 1:
        return x
    if n % 2:
        return lax.psum(x.astype(f32), "seq").astype(bf16)
    me = lax.axis_index("seq")
    mid = n // 2
    total = x
    for i in range(mid - 1):
        total = added(total, lax.ppermute(total, "seq", [(i, i + 1), (n - 1 - i, n - 2 - i)]))
    total = added(total, lax.ppermute(total, "seq", [(mid - 1, mid), (mid, mid - 1)]))
    for i in range(mid - 1):
        got = lax.ppermute(total, "seq", [(mid - 1 - i, mid - 2 - i), (mid + i, mid + 1 + i)])
        taken = (me == mid - 2 - i) | (me == mid + 1 + i)
        total = jnp.where(taken, got, total)
    return total


def line_step(live, new=None, cross=None, out=None):
    if lax.axis_size("seq") != 4:
        if new is not None:
            live["o" + new] = live["t" + new] = line_sum(live["z" + new])
        return
    inward, outward, across = [(0, 1), (3, 2)], [(1, 0), (2, 3)], [(1, 2), (2, 1)]
    x = None if new is None else live["z" + new]
    part = None
    if cross is not None:
        part = live["p" + cross] = added(live["z" + cross], live["i" + cross])
        live["x" + cross] = lax.ppermute(part, "seq", across)
        others = {k: v for k, v in live.items() if not k.endswith(cross)}
        live.update(lax.optimization_barrier((others, part))[0])
    if x is not None:
        live["i" + new] = lax.ppermute(x, "seq", inward)
    if out is not None:
        total = live["t" + out] = added(live["p" + out], live["x" + out])
        live["o" + out] = lax.ppermute(total, "seq", outward)


def is_outer():
    me, n = lax.axis_index("seq"), lax.axis_size("seq")
    return (me == 0) | (me == n - 1)


def small_sum(x, axis):
    n = lax.axis_size(axis)
    if n & (n - 1):
        return lax.psum(x, axis)
    for k in (1 << i for i in range(n.bit_length() - 1)):
        x = x + lax.ppermute(x, axis, [(i, i ^ k) for i in range(n)])
    return x


def copy_kernel(table_ref, x_ref, o_ref):
    o_ref[...] = x_ref[...].astype(o_ref.dtype)


def pick(x, table, size, dtype=None, rows_at=None):
    rows, count = x.shape[0], table.shape[0]
    if size % 128:
        return jnp.concatenate(
            [lax.dynamic_slice_in_dim(x, table[i] * size, size, 1) for i in range(count)], 1
        ).astype(dtype or x.dtype)
    if rows_at is not None:
        rows = rows_at[1]
    row = jnp.zeros((), jnp.int32) if rows_at is None else rows_at[0]
    table = jnp.concatenate([table, row.reshape(1)]).astype(jnp.int32)
    return pl.pallas_call(
        copy_kernel,
        out_shape=jax.ShapeDtypeStruct((rows, count * size), dtype or x.dtype),
        grid_spec=pltpu.PrefetchScalarGridSpec(
            num_scalar_prefetch=1,
            grid=(count,),
            in_specs=[pl.BlockSpec((rows, size), lambda i, table: (table[count], table[i]))],
            out_specs=pl.BlockSpec((rows, size), lambda i, table: (0, i)),
        ),
        cost_estimate=pl.CostEstimate(
            flops=0, transcendentals=0, bytes_accessed=rows * count * size * 4
        ),
    )(table, x)


def blank_kernel(o_ref):
    pass


def blank(shape, dtype):
    return pl.pallas_call(
        blank_kernel,
        out_shape=jax.ShapeDtypeStruct(shape, dtype),
        out_specs=pl.BlockSpec(memory_space=pl.ANY),
    )()


def turn_kernel(sign, x_ref, cos_ref, sin_ref, o_ref):
    x = x_ref[...].astype(f32)
    width = x.shape[1]
    lane = lax.broadcasted_iota(jnp.int32, x.shape, 1)
    first = (lane % HD) < HD // 2
    other = jnp.where(
        first, -pltpu.roll(x, width - HD // 2, 1), pltpu.roll(x, HD // 2, 1)
    )
    o_ref[...] = (x * cos_ref[...] + sign * other * sin_ref[...]).astype(o_ref.dtype)


def turn(x, cos_wide, sin_wide, sign):
    return pl.pallas_call(
        functools.partial(turn_kernel, float(sign)),
        out_shape=jax.ShapeDtypeStruct(x.shape, bf16),
    )(x, cos_wide, sin_wide)


def place_kernel(info_ref, buffer_ref, got_ref, total_ref, o_ref):
    o_ref[...] = jnp.where(info_ref[0] == 1, got_ref[...], total_ref[...]).astype(f32)


def place(buffer, pair, outer, where, size):
    got, total = pair
    rows = got.shape[0]
    if size % 128:
        picked = jnp.where(outer, got, total).astype(f32)
        for i in range(2):
            buffer = lax.dynamic_update_slice_in_dim(
                buffer, picked[:, i * size : (i + 1) * size], where[i] * size, 1
            )
        return buffer
    info = jnp.concatenate([outer.astype(jnp.int32).reshape(1), where.astype(jnp.int32)])
    own = pl.BlockSpec((rows, size), lambda i, info: (0, i))
    return pl.pallas_call(
        place_kernel,
        out_shape=jax.ShapeDtypeStruct(buffer.shape, f32),
        grid_spec=pltpu.PrefetchScalarGridSpec(
            num_scalar_prefetch=1,
            grid=(2,),
            in_specs=[pl.BlockSpec(memory_space=pl.ANY), own, own],
            out_specs=pl.BlockSpec((rows, size), lambda i, info: (0, info[1 + i])),
        ),
        input_output_aliases={1: 0},
    )(info, buffer, got, total)


def mask_bias(start, length, rows):
    key_place = lax.broadcasted_iota(jnp.int32, (length, rows), 0)
    query_place = start + lax.broadcasted_iota(jnp.int32, (length, rows), 1)
    return jnp.where(key_place <= query_place, 0.0, masked_value).astype(f32)


def turned_t(x, cos, sin):
    one, two = x[: HD // 2], x[HD // 2 :]
    return jnp.concatenate([one * cos - two * sin, two * cos + one * sin], 0)


def kv_head(ref, index):
    both = ref[...]
    return jnp.where(index % 2 == 0, both[:, :HD], both[:, HD:])


def attend_kernel(
    heads, per_kv, info_ref, q_ref, k_ref, v_ref, cos_ref, sin_ref, o_ref, lse_ref, bias_ref
):
    length, rows = k_ref.shape[0], q_ref.shape[0]
    scale2 = HD**-0.5 * log2e
    step = pl.program_id(0)

    @pl.when(step == 0)
    def _():
        bias_ref[...] = mask_bias(info_ref[0], length, rows)

    kv = step * heads // per_kv
    keys = kv_head(k_ref, kv)
    values_t = kv_head(v_ref, kv).astype(f32).T.astype(bf16)
    q_t = q_ref[...].T
    cos, sin = cos_ref[...], sin_ref[...]
    q_all = [
        turned_t(q_t[h * HD : (h + 1) * HD], cos, sin).astype(bf16) for h in range(heads)
    ]

    key_size = jnp.max(jnp.sum(jnp.square(keys.astype(f32)), axis=1))
    query_size = jnp.max(
        sum(
            jnp.sum(jnp.square(q.astype(f32)), axis=0, keepdims=True) for q in q_all
        )
    )
    small = key_size * query_size * scale2**2 < 80.0**2

    def run(shift):
        outs = []
        for h in range(heads):
            scores = jnp.dot(keys, q_all[h], preferred_element_type=f32) + bias_ref[...]
            if shift:
                top = jnp.max(scores, axis=0, keepdims=True)
                weights = jnp.exp2((scores - top) * scale2)
            else:
                weights = jnp.exp2(scores * scale2)
            total = jnp.sum(weights, axis=0, keepdims=True)
            out = jnp.dot(values_t, weights.astype(bf16), preferred_element_type=f32)
            outs.append(out * (1.0 / total))
            lse = jnp.log2(total)
            lse_ref[0, h : h + 1, :] = lse + top * scale2 if shift else lse
        o_ref[...] = jnp.concatenate(outs, 0).T.astype(bf16)

    pl.when(small)(lambda: run(False))
    pl.when(jnp.logical_not(small))(lambda: run(True))


def attend_specs(n, rows, length):
    heads = HEADS // n
    per_kv = HEADS // KVH
    kv_at = lambda i: (i * heads // per_kv) // 2
    return dict(
        plain=pl.BlockSpec((rows, heads * HD), lambda i, info: (0, i)),
        ordered=pl.BlockSpec((rows, heads * HD), lambda i, info: (0, info[1 + i])),
        keys=pl.BlockSpec((length, 2 * HD), lambda i, info: (0, kv_at(i))),
        values=pl.BlockSpec((length, 2 * HD), lambda i, info: (0, KVH // 2 + kv_at(i))),
        table=pl.BlockSpec((HD // 2, rows), lambda i, info: (0, 0)),
        lse=pl.BlockSpec((1, heads, rows), lambda i, info: (i, 0, 0)),
    )


def attend(info, joined, all_kv, cos_t, sin_t):
    n = lax.axis_size("fsdp")
    rows, length = joined.shape[0], all_kv.shape[0]
    heads = HEADS // n
    spec = attend_specs(n, rows, length)
    return pl.pallas_call(
        functools.partial(attend_kernel, heads, HEADS // KVH),
        out_shape=(
            jax.ShapeDtypeStruct((rows, HEADS * HD), bf16),
            jax.ShapeDtypeStruct((n, heads, rows), f32),
        ),
        grid_spec=pltpu.PrefetchScalarGridSpec(
            num_scalar_prefetch=1,
            grid=(n,),
            in_specs=[spec[k] for k in ("plain", "keys", "values", "table", "table")],
            out_specs=(spec["ordered"], spec["lse"]),
            scratch_shapes=[pltpu.VMEM((length, rows), f32)],
        ),
        compiler_params=pltpu.CompilerParams(vmem_limit_bytes=40 << 20),
        cost_estimate=pl.CostEstimate(
            flops=4 * HEADS * rows * length * HD * 4,
            bytes_accessed=6 * rows * HEADS * HD,
            transcendentals=HEADS * rows * length,
        ),
    )(info, joined, all_kv, all_kv, cos_t, sin_t)


def attend_back_kernel(
    heads, per_kv, info_ref, q_ref, k_ref, v_ref, g_ref, o_ref, cos_ref, sin_ref, lse_ref,
    dq_ref, dkv_ref, bias_ref, dk_ref, dv_ref,
):
    length, rows = k_ref.shape[0], q_ref.shape[0]
    scale = HD**-0.5
    scale2 = scale * log2e
    step = pl.program_id(0)
    steps = per_kv // heads

    @pl.when(step == 0)
    def _():
        bias_ref[...] = mask_bias(info_ref[0], length, rows)

    @pl.when(step % steps == 0)
    def _():
        dk_ref[...] = jnp.zeros_like(dk_ref)
        dv_ref[...] = jnp.zeros_like(dv_ref)

    kv = step * heads // per_kv
    keys, values = kv_head(k_ref, kv), kv_head(v_ref, kv)
    keys_t = keys.astype(f32).T.astype(bf16)
    q_t = q_ref[...].T
    g_t = g_ref[...].astype(f32).T
    deltas = g_t * o_ref[...].astype(f32).T
    g_t = g_t.astype(bf16)
    cos, sin = cos_ref[...], sin_ref[...]
    outs = []
    dk, dv = dk_ref[...], dv_ref[...]
    for h in range(heads):
        q_h = turned_t(q_t[h * HD : (h + 1) * HD], cos, sin).astype(bf16)
        g_h = g_t[h * HD : (h + 1) * HD]
        scores = jnp.dot(keys, q_h, preferred_element_type=f32) + bias_ref[...]
        weights = jnp.exp2(scores * scale2 - lse_ref[0, h : h + 1, :])
        grad_p = jnp.dot(values, g_h, preferred_element_type=f32)
        delta = jnp.sum(deltas[h * HD : (h + 1) * HD], axis=0, keepdims=True)
        grad_s = (weights * (grad_p - delta)).astype(bf16)
        grad_q = jnp.dot(keys_t, grad_s, preferred_element_type=f32) * scale
        outs.append(turned_t(grad_q.astype(bf16).astype(f32), cos, -sin))
        dk += lax.dot_general(grad_s, q_h, contract_last, preferred_element_type=f32)
        dv += lax.dot_general(
            weights.astype(bf16), g_h, contract_last, preferred_element_type=f32
        )
    dk_ref[...], dv_ref[...] = dk, dv
    dq_ref[...] = jnp.concatenate(outs, 0).T.astype(bf16)

    @pl.when(step % steps == steps - 1)
    def _():
        dkv_ref[...] = jnp.concatenate([dk * scale, dv], 1).astype(bf16)


def attend_back(info, joined, all_kv, cos_t, sin_t, grads, outs, lse):
    n = lax.axis_size("fsdp")
    rows, length = joined.shape[0], all_kv.shape[0]
    heads, per_kv = HEADS // n, HEADS // KVH
    spec = attend_specs(n, rows, length)
    names = ("plain", "keys", "values", "ordered", "ordered", "table", "table", "lse")
    return pl.pallas_call(
        functools.partial(attend_back_kernel, heads, per_kv),
        out_shape=(
            jax.ShapeDtypeStruct((rows, HEADS * HD), bf16),
            jax.ShapeDtypeStruct((length, 2 * KVH * HD), bf16),
        ),
        grid_spec=pltpu.PrefetchScalarGridSpec(
            num_scalar_prefetch=1,
            grid=(n,),
            in_specs=[spec[k] for k in names],
            out_specs=(
                spec["plain"],
                pl.BlockSpec((length, 2 * HD), lambda i, info: (0, i * heads // per_kv)),
            ),
            scratch_shapes=[
                pltpu.VMEM((length, rows), f32),
                pltpu.VMEM((length, HD), f32),
                pltpu.VMEM((length, HD), f32),
            ],
        ),
        compiler_params=pltpu.CompilerParams(vmem_limit_bytes=48 << 20),
        cost_estimate=pl.CostEstimate(
            flops=10 * HEADS * rows * length * HD * 4,
            bytes_accessed=8 * rows * HEADS * HD,
            transcendentals=HEADS * rows * length,
        ),
    )(info, joined, all_kv, all_kv, grads, outs, cos_t, sin_t, lse)


def column_chunks(total, size=256):
    return [(c, min(size, total - c)) for c in range(0, total, size)]


def part_pieces(n):
    evens = list(range(0, n, 2))
    return evens[:3], evens[3:], [k | 1 for k in evens[:3]], [k | 1 for k in evens[3:]]


def ffn_kernel(n, count, info_ref, *refs):
    x_refs, g_refs, refs = refs[:count], refs[count : 2 * count], refs[2 * count :]
    parts, (d_own, d_other), refs = refs[:4], refs[4:6], refs[6:]
    outs, (x, g, w, d, both, mid, sems) = refs[: 4 * count], refs[4 * count :]
    mixed_refs, both_refs = outs[:count], outs[count : 2 * count]
    back_refs, out_refs = outs[2 * count : 3 * count], outs[3 * count :]
    me, part = info_ref[0], info_ref[1]
    rows, width = x_refs[0].shape
    cols = d.shape[0]
    share = cols // 2
    block = width // n
    half = block // 2

    copies = []
    for source, ks in zip(parts, part_pieces(n), strict=True):
        for i, k in enumerate(ks):
            owner = (me ^ k) * block
            for j in range(2):
                at = owner if k < 2 else owner + (part if j == 0 else 1 - part) * half
                if k < 2:
                    at = at + j * half
                copies.append(
                    pltpu.make_async_copy(
                        source.at[pl.ds(i * block + j * half, half)],
                        w.at[pl.ds(pl.multiple_of(at, half), half)],
                        sems.at[len(copies)],
                    )
                )
    core = me % 2
    for source, at in ((d_own, core), (d_other, 1 - core)):
        copies.append(
            pltpu.make_async_copy(
                source, d.at[pl.ds(pl.multiple_of(at * share, share), share)], sems.at[len(copies)]
            )
        )
    for copy in copies:
        copy.start()
    for i in range(count):
        x[i * rows : (i + 1) * rows] = x_refs[i][...]
        g[i * rows : (i + 1) * rows] = g_refs[i][...]
    for copy in copies:
        copy.wait()

    def columns(at, size):
        gate_w, up_w = w[:, pl.ds(at, size)], w[:, pl.ds(cols + at, size)]
        gate = jnp.dot(x[...], gate_w, preferred_element_type=f32)
        up = jnp.dot(x[...], up_w, preferred_element_type=f32)
        grad = lax.dot_general(
            g[...], d[pl.ds(at, size)], contract_last, preferred_element_type=f32
        )
        sig = 1.0 / (1.0 + jnp.exp(-gate))
        act = gate * sig
        mid[:, pl.ds(at, size)] = (act * up).astype(bf16)
        both[:, pl.ds(at, size)] = (grad * up * (sig * (1.0 + gate * (1.0 - sig)))).astype(bf16)
        both[:, pl.ds(cols + at, size)] = (grad * act).astype(bf16)

    full = cols // 256
    pl.loop(0, full)(lambda c: columns(pl.multiple_of(c * 256, 256), 256))
    if cols % 256:
        columns(full * 256, cols % 256)
    for i in range(count):
        at = slice(i * rows, (i + 1) * rows)
        mixed_refs[i][...] = mid[at].astype(f32).T.astype(bf16)
        both_refs[i][...] = both[at]

    @pl.loop(0, width // 256)
    def _(t):
        at = pl.multiple_of(t * 256, 256)
        back = lax.dot_general(
            both[...], w[pl.ds(at, 256)], contract_last, preferred_element_type=f32
        ).astype(bf16)
        out = jnp.dot(mid[...], d[:, pl.ds(at, 256)], preferred_element_type=f32).astype(bf16)
        for i in range(count):
            back_refs[i][:, pl.ds(at, 256)] = back[i * rows : (i + 1) * rows]
            out_refs[i][:, pl.ds(at, 256)] = out[i * rows : (i + 1) * rows]


def ffn(info, xs, gs, parts, d_own, d_other):
    n = lax.axis_size("fsdp")
    count = len(xs)
    rows, width = xs[0].shape
    cols = 2 * d_own.shape[0]
    if cols % 128:
        return ffn_plain(info, xs, gs, parts, d_own, d_other)
    shapes = (
        [jax.ShapeDtypeStruct((cols, rows), bf16)] * count
        + [jax.ShapeDtypeStruct((rows, 2 * cols), bf16)] * count
        + [jax.ShapeDtypeStruct((rows, width), bf16)] * (2 * count)
    )
    vmem, hbm = pl.BlockSpec(memory_space=pltpu.VMEM), pl.BlockSpec(memory_space=pl.ANY)
    outs = pl.pallas_call(
        functools.partial(ffn_kernel, n, count),
        out_shape=shapes,
        in_specs=[pl.BlockSpec(memory_space=pltpu.SMEM)] + [vmem] * (2 * count) + [hbm] * 6,
        out_specs=[vmem] * (4 * count),
        scratch_shapes=[
            pltpu.VMEM((count * rows, width), bf16),
            pltpu.VMEM((count * rows, width), bf16),
            pltpu.VMEM((width, 2 * cols), bf16),
            pltpu.VMEM((cols, width), bf16),
            pltpu.VMEM((count * rows, 2 * cols), bf16),
            pltpu.VMEM((count * rows, cols), bf16),
            pltpu.SemaphoreType.DMA((2 * n + 2,)),
        ],
        compiler_params=pltpu.CompilerParams(vmem_limit_bytes=56 << 20),
        cost_estimate=pl.CostEstimate(
            flops=2 * count * rows * width * cols * 6,
            bytes_accessed=6 * width * cols,
            transcendentals=count * rows * cols,
        ),
    )(info, *xs, *gs, *parts, d_own, d_other)
    return [outs[i * count : (i + 1) * count] for i in range(4)]


def ffn_plain(info, xs, gs, parts, d_own, d_other):
    n = lax.axis_size("fsdp")
    me, part = info[0], info[1]
    width, share = xs[0].shape[1], d_own.shape[0]
    block, cols = width // n, 2 * share
    half = block // 2
    w = jnp.zeros((width, 2 * cols), bf16)
    for source, ks in zip(parts, part_pieces(n), strict=True):
        for i, k in enumerate(ks):
            for j in range(2):
                at = j if k < 2 else (part if j == 0 else 1 - part)
                rows = source[i * block + j * half : i * block + (j + 1) * half]
                w = lax.dynamic_update_slice_in_dim(w, rows, (me ^ k) * block + at * half, 0)
    d = jnp.where(
        me % 2 == 0, jnp.concatenate([d_own, d_other], 0), jnp.concatenate([d_other, d_own], 0)
    )
    mixed, both, back, out = [], [], [], []
    for x, g in zip(xs, gs, strict=True):
        gate, up = dot(x, w[:, :cols]), dot(x, w[:, cols:])
        sig = jax.nn.sigmoid(gate)
        act = gate * sig
        grad = dot_last(g, d)
        mid = (act * up).astype(bf16)
        two = jnp.concatenate(
            [grad * up * (sig * (1.0 + gate * (1.0 - sig))), grad * act], 1
        ).astype(bf16)
        mixed.append(mid.T)
        both.append(two)
        back.append(dot_last(two, w).astype(bf16))
        out.append(dot(mid, d).astype(bf16))
    return mixed, both, back, out


def down_grad_kernel(count, info_ref, *refs):
    lefts, rights, rest = refs[:count], refs[count : 2 * count], refs[2 * count :]
    total = sum(
        jnp.dot(one[...], two[...], preferred_element_type=f32)
        for one, two in zip(lefts, rights, strict=True)
    )
    if len(rest) == 2:
        total = total.astype(bf16).astype(f32) + rest[0][...].astype(f32)
    rest[-1][...] = total.astype(bf16)


def down_grad(info, at, mixed, gs, got=None):
    count = len(mixed)
    cols, rows = mixed[0].shape
    width = gs[0].shape[1]
    size = min(512, width)
    out = pl.BlockSpec((cols // 2, size), lambda i, info: (0, i))
    return pl.pallas_call(
        functools.partial(down_grad_kernel, count),
        out_shape=jax.ShapeDtypeStruct((cols // 2, width), bf16),
        grid_spec=pltpu.PrefetchScalarGridSpec(
            num_scalar_prefetch=1,
            grid=(width // size,),
            in_specs=[pl.BlockSpec((cols // 2, rows), lambda i, info: (info[at], 0))] * count
            + [pl.BlockSpec((rows, size), lambda i, info: (0, i))] * count
            + ([] if got is None else [out]),
            out_specs=out,
        ),
        compiler_params=pltpu.CompilerParams(vmem_limit_bytes=40 << 20),
        cost_estimate=pl.CostEstimate(
            flops=count * rows * width * cols,
            bytes_accessed=4 * width * cols,
            transcendentals=0,
        ),
    )(info, *mixed, *gs, *([] if got is None else [got]))


def up_grad_kernel(count, split, info_ref, *refs):
    lefts, rights, rest = refs[:count], refs[count : 2 * count], refs[2 * count :]
    total = sum(
        lax.dot_general(one[...], two[...], contract_first, preferred_element_type=f32)
        for one, two in zip(lefts, rights, strict=True)
    ).astype(bf16)
    if not split:
        rest[0][...] = total
        return
    total = (total.astype(f32) + rest[0][...].astype(f32)).astype(bf16)
    for i, out in enumerate(rest[1:]):

        @pl.when(pl.program_id(1) == i)
        def _(out=out):
            out[...] = total


def up_grad(table, xs, both, got=None):
    count, chips = len(xs), table.shape[0]
    rows, width = xs[0].shape
    cols = both[0].shape[1] // 2
    block = width // lax.axis_size("fsdp")
    if cols % 128 or block % 128:
        whole = sum(dot_first(one, two) for one, two in zip(xs, both, strict=True))
        outs = [
            lax.dynamic_slice_in_dim(whole, table[i] * block, block, 0).astype(bf16)
            for i in range(chips)
        ]
        if got is None:
            return jnp.concatenate(outs, 0)
        return [added(x, got[i * block : (i + 1) * block]) for i, x in enumerate(outs)]
    one = pl.BlockSpec((block, cols), lambda h, b, table: (b, h))
    outs = [
        pl.BlockSpec(
            (block, cols), lambda h, b, table, i=i: (0, jnp.where(b >= i, h, jnp.maximum(h - 1, 0)))
        )
        for i in range(chips)
    ]
    split = got is not None
    shape = jax.ShapeDtypeStruct((block, 2 * cols), bf16)
    return pl.pallas_call(
        functools.partial(up_grad_kernel, count, split),
        out_shape=[shape] * chips
        if split
        else jax.ShapeDtypeStruct((chips * block, 2 * cols), bf16),
        grid_spec=pltpu.PrefetchScalarGridSpec(
            num_scalar_prefetch=1,
            grid=(2, chips),
            in_specs=[pl.BlockSpec((rows, block), lambda h, b, table: (0, table[b]))] * count
            + [pl.BlockSpec((rows, cols), lambda h, b, table: (0, h))] * count
            + ([one] if split else []),
            out_specs=outs if split else one,
        ),
        compiler_params=pltpu.CompilerParams(vmem_limit_bytes=48 << 20),
        cost_estimate=pl.CostEstimate(
            flops=4 * count * rows * chips * block * cols,
            bytes_accessed=4 * chips * block * cols * 2,
            transcendentals=0,
        ),
    )(table, *xs, *both, *([got] if split else []))


def angle_tables(positions):
    half_dim = HD // 2
    inverse = 10000.0 ** (-jnp.arange(half_dim, dtype=f32) * 2.0 / HD)
    angles = positions.astype(f32)[:, None] * inverse[None, :]
    return jnp.cos(angles), jnp.sin(angles)


def norm_factor(values):
    return lax.rsqrt(jnp.mean(values * values, axis=-1, keepdims=True) + epsilon)


def norm_back(incoming, inputs, factor, gain):
    weighted = incoming * gain
    gain_grad = jnp.sum(incoming * (inputs * factor), axis=0)
    input_grad = weighted * factor - inputs * (factor * factor * factor) * jnp.mean(
        weighted * inputs, axis=-1, keepdims=True
    )
    return (gain_grad, input_grad)


def dot(one, two):
    return jnp.dot(one, two, preferred_element_type=f32)


def dot_last(one, two):
    return lax.dot_general(one, two, contract_last, preferred_element_type=f32)


def dot_first(one, two):
    return lax.dot_general(one, two, contract_first, preferred_element_type=f32)


def on_device(
    hidden_in, norm_attn, qkv_weight, out_weight, norm_ffn, gate_up_weight, down_weight, cotangent
):
    n = lax.axis_size("fsdp")
    me = lax.axis_index("fsdp")
    chips, chip, core = n // 2, me // 2, me % 2
    order = piece_order()
    evens = order[:chips]
    near, rest = evens[1:3], evens[3:]
    width = hidden_in.shape[2]
    rows = hidden_in.shape[0] * hidden_in.shape[1]
    q_width = HEADS * HD
    kv_width = KVH * HD
    share = FF // n
    chip_share = 2 * share
    block = width // n
    half = block // 2
    seq_at = lax.axis_index("seq")
    rank = {k: i for i, k in enumerate(order)}
    to_table = (me ^ jnp.array(order, jnp.int32)).astype(jnp.int32)
    at_table = jnp.array([rank[k] for k in range(n)], jnp.int32)[
        me ^ jnp.arange(n, dtype=jnp.int32)
    ]
    odd_table, even_table = to_table[chips:], to_table[:chips]
    assisted = lax.axis_size("seq") % 2 == 0
    part_at = seq_at % 2 if assisted else jnp.zeros_like(seq_at)

    live = {}

    def fence(**more):
        live.update(more)
        new = lax.optimization_barrier(live)
        live.clear()
        live.update(new)

    def two_hops(pieces):
        if len(rest) != 1:
            return {k: send(pieces[0], k) for k in rest}
        a, b = near
        size = pieces[0].shape[0] // 2
        lower, upper = send(pieces[b][:size], a), send(pieces[a][size:], b)
        return {rest[0]: (lower, upper)}

    def whole_piece(x):
        return jnp.concatenate(x, 0) if isinstance(x, tuple) else x

    def my_columns(k, at):
        cols = chip ^ (k // 2)
        spots = jnp.stack([cols, cols + chips]).astype(jnp.int32)
        if at is None:
            return pick(live["gate_up"], spots, chip_share)
        if chip_share % 128:
            part = pick(live["gate_up"], spots, chip_share)
            return lax.dynamic_slice_in_dim(part, at * half, half, 0)
        return pick(live["gate_up"], spots, chip_share, rows_at=(at, half))

    def other_half(k, first):
        return neighbour(first) if assisted else send(live["others"][k], k)

    full_qkv = lax.all_gather(qkv_weight, "fsdp", axis=0, tiled=True)
    fence(
        gains=gather_small(jnp.stack([norm_attn, norm_ffn])),
        hidden=hidden_in.reshape(rows, width),
        grad=cotangent.reshape(rows, width),
        gate_up=gate_up_weight,
        down=down_weight,
        out=out_weight,
    )

    firsts = {k: send(my_columns(k, part_at), k) for k in near}
    fence(
        firsts=firsts,
        others={} if assisted else {k: my_columns(k, 1 - part_at) for k in evens[1:]},
        own=my_columns(0, None),
        d_other=send(live["down"], 1),
    )
    inputs = live["hidden"].astype(f32)
    factor_one = norm_factor(inputs)
    gains = live["gains"].astype(f32)
    normed_one = (inputs * factor_one * gains[:1]).astype(bf16)
    fence(
        seconds={k: other_half(k, live["firsts"][k]) for k in near},
        mine={k: my_columns(k, part_at) for k in rest},
        qkv=full_qkv,
        normed_one=normed_one,
        normed_one_x=pick(normed_one, to_table, block),
    )
    del live["gate_up"]

    normed_one = live.pop("normed_one")
    joined = dot(normed_one, live["qkv"][:, q_width:])
    positions = seq_at * rows + jnp.arange(rows, dtype=jnp.int32)
    cosine, sine = angle_tables(positions)
    cos_wide, sin_wide = jnp.tile(cosine, (1, 2 * KVH)), jnp.tile(sine, (1, 2 * KVH))
    cos_t, sin_t = cosine.T, sine.T
    keys_values = jnp.concatenate(
        [turn(joined[:, :kv_width], cos_wide, sin_wide, 1), joined[:, kv_width:].astype(bf16)], 1
    )
    all_kv = lax.all_gather(keys_values, "seq", axis=0, tiled=True)
    joined = dot(normed_one, live["qkv"][:, :q_width])
    outs = {0: live.pop("out")}
    outs |= {k: send(outs[0], k) for k in near}
    firsts, seconds = live.pop("firsts"), live.pop("seconds")
    w_own = jnp.concatenate(sum([[firsts[k], seconds[k]] for k in near], [live.pop("own")]), 0)
    firsts = {k: send(x, k) for k, x in live.pop("mine").items()}
    fence(w_own=w_own, joined=joined, kv=all_kv, outs=outs, firsts=firsts)

    outs = live.pop("outs")
    outs |= two_hops(outs)
    firsts = live.pop("firsts")
    seconds = {k: other_half(k, firsts[k]) for k in rest}
    info = jnp.concatenate([(seq_at * rows).reshape(1), at_table]).astype(jnp.int32)
    attended, lse = attend(info, live["joined"], live["kv"], cos_t, sin_t)
    fence(
        firsts=firsts,
        seconds=seconds,
        outs=outs,
        attended=attended,
        lse=lse,
        w_other=send(live["w_own"], 1),
    )

    outs, firsts, seconds = live.pop("outs"), live.pop("firsts"), live.pop("seconds")
    out_even = jnp.concatenate([whole_piece(outs[k]) for k in evens], 0)
    out_odd = send(out_even, 1)
    grads = {0: live["grad"]}
    grads |= {k: send(grads[0], k) for k in near}
    w_rest = sum([[firsts[k], seconds[k]] for k in rest], [])
    w_rest = jnp.concatenate(w_rest or [live["w_own"]], 0)
    middle = dot(live["attended"][:, : q_width // 2], out_even)
    middle = live["hidden"].astype(f32) + (
        middle + dot(live["attended"][:, q_width // 2 :], out_odd)
    )
    factor_two = norm_factor(middle)
    gain_two = live["gains"][1:].astype(f32)
    normed_two = (middle * factor_two * gain_two).astype(bf16)
    fence(
        w_rest=w_rest,
        w_rest_other=send(w_rest, 1),
        out_even=out_even,
        out_odd=out_odd,
        grads=grads,
        middle=middle,
        tokens={0: normed_two},
    )

    ffn_info = jnp.stack([me, part_at, core, 1 - core]).astype(jnp.int32)

    def ffn_of(group):
        names = ("mixed", "both", "back", "parts")
        weights = [live[k] for k in ("w_own", "w_rest", "w_other", "w_rest_other")]
        results = ffn(
            ffn_info,
            [whole_piece(live["tokens"][k]) for k in group],
            [whole_piece(live["grads"][k]) for k in group],
            weights,
            live["down"],
            live["d_other"],
        )
        for name, new in zip(names, results, strict=True):
            live[name] = live.get(name, {}) | dict(zip(group, new, strict=True))

    new = {k: send(live["tokens"][0], k) for k in near}
    ffn_of([0])
    live["tokens"] |= new
    fence()
    far_tokens, far_grads = two_hops(live["tokens"]), two_hops(live["grads"])
    ffn_of(near)
    live["tokens"] |= far_tokens
    live["grads"] |= far_grads
    fence()
    new = {k: send(live["back"][k], k) for k in near}
    if rest:
        ffn_of(rest)
    def each(name):
        return [whole_piece(live[name][k]) for k in evens]

    theirs = down_grad(ffn_info, 3, each("mixed"), each("grads"))
    fence(returned=new, theirs=theirs)

    live["returned"] |= {k: send(live["back"][k], k) for k in rest}

    gots = up_grad(odd_table, each("tokens"), each("both"))
    got = send(live.pop("theirs"), 1)
    grad_down = down_grad(after(ffn_info, gots), 2, each("mixed"), each("grads"), got)
    fence(gots=gots, zd=grad_down[: share // 2], ze=grad_down[share // 2 :])

    line_step(live, new="d")
    gots = send(live.pop("gots"), 1)
    grad_normed_two = live["back"][0].astype(f32)
    for k in evens[1:]:
        grad_normed_two = grad_normed_two + live["returned"][k].astype(f32)
    middle = live["middle"]
    factor_two = norm_factor(middle)
    gain_two = live["gains"][1:].astype(f32)
    grad_gain_two, grad_norm_two = norm_back(grad_normed_two, middle, factor_two, gain_two)
    grad_middle = live["grad"].astype(f32) + grad_norm_two
    grad_branch = grad_middle.astype(bf16)
    grad_attended = jnp.concatenate(
        [dot_last(grad_branch, live[k]).astype(bf16) for k in ("out_even", "out_odd")], 1
    )
    parts = up_grad(even_table, each("tokens"), each("both"), gots)
    for k in ("tokens", "grads", "both", "mixed", "back", "returned", "d_other"):
        del live[k]
    for k in ("w_own", "w_rest", "w_other", "w_rest_other"):
        del live[k]
    del live["out_even"], live["out_odd"], live["down"], live["grad"]
    fence(
        ups=dict(zip(evens, parts, strict=True)),
        grad_gain_two=grad_gain_two,
        grad_middle=grad_middle,
        grad_branch=grad_branch,
        grad_attended=grad_attended,
    )

    names = [str(k) for k in evens]

    def blocks(whole, got):
        return {
            k: added(whole[i * block : (i + 1) * block], got[i * block : (i + 1) * block])
            for i, k in enumerate(evens)
        }

    def far_sends(parts):
        if len(rest) != 1:
            return [send(parts[k], k) for k in rest]
        far = parts[rest[0]]
        size = far.shape[0] // 2
        return [send(far[:size], near[0]), send(far[size:], near[1])]

    def near_sends(parts, got):
        if len(rest) != 1:
            return [send(parts[k], k) for k in near]
        size = parts[0].shape[0] // 2
        lower, upper = got
        one, two = parts[near[0]], parts[near[1]]
        one = jnp.concatenate([one[:size], added(one[size:], upper)], 0)
        two = jnp.concatenate([added(two[:size], lower), two[size:]], 0)
        return [send(one, near[0]), send(two, near[1])]

    def total_of(parts, *got):
        total = parts[0].astype(f32)
        for x in sum([g for g in got if g[0].shape == parts[0].shape], []):
            total = total + x.astype(f32)
        return total

    line_step(live, new="e", cross="d")
    sent = {k: send(live["ups"][k], k) for k in near}
    grad_queries, kv_parts = attend_back(
        info,
        live["joined"],
        live["kv"],
        cos_t,
        sin_t,
        live["grad_attended"],
        live["attended"],
        live["lse"],
    )
    fence(sent=sent, grad_queries=grad_queries, kv_parts=kv_parts)
    for k in ("grad_attended", "joined", "kv", "lse"):
        del live[k]

    ups = live.pop("ups")
    live["z0"] = ups[0]
    for k, x in live.pop("sent").items():
        live[f"z{k}"] = x
    line_step(live, new=names[0], cross="e", out="d")
    sent = {k: send(ups[k], k) for k in rest}
    kv_sums = lax.psum_scatter(live.pop("kv_parts"), "seq", scatter_dimension=0, tiled=True)
    kv_sums = kv_sums.reshape(rows, KVH, 2, HD).transpose(0, 2, 1, 3).reshape(rows, 2 * kv_width)
    grad_joined = jnp.concatenate(
        [
            live.pop("grad_queries"),
            turn(kv_sums[:, :kv_width], cos_wide, sin_wide, -1),
            kv_sums[:, kv_width:],
        ],
        1,
    )
    normed_one_x = live.pop("normed_one_x")
    theirs = dot_first(normed_one_x[:, width // 2 :], grad_joined).astype(bf16)
    attended = pick(live.pop("attended"), at_table, block)
    grad_out = dot_first(attended, live.pop("grad_branch")).astype(bf16)
    fence(
        sent=sent,
        grad_out=grad_out,
        grad_joined=grad_joined,
        normed_one_x=normed_one_x,
        theirs=theirs,
    )

    for k, x in live.pop("sent").items():
        live[f"z{k}"] = x
    line_step(live, new=names[1], cross=names[0], out="e")
    out_total = lax.psum_scatter(live.pop("grad_out"), "fsdp", scatter_dimension=0, tiled=True)
    mine = dot_first(live.pop("normed_one_x")[:, : width // 2], live["grad_joined"])
    fence(got_qkv=send(live.pop("theirs"), 1), mine=mine.astype(bf16))

    gate_up_sums = blank((block, 2 * FF), f32)
    outer = is_outer()

    def summed(k):
        return jnp.where(outer, live.pop("o" + k), live.pop("t" + k)).astype(f32)

    def placed_in(buffer, k):
        cols = chip ^ (k // 2)
        spots = jnp.stack([cols, cols + chips])
        return place(buffer, (live.pop(f"o{k}"), live.pop(f"t{k}")), outer, spots, chip_share)

    line_step(live, new=names[2] if chips > 2 else None, cross=names[1], out=names[0])
    parts_qkv = blocks(live.pop("mine"), live.pop("got_qkv"))
    down_sums = jnp.concatenate([summed("d"), summed("e")], 0)
    fence(parts_qkv=parts_qkv, far_qkv=far_sends(parts_qkv), down_sums=down_sums)

    line_step(live, new=names[3] if chips > 3 else None, cross=names[2], out=names[1])
    for k in evens[4:]:
        line_step(live, new=str(k))
    gate_up_sums = placed_in(gate_up_sums, 0)
    inputs = live["hidden"].astype(f32)
    factor_one = norm_factor(inputs)
    grad_normed_one = dot_last(live.pop("grad_joined"), live.pop("qkv"))
    grad_gain_one, grad_norm_one = norm_back(
        grad_normed_one, inputs, factor_one, live["gains"][:1].astype(f32)
    )
    grad_input = (live["grad_middle"] + grad_norm_one).astype(bf16)
    fence(
        near_qkv=near_sends(live["parts_qkv"], live["far_qkv"]),
        zout=out_total,
        sums=gate_up_sums,
        grad_input=grad_input,
        grad_gains=jnp.stack([grad_gain_one, live.pop("grad_gain_two")]),
    )

    total = total_of(live.pop("parts_qkv"), live.pop("far_qkv"), live.pop("near_qkv"))
    live["zq"] = total.astype(bf16)
    line_step(live, new="q", cross=names[3], out=names[2])
    gate_up_sums = placed_in(live.pop("sums"), evens[1])
    fence(far=far_sends(live["parts"]), sums=gate_up_sums)

    line_step(live, new="out", cross="q", out=names[3])
    gate_up_sums = placed_in(live.pop("sums"), evens[2])
    fence(near=near_sends(live["parts"], live["far"]), sums=gate_up_sums)

    line_step(live, cross="out", out="q")
    gate_up_sums = live.pop("sums")
    for k in evens[3:]:
        gate_up_sums = placed_in(gate_up_sums, k)
    grad_gains = small_sum(live.pop("grad_gains"), "fsdp")
    out = total_of(live.pop("parts"), live.pop("far"), live.pop("near"))
    out = (live["middle"] + out).astype(bf16)
    fence(sums=gate_up_sums, grad_gains=grad_gains, out_final=out)

    line_step(live, out="out")
    out_sums = summed("out")
    grad_gains = small_sum(live.pop("grad_gains"), "seq")
    qkv_sums = summed("q")
    grad_gains = lax.dynamic_slice_in_dim(grad_gains, me * block, block, 1)
    return (
        live["out_final"].reshape(hidden_in.shape),
        live["grad_input"].reshape(hidden_in.shape),
        grad_gains[0],
        qkv_sums,
        out_sums,
        grad_gains[1],
        live["sums"],
        live["down_sums"],
    )


def solution(mesh):
    placed = (
        P("fsdp", "seq", None),
        P("fsdp"),
        P("fsdp", None),
        P("fsdp", None),
        P("fsdp"),
        P("fsdp", None),
        P("fsdp", None),
        P("fsdp", "seq", None),
    )
    return jax.shard_map(
        on_device,
        mesh=mesh,
        in_specs=placed,
        out_specs=(
            P("fsdp", "seq", None),
            P("fsdp", "seq", None),
            P("fsdp"),
            P("fsdp", None),
            P("fsdp", None),
            P("fsdp"),
            P("fsdp", None),
            P("fsdp", None),
        ),
        check_vma=False,
    )
```
